32 devices in a mesh: groups: 1, ep: 32 (over z, y, x, core), tp: 1.
Axes of the slice: x: 2, y: 2, z: 4, core: 2. Of those that a mesh axis runs over, the one named last changes fastest.
Arguments:
- query_latent: bfloat16 [32, 128, 576], P(('groups', 'ep')), may hold values from -40 to 40
- latent_cache: bfloat16 [32, 1024, 576], P(('groups', 'ep'), 'tp'), may hold values from -5 to 5
- cache_length: int32 [32], P(('groups', 'ep')), may hold values from 1 to 1024, 16384 in all
- prefill_latent: bfloat16 [32, 32, 4, 576], P(('groups', 'ep'), 'tp'), may hold values from -5 to 5
- block_owner: int32 [32, 32, 1], P(('groups', 'ep'), 'tp'), may hold values from 0 to 31; in each aligned block of 32 rows (0 to 31, 32 to 63, ..., all dimensions but the last counted through in order) at most 2 rows name the same one
- tokens: bfloat16 [1024, 3584], P(('groups', 'ep')), may hold values from -6 to 6
- expert_ids: int32 [1024, 8], P(('groups', 'ep')), may hold values from 0 to 15, all different within a row; in each aligned block of 32 rows (0 to 31, 32 to 63, ...) at most 32 rows name the same one
- route_weight: float32 [1024, 8], P(('groups', 'ep')), may hold values from 0.1 to 1
- gate_weight: bfloat16 [32, 3584, 512], P('ep', None, 'tp'), may hold values from -0.09375 to 0.09375
- up_weight: bfloat16 [32, 3584, 512], P('ep', None, 'tp'), may hold values from -0.09375 to 0.09375
- down_weight: bfloat16 [32, 512, 3584], P('ep', None, 'tp'), may hold values from -0.1875 to 0.1875
Outputs:
- attn_out: bfloat16 [32, 128, 512], P(('groups', 'ep'))
- moe_out: bfloat16 [1024, 3584], P(('groups', 'ep'), 'tp')
The draws below stay inside these ranges and needn't reach their ends.
Inputs may be any that keep to these rules, and one draw needn't show every extreme that they name: `expert_ids`: each row names 8 different experts; the 32 rows of one device name one expert at most 32 times. `block_owner`: the 32 blocks of one device name one request at most 2 times.
All inputs are finite; a program needn't handle non-finite values. No bound on the sum of `cache_length` on one device may be relied on, other than what follows from the above.
Results may differ from the reference program's by a relative error of at most 0.00235.
The reference program's roundings to bfloat16 on the way count: a program that leaves them out, or rounds other values in their place, can miss the bound.
Values may be sent and summed in bfloat16 or wider, within the bound.
No kernel may reach another device: no remote copies, remote signals or barrier semaphores. Data moves between devices by JAX's collectives and lax.ppermute only.
A program may use at most 128 MiB of HBM per device.

```python
import math
import jax
import jax.numpy as jnp
import numpy as np
from jax import lax

D = 3584
FE_HALF = 512
H = 128
LAT = 576
VAL = 512
TOK_DEV = 32
CL = 1024
BLK = 4
NB = 32
REQS = 32
EXPERTS = 16
TOP = 8
CAP = 32
TOKENS = 1024
N_EP = 32
N_TP = 1


def drawn_entries():
    index = jnp.arange(LAT, dtype=jnp.int32)
    return jnp.logical_or(index >= VAL, index < VAL // 2)


def cache_parts(key):
    values = jnp.clip(jax.random.normal(key, (REQS, CL, LAT), jnp.float32), -5.0, 5.0)
    magnitude = jax.random.uniform(jax.random.fold_in(key, 11), (REQS, LAT), jnp.float32, 3.0, 5.0)
    signs = 2.0 * jax.random.randint(jax.random.fold_in(key, 12), (REQS, LAT), 0, 2).astype(jnp.float32) - 1.0
    strong = magnitude * signs
    aligned = drawn_entries()
    first_row = jnp.where(aligned[None, :], strong, values[:, 0, :])
    second_row = jnp.where(aligned[None, :], 0.99 * strong, values[:, 1, :])
    values = values.at[:, 0, :].set(first_row)
    values = values.at[:, 1, :].set(second_row)
    return (values, strong)


def draw_latent_cache(key, part):
    values, strong = cache_parts(key)
    return values.astype(jnp.bfloat16)


def aligned_query(noise, strong, lowest, highest):
    aligned = drawn_entries()
    count_aligned = LAT - VAL + VAL // 2
    heads_hit = min(8, H // 2)
    head_ids = jnp.arange(H, dtype=jnp.float32)
    strength = lowest + (highest - lowest) * head_ids / max(heads_hit - 1, 1)
    factor = strength * 192.0 ** 0.5 / (count_aligned * 16.33)
    hit = head_ids < heads_hit
    lined = factor[None, :, None] * strong[:, None, :]
    lined = jnp.where(aligned[None, None, :], lined, 0.0)
    values = jnp.where(hit[None, :, None], lined, noise)
    return jnp.clip(values, -40.0, 40.0)


def draw_query_latent(key, part):
    values, strong = cache_parts(key)
    key = jax.random.fold_in(key, 7)
    noise = jnp.clip(jax.random.normal(key, (REQS, H, LAT), jnp.float32), -5.0, 5.0)
    result = aligned_query(noise, strong, 100.0, 300.0)
    return result.astype(jnp.bfloat16)


def block_scale(rng, shape, split, least, high):
    loudness, own = 1.0, jax.random.fold_in(rng, 6)
    for axis_at, parts in split:
        draws = jnp.exp(jax.random.uniform(jax.random.fold_in(own, axis_at), (parts,), jnp.float32, least / len(split), high / len(split)))
        loudness = loudness * jnp.repeat(draws, shape[axis_at] // parts).reshape([-1 if axis == axis_at else 1 for axis in range(len(shape))])
    return loudness


def length_profile(amount, total, limit, slope):
    portions = [(1 << 20) // math.isqrt(grade ** slope) + 1 for grade in range(2, amount + 1)]
    surplus, holding = total - limit - (amount - 1), [1] * (amount - 1)
    while surplus > 0:
        free = [i for i in range(amount - 1) if holding[i] < limit]
        mass, budget = sum([portions[i] for i in free]), surplus
        for i in free:
            more = min(limit - holding[i], max(1, budget * portions[i] // mass), surplus)
            holding[i] = holding[i] + more
            surplus = surplus - more
    return np.array([limit] + holding)


def uneven(own_key, number_of, total, most, skew):
    if number_of == 2:
        one = jax.random.randint(own_key, (), max(1, total - most), min(most, total - 1) + 1)
        return jnp.stack([one, total - one])
    lengths = jnp.asarray(length_profile(number_of, total, most, skew), jnp.int32)
    pairs = (number_of - 1) // 2
    giver, taker = lengths[1:1 + 2 * pairs:2], lengths[2:2 + 2 * pairs:2]
    room = jnp.minimum(giver - 1, most - taker)
    shifted = jax.random.randint(jax.random.fold_in(own_key, 1), (pairs,), 0, 1 << 20) % (room + 1)
    lengths = lengths.at[1:1 + 2 * pairs:2].set(giver - shifted).at[2:2 + 2 * pairs:2].set(taker + shifted)
    return lengths[jax.random.permutation(jax.random.fold_in(own_key, 2), number_of)]


def assign_block(key, own, number, rows, count, top, limit, lean):
    order = jax.random.permutation(key, count)
    heavy_load, ordinary = shares(count, rows * top, limit, lean, True), shares(count, rows * top, limit, lean, False)
    places = jnp.arange(count)

    def named(tallies, turn):
        used = int((tallies > 0).sum())
        fixed = max(1, used // 4)
        moved = fixed + (places - fixed + turn * (used - fixed)) % max(1, count - fixed)
        return jnp.zeros((count,), jnp.int32).at[order[jnp.where(places < fixed, places, moved)]].set(jnp.asarray(tallies, jnp.int32))

    tallies = jnp.where(number % 4 == 0, named(heavy_load, number // 4), named(ordinary, number - number // 4 - 1))
    mixed = jax.random.permutation(jax.random.fold_in(own, 3), count)
    giver, receiver = mixed[0:count // 2 * 2:2], mixed[1:count // 2 * 2:2]
    room = jnp.minimum(tallies[giver] - 1, limit - tallies[receiver]) // 2
    room = jnp.where((giver == order[0]) | (receiver == order[0]) | (tallies[receiver] == 0), 0, jnp.maximum(room, 0))
    moved = jax.random.randint(jax.random.fold_in(own, 4), (count // 2,), 0, 1 << 20) % (room + 1)
    tallies = tallies.at[giver].add(-moved).at[receiver].add(moved)
    members = jnp.searchsorted(jnp.cumsum(tallies), jnp.arange(rows * top), side="right").astype(jnp.int32)
    listing = members.reshape(top, rows).T
    listing = listing[jax.random.permutation(jax.random.fold_in(own, 1), rows)]
    turn = jax.random.randint(jax.random.fold_in(own, 2), (rows, 1), 0, top)
    return jnp.take_along_axis(listing, (jnp.arange(top)[None, :] + turn) % top, axis=1)


def shares(count, total, limit, lean, full):
    portions = [(1 << 20) // math.isqrt(standing ** lean) + 1 for standing in range(1, count + 1)]
    largest = limit if full else min(limit, max(-(-total // count), total * portions[0] // sum(portions)))
    least = 1 if total - largest >= count - 1 else 0
    given, rest = [largest] + [least] * (count - 1), total - largest - least * (count - 1)
    while rest > 0:
        candidates = [i for i in range(1, count) if given[i] < largest] or [i for i in range(1, count) if given[i] < limit]
        pool, remaining = sum([portions[i] for i in candidates]), rest
        for i in candidates:
            addition = min(limit - given[i], max(1, remaining * portions[i] // pool), rest)
            given[i] = given[i] + addition
            rest = rest - addition
    return np.array(given)


def scatter_about(rng, dims, width, most, cuts=(), kind=jnp.bfloat16):
    entries = jax.random.normal(rng, dims, jnp.float32) * width
    if len(cuts) > 0:
        entries = block_scale(rng, dims, cuts, -0.22, 0.18) * entries
    return jnp.clip(entries, min=-most, max=most).astype(kind)


def setup_inputs(seed: int = 0, part: int = 0) -> dict:
    key_list = jax.random.split(jax.random.key(seed), 12)
    own_keys = jax.random.split(jax.random.fold_in(key_list[11], part), 12)
    query_latent = draw_query_latent(jax.random.fold_in(jax.random.fold_in(key_list[11], part), 71), part)
    latent_cache = draw_latent_cache(jax.random.fold_in(jax.random.fold_in(key_list[11], part), 71), part)
    cache_length = uneven(own_keys[2], REQS, N_EP * CL // 2, CL, 2).astype(jnp.int32)
    prefill_latent = scatter_about(own_keys[3], (N_EP, N_TP * NB, BLK, LAT), 1.0, 5.0, ((0, 32),))
    block_owner_keys = jax.random.split(jax.random.fold_in(own_keys[4], 1), N_EP * (N_TP * NB) // NB)
    block_owner_turns = jax.random.permutation(jax.random.fold_in(own_keys[4], 3), N_EP * (N_TP * NB) // NB)
    block_owner = jax.vmap(lambda own, number: assign_block(jax.random.fold_in(own_keys[4], 2), own, number, NB, N_EP, 1, 2, 1))(block_owner_keys, block_owner_turns).reshape((N_EP, N_TP * NB, 1))
    tokens = scatter_about(own_keys[5], (TOKENS, D), 1.0, 6.0, ((0, 32),))
    expert_ids_keys = jax.random.split(jax.random.fold_in(own_keys[6], 1), TOKENS // TOK_DEV)
    expert_ids_turns = jax.random.permutation(jax.random.fold_in(own_keys[6], 3), TOKENS // TOK_DEV)
    expert_ids = jax.vmap(lambda own, number: assign_block(jax.random.fold_in(own_keys[6], 2), own, number, TOK_DEV, EXPERTS, TOP, CAP, 2))(expert_ids_keys, expert_ids_turns).reshape((TOKENS, TOP))
    route_weight = jnp.clip(0.1 + 0.9 * jax.random.uniform(own_keys[7], (TOKENS, TOP), jnp.float32) ** block_scale(own_keys[7], (TOKENS, TOP), ((0, 32),), -0.2, 0.2), 0.1, 1.0)
    gate_weight = scatter_about(key_list[8], (N_EP, D, FE_HALF), D ** -0.5, 0.09375, ((0, 32),))
    up_weight = scatter_about(key_list[9], (N_EP, D, FE_HALF), D ** -0.5, 0.09375, ((0, 32),))
    down_weight = scatter_about(key_list[10], (N_EP, FE_HALF, D), (2 * FE_HALF) ** -0.5, 0.1875, ((0, 32),))
    return dict(query_latent=query_latent, latent_cache=latent_cache, cache_length=cache_length, prefill_latent=prefill_latent, block_owner=block_owner, tokens=tokens, expert_ids=expert_ids, route_weight=route_weight, gate_weight=gate_weight, up_weight=up_weight, down_weight=down_weight)


SCALE = 192.0 ** -0.5
NEG = -1.0e30


def latent_attention(query_latent, latent_cache, cache_length, prefill_latent, block_owner):
    count = N_EP * N_TP * NB
    flat_blocks = prefill_latent.reshape(count, BLK, LAT)
    owners = block_owner.reshape(count).astype(jnp.int32)
    order = jnp.argsort(owners, stable=True).astype(jnp.int32)
    loads = jnp.sum((owners[None, :] == jnp.arange(REQS, dtype=jnp.int32)[:, None]).astype(jnp.int32), axis=1).astype(jnp.int32)
    starts = (jnp.cumsum(loads) - loads).astype(jnp.int32)
    most = 2 * N_EP * N_TP

    def one_request(request):
        place = starts[request] + jnp.arange(most, dtype=jnp.int32)
        live = jnp.arange(most, dtype=jnp.int32) < loads[request]
        picked = order[jnp.minimum(place, count - 1)]
        blocks = flat_blocks[picked].reshape(most * BLK, LAT)
        keys = jnp.concatenate([latent_cache[request], blocks], axis=0)
        valid = jnp.concatenate([jnp.arange(CL, dtype=jnp.int32) < cache_length[request], jnp.repeat(live, BLK)])
        scores = lax.dot_general(query_latent[request], keys, (((1,), (1,)), ((), ())), preferred_element_type=jnp.float32) * SCALE
        scores = jnp.where(valid[None, :], scores, NEG)
        peak = jnp.max(scores, axis=1, keepdims=True)
        expo = jnp.where(valid[None, :], jnp.exp(scores - peak), 0.0)
        total = jnp.sum(expo, axis=1, keepdims=True)
        mixed = jnp.dot(expo.astype(jnp.bfloat16), keys[:, :VAL], preferred_element_type=jnp.float32)
        return (mixed / total).astype(jnp.bfloat16)

    return lax.map(one_request, jnp.arange(REQS, dtype=jnp.int32))


def expert_mix(tokens, expert_ids, route_weight, gate_weight, up_weight, down_weight):
    count = TOKENS * TOP
    flat = expert_ids.reshape(count).astype(jnp.int32)
    weights = route_weight.reshape(count)
    owners = (jnp.arange(count, dtype=jnp.int32) // TOP).astype(jnp.int32)
    order = jnp.argsort(flat, stable=True).astype(jnp.int32)
    loads = jnp.sum((flat[None, :] == jnp.arange(EXPERTS, dtype=jnp.int32)[:, None]).astype(jnp.int32), axis=1).astype(jnp.int32)
    starts = (jnp.cumsum(loads) - loads).astype(jnp.int32)
    most = N_EP * CAP

    def one_expert(summed_all, expert):
        place = starts[expert] + jnp.arange(most, dtype=jnp.int32)
        live = jnp.arange(most, dtype=jnp.int32) < loads[expert]
        picked = order[jnp.minimum(place, count - 1)]
        rows = tokens[owners[picked]]
        summed = jnp.zeros((most, D), jnp.float32)
        for half in range(2):
            index = 2 * expert + half
            gate = jnp.dot(rows, gate_weight[index], preferred_element_type=jnp.float32)
            upper = jnp.dot(rows, up_weight[index], preferred_element_type=jnp.float32)
            hidden = (jax.nn.silu(gate) * upper).astype(jnp.bfloat16)
            summed = summed + jnp.dot(hidden, down_weight[index], preferred_element_type=jnp.float32)
        scaled = jnp.where(live[:, None], summed * weights[picked][:, None], 0.0)
        return summed_all.at[owners[picked]].add(scaled), None

    summed_all, _ = lax.scan(one_expert, jnp.zeros((TOKENS, D), jnp.float32), jnp.arange(EXPERTS, dtype=jnp.int32))
    return summed_all.astype(jnp.bfloat16)


def reference(query_latent, latent_cache, cache_length, prefill_latent, block_owner, tokens, expert_ids, route_weight, gate_weight, up_weight, down_weight):
    attn_out = latent_attention(query_latent, latent_cache, cache_length, prefill_latent, block_owner)
    moe_out = expert_mix(tokens, expert_ids, route_weight, gate_weight, up_weight, down_weight)
    return (attn_out, moe_out)
```

```python
import jax
import jax.numpy as jnp
from jax import lax
from jax.sharding import PartitionSpec as P

VAL = 512


SCALE = 192.0 ** (-0.5)
NEG = -1e30


def combined_all(x, axis, combine):
    if lax.axis_size(axis) == 1:
        return x
    everything = jax.tree.map(lambda part: lax.all_gather(part, axis), x)
    leading = jax.tree.map(lambda part: part[0], everything)

    def lap(k, so_far):
        return combine(so_far, jax.tree.map(lambda part: part[k], everything))

    return lax.fori_loop(1, lax.axis_size(axis), lap, leading)


def attend_keys(query, keys, valid, value_width):
    scores = (
        lax.dot_general(query, keys, (((1,), (1,)), ((), ())), preferred_element_type=jnp.float32)
        * SCALE
    )
    scores = jnp.where(valid[None, :], scores, NEG)
    peak = jnp.max(scores, axis=1)
    expo = jnp.where(valid[None, :], jnp.exp(scores - peak[:, None]), 0.0)
    total = jnp.sum(expo, axis=1)
    mixed = jnp.dot(
        expo.astype(jnp.bfloat16), keys[:, :value_width], preferred_element_type=jnp.float32
    )
    return (peak, total, mixed)


def join_parts(first, second):
    peak = jnp.maximum(first[0], second[0])
    left = jnp.exp(first[0] - peak)
    right = jnp.exp(second[0] - peak)
    return (
        peak,
        first[1] * left + second[1] * right,
        first[2] * left[:, None] + second[2] * right[:, None],
    )


def per_device(
    query_latent,
    latent_cache,
    cache_length,
    prefill_latent,
    block_owner,
    tokens,
    expert_ids,
    route_weight,
    gate_weight,
    up_weight,
    down_weight,
):
    peers = lax.axis_size("ep")
    blocks = prefill_latent.shape[1]
    block_len = prefill_latent.shape[2]
    latent = prefill_latent.shape[3]
    tok_rows, top_k = expert_ids.shape

    rows = lax.all_gather(tokens, "ep", axis=0, tiled=True)

    owner = block_owner.reshape(blocks)
    same = owner[:, None] == owner[None, :]
    earlier = jnp.arange(blocks)[None, :] < jnp.arange(blocks)[:, None]
    order_in = jnp.sum(jnp.logical_and(same, earlier).astype(jnp.int32), axis=1)
    target = owner * 2 + order_in
    chosen = jnp.arange(2 * peers, dtype=jnp.int32)[:, None] == target[None, :]
    filled = jnp.sum(chosen.astype(jnp.float32), axis=1)
    expert_of = jnp.arange(peers, dtype=jnp.int32) // 2
    named = expert_ids[None, :, :] == expert_of[:, None, None]
    share = jnp.sum(jnp.where(named, route_weight[None, :, :], 0.0), axis=2)
    small = lax.all_to_all(
        jnp.concatenate([share, filled.reshape(peers, 2)], axis=1),
        "ep",
        split_axis=0,
        concat_axis=0,
        tiled=True,
    )
    scale_rows = small[:, :tok_rows].reshape(peers * tok_rows)
    present = small[:, tok_rows:].reshape(peers * 2)

    packed = jnp.dot(
        chosen.astype(jnp.bfloat16),
        prefill_latent.reshape(blocks, block_len * latent),
        preferred_element_type=jnp.float32,
    ).astype(jnp.bfloat16)
    arrived = lax.all_to_all(
        packed.reshape(peers, 2 * block_len, latent),
        "ep",
        split_axis=0,
        concat_axis=0,
        tiled=True,
    )
    shard_len = latent_cache.shape[1]
    positions = lax.axis_index("tp") * shard_len + jnp.arange(shard_len, dtype=jnp.int32)
    keys = jnp.concatenate(
        [latent_cache[0], arrived.reshape(peers * 2 * block_len, latent)], axis=0
    )
    valid = jnp.concatenate([positions < cache_length[0], jnp.repeat(present > 0, block_len)])
    peak, total, mixed = attend_keys(query_latent[0], keys, valid, VAL)
    peak, total, mixed = combined_all((peak, total, mixed), "tp", join_parts)
    attn_out = (mixed / total[:, None]).astype(jnp.bfloat16)[None]

    gate = jnp.dot(rows, gate_weight[0], preferred_element_type=jnp.float32)
    upper = jnp.dot(rows, up_weight[0], preferred_element_type=jnp.float32)
    hidden = (jax.nn.silu(gate) * upper).astype(jnp.bfloat16)
    if lax.axis_size("tp") > 1:
        hidden = lax.all_gather(hidden, "tp", axis=1, tiled=True)
    partial_out = (
        jnp.dot(hidden, down_weight[0], preferred_element_type=jnp.float32) * scale_rows[:, None]
    )
    combined = lax.psum_scatter(partial_out, "ep", scatter_dimension=0, tiled=True)
    moe_out = combined.astype(jnp.bfloat16)
    return (attn_out, moe_out)


def solution(mesh):
    in_specs = (
        P(("groups", "ep"), None, None),
        P(("groups", "ep"), "tp", None),
        P(("groups", "ep")),
        P(("groups", "ep"), "tp", None, None),
        P(("groups", "ep"), "tp", None),
        P(("groups", "ep"), None),
        P(("groups", "ep"), None),
        P(("groups", "ep"), None),
        P("ep", None, "tp"),
        P("ep", None, "tp"),
        P("ep", None, "tp"),
    )
    out_specs = (P(("groups", "ep"), None, None), P(("groups", "ep"), "tp"))
    return jax.shard_map(
        per_device, mesh=mesh, in_specs=in_specs, out_specs=out_specs, check_vma=False
    )
```

```python
import jax
import jax.numpy as jnp
from jax import lax
from jax.sharding import PartitionSpec as P

VAL = 512


SCALE = 192.0 ** (-0.5)
NEG = -1e30


def combined_all(x, axis, combine):
    if lax.axis_size(axis) == 1:
        return x
    everything = jax.tree.map(lambda part: lax.all_gather(part, axis), x)
    leading = jax.tree.map(lambda part: part[0], everything)

    def lap(k, so_far):
        return combine(so_far, jax.tree.map(lambda part: part[k], everything))

    return lax.fori_loop(1, lax.axis_size(axis), lap, leading)


def attend_keys(query, keys, valid, value_width):
    scores = (
        lax.dot_general(query, keys, (((1,), (1,)), ((), ())), preferred_element_type=jnp.float32)
        * SCALE
    )
    scores = jnp.where(valid[None, :], scores, NEG)
    peak = jnp.max(scores, axis=1)
    expo = jnp.where(valid[None, :], jnp.exp(scores - peak[:, None]), 0.0)
    total = jnp.sum(expo, axis=1)
    mixed = jnp.dot(
        expo.astype(jnp.bfloat16), keys[:, :value_width], preferred_element_type=jnp.float32
    )
    return (peak, total, mixed)


def join_parts(first, second):
    peak = jnp.maximum(first[0], second[0])
    left = jnp.exp(first[0] - peak)
    right = jnp.exp(second[0] - peak)
    return (
        peak,
        first[1] * left + second[1] * right,
        first[2] * left[:, None] + second[2] * right[:, None],
    )


def ring_experts(tokens, scale_rows, gate_weight, up_weight, down_weight):
    rows = lax.all_gather(tokens, "ep", axis=0, tiled=True)
    gate = jnp.dot(rows, gate_weight[0], preferred_element_type=jnp.float32)
    upper = jnp.dot(rows, up_weight[0], preferred_element_type=jnp.float32)
    hidden = (jax.nn.silu(gate) * upper).astype(jnp.bfloat16)
    if lax.axis_size("tp") > 1:
        hidden = lax.all_gather(hidden, "tp", axis=1, tiled=True)
    partial_out = (
        jnp.dot(hidden, down_weight[0], preferred_element_type=jnp.float32) * scale_rows[:, None]
    )
    return lax.psum_scatter(partial_out, "ep", scatter_dimension=0, tiled=True)


def grid_experts(tokens, share, gate_weight, up_weight, down_weight):
    peers = lax.axis_size("ep")
    chips = peers // 2
    planes = chips // 4

    def flip(value, chip_bits):
        return lax.ppermute(value, "ep", [(i, i ^ (2 * chip_bits)) for i in range(peers)])

    def swap(value):
        return lax.ppermute(value, "ep", [(i, i ^ 1) for i in range(peers)])

    gate_both = jnp.concatenate([gate_weight[0], swap(gate_weight[0])], axis=1)
    up_both = jnp.concatenate([up_weight[0], swap(up_weight[0])], axis=1)
    down_both = jnp.concatenate([down_weight[0], swap(down_weight[0])], axis=0)

    held = {}
    for plane in range(planes):
        held[plane, 0] = tokens if plane == 0 else flip(tokens, 4 * plane)
    for plane in range(planes):
        held[plane, 1] = flip(held[plane, 0], 1)
        held[plane, 2] = flip(held[plane, 0], 2)
        if plane % 2 == 0:
            held[plane, 3] = flip(held[plane, 2], 1)
        else:
            held[plane, 3] = flip(held[plane, 1], 2)

    tok_rows = tokens.shape[0]
    me = lax.axis_index("ep")
    slots = jnp.bitwise_xor(me, 2 * jnp.arange(chips, dtype=jnp.int32))
    picks = slots[:, None] == jnp.arange(peers, dtype=jnp.int32)[None, :]
    scales = jnp.sum(jnp.where(picks[:, :, None], share[None, :, :], 0.0), axis=1)

    partial_of = {}
    for first in range(planes - 2, -1, -2):
        keys = [(plane, kind) for plane in (first, first + 1) for kind in range(4)]
        rows = jnp.concatenate([held[key] for key in keys], axis=0)
        gate = jnp.dot(rows, gate_both, preferred_element_type=jnp.float32)
        upper = jnp.dot(rows, up_both, preferred_element_type=jnp.float32)
        hidden = (jax.nn.silu(gate) * upper).astype(jnp.bfloat16)
        scale = scales[4 * first : 4 * first + 8].reshape(8 * tok_rows)
        outs = jnp.dot(hidden, down_both, preferred_element_type=jnp.float32) * scale[:, None]
        for at, key in enumerate(keys):
            partial_of[key] = outs[at * tok_rows : (at + 1) * tok_rows]

    total = None
    for plane in range(planes - 1, -1, -1):
        if plane % 2 == 0:
            via_x = partial_of[plane, 1]
            via_y = partial_of[plane, 2] + flip(partial_of[plane, 3], 1)
        else:
            via_x = partial_of[plane, 1] + flip(partial_of[plane, 3], 2)
            via_y = partial_of[plane, 2]
        mine = partial_of[plane, 0] + flip(via_x, 1) + flip(via_y, 2)
        if plane > 0:
            mine = flip(mine, 4 * plane)
        total = mine if total is None else total + mine
    return total


def per_device(
    query_latent,
    latent_cache,
    cache_length,
    prefill_latent,
    block_owner,
    tokens,
    expert_ids,
    route_weight,
    gate_weight,
    up_weight,
    down_weight,
):
    peers = lax.axis_size("ep")
    blocks = prefill_latent.shape[1]
    block_len = prefill_latent.shape[2]
    latent = prefill_latent.shape[3]
    tok_rows, top_k = expert_ids.shape
    experts = peers // 2

    owner = block_owner.reshape(blocks)
    named = expert_ids[:, :, None] == jnp.arange(experts, dtype=jnp.int32)[None, None, :]
    share = jnp.sum(jnp.where(named, route_weight[:, :, None], 0.0), axis=1)
    routing = lax.all_gather(
        jnp.concatenate([share.reshape(tok_rows * experts), owner.astype(jnp.float32)]), "ep"
    )
    me = lax.axis_index("ep")
    share_all = routing[:, : tok_rows * experts].reshape(peers, tok_rows, experts)
    my_expert = jnp.arange(experts, dtype=jnp.int32) == me // 2
    share_mine = jnp.sum(jnp.where(my_expert[None, None, :], share_all, 0.0), axis=2)
    sent_here = jnp.sum(
        (routing[:, tok_rows * experts :] == me.astype(jnp.float32)).astype(jnp.int32), axis=1
    )
    present = (jnp.arange(2)[None, :] < sent_here[:, None]).reshape(peers * 2)

    same = owner[:, None] == owner[None, :]
    earlier = jnp.arange(blocks)[None, :] < jnp.arange(blocks)[:, None]
    order_in = jnp.sum(jnp.logical_and(same, earlier).astype(jnp.int32), axis=1)
    target = owner * 2 + order_in
    chosen = jnp.arange(2 * peers, dtype=jnp.int32)[:, None] == target[None, :]
    packed = jnp.dot(
        chosen.astype(jnp.bfloat16),
        prefill_latent.reshape(blocks, block_len * latent),
        preferred_element_type=jnp.float32,
    ).astype(jnp.bfloat16)
    arrived = lax.all_to_all(
        packed.reshape(peers, 2 * block_len, latent),
        "ep",
        split_axis=0,
        concat_axis=0,
        tiled=True,
    )
    shard_len = latent_cache.shape[1]
    positions = lax.axis_index("tp") * shard_len + jnp.arange(shard_len, dtype=jnp.int32)
    keys = jnp.concatenate(
        [latent_cache[0], arrived.reshape(peers * 2 * block_len, latent)], axis=0
    )
    valid = jnp.concatenate([positions < cache_length[0], jnp.repeat(present, block_len)])
    peak, total, mixed = attend_keys(query_latent[0], keys, valid, VAL)
    peak, total, mixed = combined_all((peak, total, mixed), "tp", join_parts)
    attn_out = (mixed / total[:, None]).astype(jnp.bfloat16)[None]

    if peers == 32 and lax.axis_size("tp") == 1:
        combined = grid_experts(tokens, share_mine, gate_weight, up_weight, down_weight)
    else:
        combined = ring_experts(
            tokens, share_mine.reshape(peers * tok_rows), gate_weight, up_weight, down_weight
        )
    moe_out = combined.astype(jnp.bfloat16)
    return (attn_out, moe_out)


def solution(mesh):
    in_specs = (
        P(("groups", "ep"), None, None),
        P(("groups", "ep"), "tp", None),
        P(("groups", "ep")),
        P(("groups", "ep"), "tp", None, None),
        P(("groups", "ep"), "tp", None),
        P(("groups", "ep"), None),
        P(("groups", "ep"), None),
        P(("groups", "ep"), None),
        P("ep", None, "tp"),
        P("ep", None, "tp"),
        P("ep", None, "tp"),
    )
    out_specs = (P(("groups", "ep"), None, None), P(("groups", "ep"), "tp"))
    return jax.shard_map(
        per_device, mesh=mesh, in_specs=in_specs, out_specs=out_specs, check_vma=False
    )
```

```python
import functools

import jax
import jax.numpy as jnp
from jax import lax
from jax.experimental import pallas as pl
from jax.experimental.pallas import tpu as pltpu
from jax.sharding import PartitionSpec as P

VAL = 512


SCALE = 192.0 ** (-0.5)
NEG = -1e30


def combined_all(x, axis, combine):
    if lax.axis_size(axis) == 1:
        return x
    everything = jax.tree.map(lambda part: lax.all_gather(part, axis), x)
    leading = jax.tree.map(lambda part: part[0], everything)

    def lap(k, so_far):
        return combine(so_far, jax.tree.map(lambda part: part[k], everything))

    return lax.fori_loop(1, lax.axis_size(axis), lap, leading)


def attend_keys(query, keys, valid, value_width):
    scores = (
        lax.dot_general(query, keys, (((1,), (1,)), ((), ())), preferred_element_type=jnp.float32)
        * SCALE
    )
    scores = jnp.where(valid[None, :], scores, NEG)
    peak = jnp.max(scores, axis=1)
    expo = jnp.where(valid[None, :], jnp.exp(scores - peak[:, None]), 0.0)
    total = jnp.sum(expo, axis=1)
    mixed = jnp.dot(
        expo.astype(jnp.bfloat16), keys[:, :value_width], preferred_element_type=jnp.float32
    )
    return (peak, total, mixed)


def join_parts(first, second):
    peak = jnp.maximum(first[0], second[0])
    left = jnp.exp(first[0] - peak)
    right = jnp.exp(second[0] - peak)
    return (
        peak,
        first[1] * left + second[1] * right,
        first[2] * left[:, None] + second[2] * right[:, None],
    )


def ring_experts(tokens, share, gate_weight, up_weight, down_weight):
    rows = lax.all_gather(tokens, "ep", axis=0, tiled=True)
    gate = jnp.dot(rows, gate_weight[0], preferred_element_type=jnp.float32)
    upper = jnp.dot(rows, up_weight[0], preferred_element_type=jnp.float32)
    hidden = (jax.nn.silu(gate) * upper).astype(jnp.bfloat16)
    if lax.axis_size("tp") > 1:
        hidden = lax.all_gather(hidden, "tp", axis=1, tiled=True)
    partial_out = jnp.dot(hidden, down_weight[0], preferred_element_type=jnp.float32)
    scaled = partial_out * share.reshape(-1)[:, None]
    return lax.psum_scatter(scaled, "ep", scatter_dimension=0, tiled=True).astype(jnp.bfloat16)


VMEM_LIMIT = 48 * 1024 * 1024


def hidden_kernel(chips, chip_ref, rows_ref, gate_ref, up_ref, hidden_ref):
    rows = rows_ref[...]
    gate = jnp.dot(rows, gate_ref[...], preferred_element_type=jnp.float32)
    upper = jnp.dot(rows, up_ref[...], preferred_element_type=jnp.float32)
    hidden = (gate / (1.0 + jnp.exp(-gate)) * upper).astype(jnp.bfloat16)
    unit = rows.shape[0] // chips
    for chip in range(chips):
        slot = jnp.bitwise_xor(chip_ref[0], chip)
        place = pl.ds(pl.multiple_of(slot * unit, unit), unit)
        hidden_ref[place, :] = hidden[chip * unit : (chip + 1) * unit]


def expert_hidden(chip, rows, gate, up, chips):
    count, width = rows.shape
    units = gate.shape[1]
    tile = 256
    return pl.pallas_call(
        functools.partial(hidden_kernel, chips),
        grid=(units // tile,),
        in_specs=[
            pl.BlockSpec(memory_space=pltpu.SMEM),
            pl.BlockSpec((count, width), lambda i: (0, 0)),
            pl.BlockSpec((width, tile), lambda i: (0, i)),
            pl.BlockSpec((width, tile), lambda i: (0, i)),
        ],
        out_specs=pl.BlockSpec((count, tile), lambda i: (0, i)),
        out_shape=jax.ShapeDtypeStruct((count, units), jnp.bfloat16),
        compiler_params=pltpu.CompilerParams(vmem_limit_bytes=VMEM_LIMIT),
        cost_estimate=pl.CostEstimate(
            flops=4 * count * width * units,
            bytes_accessed=2 * (count * width + 2 * width * units + count * units),
            transcendentals=count * units,
        ),
        name="expert_hidden",
    )(chip, rows, gate, up)


def output_kernel(scale_ref, first_ref, second_ref, down_ref, down_other_ref, out_ref):
    out = jnp.dot(first_ref[...], down_ref[...], preferred_element_type=jnp.float32)
    out += jnp.dot(second_ref[...], down_other_ref[...], preferred_element_type=jnp.float32)
    out_ref[...] = out * scale_ref[...]


def expert_output(plane, scale, first, second, down, down_other):
    units, width = down.shape
    count = first.shape[0] // 4
    tile = width // 4
    return pl.pallas_call(
        output_kernel,
        grid=(4,),
        in_specs=[
            pl.BlockSpec((count, 1), lambda i: (plane, 0)),
            pl.BlockSpec((count, units), lambda i: (plane, 0)),
            pl.BlockSpec((count, units), lambda i: (plane, 0)),
            pl.BlockSpec((units, tile), lambda i: (0, i)),
            pl.BlockSpec((units, tile), lambda i: (0, i)),
        ],
        out_specs=pl.BlockSpec((count, tile), lambda i: (0, i)),
        out_shape=jax.ShapeDtypeStruct((count, width), jnp.float32),
        compiler_params=pltpu.CompilerParams(vmem_limit_bytes=VMEM_LIMIT),
        cost_estimate=pl.CostEstimate(
            flops=4 * count * width * units,
            bytes_accessed=4 * width * units + 4 * count * width,
            transcendentals=0,
        ),
        name="expert_output",
    )(scale, first, second, down, down_other)


def round_kernel(has_recv, has_plane, has_next, has_done, *refs):
    refs = list(refs)
    take = lambda: refs.pop(0)
    from_x, from_y = (take(), take()) if has_recv else (None, None)
    slot_x, slot_y = (take(), take()) if has_plane else (None, None)
    slot_d = take() if has_next else None
    own = take() if has_done else None
    at = 0
    to_x, to_y = (take(), take()) if has_plane or has_next else (None, None)
    head = own.shape[0] if has_done else 0
    if has_plane:
        unit = slot_x.shape[0]
        half = unit // 2
        to_x[:half] = slot_x[:half]
        to_x[half:unit] = slot_x[half:] + from_y[head : head + half]
        to_y[:half] = slot_y[:half] + from_x[head : head + half]
        to_y[half:unit] = slot_y[half:]
        at = unit
    if has_next:
        half = slot_d.shape[0] // 2
        to_x[at : at + half] = slot_d[:half]
        to_y[at : at + half] = slot_d[half:]
    if has_done:
        done = take()
        done[...] = own[...] + from_x[:head] + from_y[:head]


def message_round(received, plane, following, finished):
    parts = [part for part in (plane, following, finished) if part is not None]
    count, width = parts[0].shape
    unit = count // 4
    tile = width // 4
    operands, in_specs, out_specs, out_shape = [], [], [], []

    def whole(array, out=False):
        spec = pl.BlockSpec((array.shape[0], tile), lambda i: (0, i))
        if out:
            out_specs.append(spec)
            out_shape.append(array)
        else:
            operands.append(array)
            in_specs.append(spec)

    def slot(array, at):
        operands.append(array)
        in_specs.append(pl.BlockSpec((unit, tile), lambda i: (at, i)))

    if received is not None:
        whole(received[0])
        whole(received[1])
    if plane is not None:
        slot(plane, 1)
        slot(plane, 2)
    if following is not None:
        slot(following, 3)
    if finished is not None:
        slot(finished, 0)
    length = (unit if plane is not None else 0) + (unit // 2 if following is not None else 0)
    if length:
        whole(jax.ShapeDtypeStruct((length, width), jnp.float32), True)
        whole(jax.ShapeDtypeStruct((length, width), jnp.float32), True)
    if finished is not None:
        whole(jax.ShapeDtypeStruct((unit, width), jnp.float32), True)
    return pl.pallas_call(
        functools.partial(
            round_kernel,
            received is not None,
            plane is not None,
            following is not None,
            finished is not None,
        ),
        grid=(4,),
        in_specs=in_specs,
        out_specs=out_specs,
        out_shape=out_shape,
        compiler_params=pltpu.CompilerParams(vmem_limit_bytes=VMEM_LIMIT),
        cost_estimate=pl.CostEstimate(
            flops=4 * unit * width, bytes_accessed=40 * unit * width, transcendentals=0
        ),
        name="message_round",
    )(*operands)


def grid_experts(tokens, share, gate_weight, up_weight, down_weight):
    peers = lax.axis_size("ep")
    chips = peers // 2
    planes = chips // 4
    tok_rows = tokens.shape[0]
    me = lax.axis_index("ep")

    def flip(value, chip_bits):
        return lax.ppermute(value, "ep", [(i, i ^ (2 * chip_bits)) for i in range(peers)])

    def swap(value):
        return lax.ppermute(value, "ep", [(i, i ^ 1) for i in range(peers)])

    same_core = [list(range(core, peers, 2)) for core in range(2)]
    rows = lax.all_gather(tokens, "ep", axis=0, tiled=True, axis_index_groups=same_core)
    gate_other, up_other, down_other = swap(gate_weight[0]), swap(up_weight[0]), swap(down_weight[0])

    slots = jnp.bitwise_xor(me, 2 * jnp.arange(chips, dtype=jnp.int32))
    picks = slots[:, None] == jnp.arange(peers, dtype=jnp.int32)[None, :]
    scale = jnp.sum(jnp.where(picks[:, :, None], share[None, :, :], 0.0), axis=1)
    scale = scale.reshape(chips * tok_rows, 1)

    chip = (me // 2).astype(jnp.int32).reshape(1)
    first = expert_hidden(chip, rows, gate_weight[0], up_weight[0], chips)
    second = expert_hidden(chip, rows, gate_other, up_other, chips)
    outs = {
        plane: expert_output(plane, scale, first, second, down_weight[0], down_other)
        for plane in range(planes)
    }

    received, sums = None, []
    for plane in range(planes, -2, -1):
        results = list(
            message_round(
                received,
                outs.get(plane),
                outs.get(plane - 1),
                outs.get(plane + 1),
            )
        )
        if plane >= 0:
            received = (flip(results[0], 1), flip(results[1], 2))
            results = results[2:]
        if results:
            sums.append(flip(results[0], 4 * (plane + 1)) if plane >= 0 else results[0])
    total = sums[-1]
    for part in sums[:-1]:
        total = total + part
    return total.astype(jnp.bfloat16)


def per_device(
    query_latent,
    latent_cache,
    cache_length,
    prefill_latent,
    block_owner,
    tokens,
    expert_ids,
    route_weight,
    gate_weight,
    up_weight,
    down_weight,
):
    peers = lax.axis_size("ep")
    blocks = prefill_latent.shape[1]
    block_len = prefill_latent.shape[2]
    latent = prefill_latent.shape[3]
    tok_rows, top_k = expert_ids.shape

    owner = block_owner.reshape(blocks)
    same = owner[:, None] == owner[None, :]
    earlier = jnp.arange(blocks)[None, :] < jnp.arange(blocks)[:, None]
    order_in = jnp.sum(jnp.logical_and(same, earlier).astype(jnp.int32), axis=1)
    target = owner * 2 + order_in
    chosen = jnp.arange(2 * peers, dtype=jnp.int32)[:, None] == target[None, :]
    packed = jnp.dot(
        chosen.astype(jnp.bfloat16),
        prefill_latent.reshape(blocks, block_len * latent),
        preferred_element_type=jnp.float32,
    ).astype(jnp.bfloat16)

    expert_of = jnp.arange(peers, dtype=jnp.int32) // 2
    named = expert_ids[None, :, :] == expert_of[:, None, None]
    share = jnp.sum(jnp.where(named, route_weight[None, :, :], 0.0), axis=2)
    high = lax.reduce_precision(share, 8, 7)
    middle = lax.reduce_precision(share - high, 8, 7)
    low = share - high - middle
    filled = jnp.sum(chosen.astype(jnp.float32), axis=1).reshape(peers, 1, 2)
    side = jnp.zeros((peers, 2 * block_len, max(tok_rows, 2)), jnp.float32)
    side = side.at[:, :3, :tok_rows].set(jnp.stack([high, middle, low], axis=1))
    side = side.at[:, 3:4, :2].set(filled)
    arrived = lax.all_to_all(
        jnp.concatenate(
            [packed.reshape(peers, 2 * block_len, latent), side.astype(jnp.bfloat16)], axis=2
        ),
        "ep",
        split_axis=0,
        concat_axis=0,
        tiled=True,
    )
    side_in = arrived[:, :, latent:].astype(jnp.float32)
    share_in = side_in[:, 0, :tok_rows] + side_in[:, 1, :tok_rows] + side_in[:, 2, :tok_rows]
    present = side_in[:, 3, :2].reshape(peers * 2)
    arrived = arrived[:, :, :latent]
    shard_len = latent_cache.shape[1]
    positions = lax.axis_index("tp") * shard_len + jnp.arange(shard_len, dtype=jnp.int32)
    keys = jnp.concatenate(
        [latent_cache[0], arrived.reshape(peers * 2 * block_len, latent)], axis=0
    )
    valid = jnp.concatenate([positions < cache_length[0], jnp.repeat(present > 0, block_len)])
    peak, total, mixed = attend_keys(query_latent[0], keys, valid, VAL)
    peak, total, mixed = combined_all((peak, total, mixed), "tp", join_parts)
    attn_out = (mixed / total[:, None]).astype(jnp.bfloat16)[None]

    if peers == 32 and lax.axis_size("tp") == 1:
        serve = grid_experts
    else:
        serve = ring_experts
    moe_out = serve(tokens, share_in, gate_weight, up_weight, down_weight)
    return (attn_out, moe_out)


def solution(mesh):
    in_specs = (
        P(("groups", "ep"), None, None),
        P(("groups", "ep"), "tp", None),
        P(("groups", "ep")),
        P(("groups", "ep"), "tp", None, None),
        P(("groups", "ep"), "tp", None),
        P(("groups", "ep"), None),
        P(("groups", "ep"), None),
        P(("groups", "ep"), None),
        P("ep", None, "tp"),
        P("ep", None, "tp"),
        P("ep", None, "tp"),
    )
    out_specs = (P(("groups", "ep"), None, None), P(("groups", "ep"), "tp"))
    return jax.shard_map(
        per_device, mesh=mesh, in_specs=in_specs, out_specs=out_specs, check_vma=False
    )
```

```python
import functools

import jax
import jax.numpy as jnp
from jax import lax
from jax.experimental import pallas as pl
from jax.experimental.pallas import tpu as pltpu
from jax.sharding import PartitionSpec as P

VAL = 512


SCALE = 192.0 ** (-0.5)
NEG = -1e30


def combined_all(x, axis, combine):
    if lax.axis_size(axis) == 1:
        return x
    everything = jax.tree.map(lambda part: lax.all_gather(part, axis), x)
    leading = jax.tree.map(lambda part: part[0], everything)

    def lap(k, so_far):
        return combine(so_far, jax.tree.map(lambda part: part[k], everything))

    return lax.fori_loop(1, lax.axis_size(axis), lap, leading)


def attend_keys(query, keys, valid, value_width):
    scores = (
        lax.dot_general(query, keys, (((1,), (1,)), ((), ())), preferred_element_type=jnp.float32)
        * SCALE
    )
    scores = jnp.where(valid[None, :], scores, NEG)
    peak = jnp.max(scores, axis=1)
    expo = jnp.where(valid[None, :], jnp.exp(scores - peak[:, None]), 0.0)
    total = jnp.sum(expo, axis=1)
    mixed = jnp.dot(
        expo.astype(jnp.bfloat16), keys[:, :value_width], preferred_element_type=jnp.float32
    )
    return (peak, total, mixed)


def join_parts(first, second):
    peak = jnp.maximum(first[0], second[0])
    left = jnp.exp(first[0] - peak)
    right = jnp.exp(second[0] - peak)
    return (
        peak,
        first[1] * left + second[1] * right,
        first[2] * left[:, None] + second[2] * right[:, None],
    )


def ring_experts(tokens, share, gate_weight, up_weight, down_weight):
    rows = lax.all_gather(tokens, "ep", axis=0, tiled=True)
    gate = jnp.dot(rows, gate_weight[0], preferred_element_type=jnp.float32)
    upper = jnp.dot(rows, up_weight[0], preferred_element_type=jnp.float32)
    hidden = (jax.nn.silu(gate) * upper).astype(jnp.bfloat16)
    if lax.axis_size("tp") > 1:
        hidden = lax.all_gather(hidden, "tp", axis=1, tiled=True)
    partial_out = jnp.dot(hidden, down_weight[0], preferred_element_type=jnp.float32)
    scaled = partial_out * share.reshape(-1)[:, None]
    return lax.psum_scatter(scaled, "ep", scatter_dimension=0, tiled=True).astype(jnp.bfloat16)


MIB = 1024 * 1024


def hidden_kernel(places, *refs):
    sources = refs[: len(places)]
    gate_ref, up_ref, gate_other_ref, up_other_ref, hidden_ref, rows_ref = refs[len(places) :]
    step = pl.program_id(0)
    own_steps = pl.num_programs(0) // 2

    @pl.when(step == 0)
    def _():
        at = 0
        for source, (start, stop) in zip(sources, places):
            rows_ref[at : at + stop - start] = source[start:stop]
            at += stop - start

    def units(gate_tile, up_tile):
        rows = rows_ref[...]
        gate = jnp.dot(rows, gate_tile[...], preferred_element_type=jnp.float32)
        upper = jnp.dot(rows, up_tile[...], preferred_element_type=jnp.float32)
        hidden_ref[...] = (gate / (1.0 + jnp.exp(-gate)) * upper).astype(jnp.bfloat16)

    @pl.when(step < own_steps)
    def _():
        units(gate_ref, up_ref)

    @pl.when(step >= own_steps)
    def _():
        units(gate_other_ref, up_other_ref)


def packed_weights(gate, up, down, after):
    width, units = gate.shape
    blocks = width // units

    def kernel(gate_ref, up_ref, down_ref, after_ref, out_ref, sems):
        copies = [
            pltpu.make_async_copy(gate_ref, out_ref.at[pl.ds(0, width)], sems.at[0]),
            pltpu.make_async_copy(up_ref, out_ref.at[pl.ds(width, width)], sems.at[1]),
        ]
        for at in range(blocks):
            copies.append(
                pltpu.make_async_copy(
                    down_ref.at[:, pl.ds(at * units, units)],
                    out_ref.at[pl.ds(2 * width + at * units, units)],
                    sems.at[2 + at],
                )
            )
        for copy in copies:
            copy.start()
        for copy in copies:
            copy.wait()

    return pl.pallas_call(
        kernel,
        in_specs=[pl.BlockSpec(memory_space=pl.ANY)] * 4,
        out_specs=pl.BlockSpec(memory_space=pl.ANY),
        out_shape=jax.ShapeDtypeStruct((3 * width, units), gate.dtype),
        scratch_shapes=[pltpu.SemaphoreType.DMA((2 + blocks,))],
        compiler_params=pltpu.CompilerParams(vmem_limit_bytes=56 * MIB),
        cost_estimate=pl.CostEstimate(
            flops=0, bytes_accessed=12 * width * units, transcendentals=0
        ),
        name="packed_weights",
    )(gate, up, down, after)


def expert_hidden(pieces, gate, up, other):
    width, units = gate.shape
    count = sum(stop - start for _, start, stop in pieces)
    tile = 256
    steps = units // tile
    own = pl.BlockSpec((width, tile), lambda i: (0, jnp.minimum(i, steps - 1)))
    gate_other = pl.BlockSpec((width, tile), lambda i: (0, jnp.maximum(i - steps, 0)))
    up_other = pl.BlockSpec((width, tile), lambda i: (1, jnp.maximum(i - steps, 0)))
    return pl.pallas_call(
        functools.partial(hidden_kernel, [(start, stop) for _, start, stop in pieces]),
        grid=(2 * steps,),
        in_specs=[pl.BlockSpec(array.shape, lambda i: (0, 0)) for array, _, _ in pieces]
        + [own, own, gate_other, up_other],
        out_specs=pl.BlockSpec((count, tile), lambda i: (0, i)),
        out_shape=jax.ShapeDtypeStruct((count, 2 * units), jnp.bfloat16),
        scratch_shapes=[pltpu.VMEM((count, width), jnp.bfloat16)],
        compiler_params=pltpu.CompilerParams(vmem_limit_bytes=52 * MIB),
        cost_estimate=pl.CostEstimate(
            flops=8 * count * width * units,
            bytes_accessed=2 * (count * width + 4 * width * units + 2 * count * units),
            transcendentals=2 * count * units,
        ),
        name="expert_hidden",
    )(*[array for array, _, _ in pieces], gate, up, other, other)


def output_kernel(scale_ref, hidden_ref, down_ref, down_other_ref, *out_refs):
    units = down_ref.shape[0]
    hidden = hidden_ref[...]
    out = jnp.dot(hidden[:, :units], down_ref[...], preferred_element_type=jnp.float32)
    out += jnp.dot(hidden[:, units:], down_other_ref[...], preferred_element_type=jnp.float32)
    out = out * scale_ref[...]
    unit = out_refs[0].shape[0]
    for at, out_ref in enumerate(out_refs):
        out_ref[...] = out[at * unit : (at + 1) * unit]


def expert_output(plane, block, unit, scale, hidden, down, other):
    units, width = down.shape
    steps = width // units
    slot = jax.ShapeDtypeStruct((unit, width), jnp.float32)
    return pl.pallas_call(
        output_kernel,
        grid=(steps,),
        in_specs=[
            pl.BlockSpec((4 * unit, 1), lambda i: (plane, 0)),
            pl.BlockSpec((4 * unit, 2 * units), lambda i: (block, 0)),
            pl.BlockSpec((units, units), lambda i: (0, i)),
            pl.BlockSpec((units, units), lambda i: (2 * steps + i, 0)),
        ],
        out_specs=[pl.BlockSpec((unit, units), lambda i: (0, i))] * 4,
        out_shape=[slot] * 4,
        compiler_params=pltpu.CompilerParams(vmem_limit_bytes=44 * MIB),
        cost_estimate=pl.CostEstimate(
            flops=16 * unit * width * units,
            bytes_accessed=4 * width * units + 16 * unit * width,
            transcendentals=0,
        ),
        name="expert_output",
    )(scale, hidden, down, other)


def whole_call(kernel, operands, out_shape, name):
    return pl.pallas_call(
        kernel,
        in_specs=[pl.BlockSpec(memory_space=pltpu.VMEM)] * len(operands),
        out_specs=[pl.BlockSpec(memory_space=pltpu.VMEM)] * len(out_shape),
        out_shape=out_shape,
        compiler_params=pltpu.CompilerParams(vmem_limit_bytes=12 * MIB),
        cost_estimate=pl.CostEstimate(
            flops=0,
            bytes_accessed=sum(x.size * x.dtype.itemsize for x in list(operands) + list(out_shape)),
            transcendentals=0,
        ),
        name=name,
    )(*operands)


def gather_round(unit, column, from_x, from_y, extra):
    width = from_x.shape[1]
    half = unit // 2
    head = unit if column is not None else 0
    operands = [x for x in (from_x, from_y, column, extra) if x is not None]
    message = jax.ShapeDtypeStruct((head + half, width), from_x.dtype)
    out_shape = [message, message] + ([extra] if extra is not None else [])

    def kernel(x_ref, y_ref, *refs):
        refs = list(refs)
        column_ref = refs.pop(0) if column is not None else None
        extra_ref = refs.pop(0) if extra is not None else None
        if column is not None:
            refs[0][:head] = column_ref[...]
            refs[1][:head] = column_ref[...]
        refs[0][head:] = y_ref[:half]
        refs[1][head:] = x_ref[half:unit]
        if extra is not None:
            refs[2][...] = extra_ref[...]

    return whole_call(kernel, operands, out_shape, "gather_round")


def scatter_round(received, plane, following, finished, column, base=()):
    unit, width = (plane or following or finished)[0].shape
    half = unit // 2
    operands = list(received) if received is not None else []
    operands += [plane[1], plane[2]] if plane is not None else []
    operands += [following[3]] if following is not None else []
    operands += [finished[0]] if finished is not None else []
    operands += list(column) + list(base)
    length = (unit if plane is not None else 0) + (half if following is not None else 0)
    out_shape = [jax.ShapeDtypeStruct((length, width), jnp.float32)] * 2 if length else []
    if finished is not None:
        out_shape = out_shape + [jax.ShapeDtypeStruct((unit, width), jnp.float32)]
    if base:
        out_shape = out_shape + [jax.ShapeDtypeStruct((unit, width), jnp.float32)]
    head = unit if finished is not None else 0

    def kernel(*refs):
        refs = list(refs)
        from_x, from_y = (refs.pop(0), refs.pop(0)) if received is not None else (None, None)
        at = 0
        slot_x, slot_y = (refs.pop(0), refs.pop(0)) if plane is not None else (None, None)
        slot_d = refs.pop(0) if following is not None else None
        own = refs.pop(0) if finished is not None else None
        more = [refs.pop(0) for _ in column]
        bases = [refs.pop(0) for _ in base]
        if base:
            refs.pop()[...] = bases[0][...] + bases[1][...]
        if plane is not None:
            refs[0][:half] = slot_x[:half]
            refs[0][half:unit] = slot_x[half:] + from_y[head : head + half]
            refs[1][:half] = slot_y[:half] + from_x[head : head + half]
            refs[1][half:unit] = slot_y[half:]
            at = unit
        if following is not None:
            refs[0][at : at + half] = slot_d[:half]
            refs[1][at : at + half] = slot_d[half:]
        if finished is not None:
            total = own[...] + from_x[:head] + from_y[:head]
            for part in more:
                total = total + part[...]
            refs[-1][...] = total

    return list(whole_call(kernel, operands, out_shape, "scatter_round"))


def grid_experts(tokens, share, gate_weight, up_weight, down_weight):
    peers = lax.axis_size("ep")
    chips = peers // 2
    unit = tokens.shape[0]
    half = unit // 2
    me = lax.axis_index("ep")

    def flip(value, chip_bits):
        return lax.ppermute(value, "ep", [(i, i ^ (2 * chip_bits)) for i in range(peers)])

    def swap(value):
        return lax.ppermute(value, "ep", [(i, i ^ 1) for i in range(peers)])

    gate, up, down = gate_weight[0], up_weight[0], down_weight[0]

    column = {0: tokens, 1: flip(tokens, 4), 2: flip(tokens, 8)}
    by_x, by_y = {0: flip(tokens, 1)}, {0: flip(tokens, 2)}
    for plane in (1, 2, 3):
        extra = tokens if plane == 1 else None
        to_x, to_y, *passed = gather_round(
            unit, column[plane], by_x[plane - 1], by_y[plane - 1], extra
        )
        by_x[plane], by_y[plane] = flip(to_x, 1), flip(to_y, 2)
        if passed:
            column[3] = flip(passed[0], 12)
            other = swap(packed_weights(gate, up, down, to_x))
    to_x, to_y = gather_round(unit, None, by_x[3], by_y[3], None)
    by_x[4], by_y[4] = flip(to_x, 1), flip(to_y, 2)

    slots = jnp.bitwise_xor(me, 2 * jnp.arange(chips, dtype=jnp.int32))
    picks = slots[:, None] == jnp.arange(peers, dtype=jnp.int32)[None, :]
    scale = jnp.sum(jnp.where(picks[:, :, None], share[None, :, :], 0.0), axis=1)
    scale = scale.reshape(chips * unit, 1)

    def plane_rows(plane):
        tail = unit if plane < 3 else 0
        return [
            (column[plane], 0, unit),
            (by_x[plane], 0, unit),
            (by_y[plane], 0, unit),
            (by_x[plane + 1], tail, tail + half),
            (by_y[plane + 1], tail, tail + half),
        ]

    outs = {}
    for planes in ((0, 1), (2,), (3,)):
        pieces = [piece for plane in planes for piece in plane_rows(plane)]
        hidden = expert_hidden(pieces, gate, up, other)
        for block, plane in enumerate(planes):
            outs[plane] = expert_output(plane, block, unit, scale, hidden, down, other)

    order = [2, 3, 1, 0]
    sums = []
    received = None
    for at in range(-1, len(order)):
        plane = outs[order[at]] if at >= 0 else None
        following = outs[order[at + 1]] if at + 1 < len(order) else None
        finished = outs[order[at - 1]] if at >= 1 else None
        base = (outs[0][0], sums[0]) if at == 3 else ()
        results = scatter_round(received, plane, following, finished, [], base)
        received = (flip(results[0], 1), flip(results[1], 2))
        if finished is not None:
            sums.append(flip(results[2], 4 * order[at - 1]))
    own = (results[3],)
    (total,) = scatter_round(received, None, None, own, sums[1:])
    return total.astype(jnp.bfloat16)


def per_device(
    query_latent,
    latent_cache,
    cache_length,
    prefill_latent,
    block_owner,
    tokens,
    expert_ids,
    route_weight,
    gate_weight,
    up_weight,
    down_weight,
):
    peers = lax.axis_size("ep")
    blocks = prefill_latent.shape[1]
    block_len = prefill_latent.shape[2]
    latent = prefill_latent.shape[3]
    tok_rows, top_k = expert_ids.shape

    owner = block_owner.reshape(blocks)
    same = owner[:, None] == owner[None, :]
    earlier = jnp.arange(blocks)[None, :] < jnp.arange(blocks)[:, None]
    order_in = jnp.sum(jnp.logical_and(same, earlier).astype(jnp.int32), axis=1)
    target = owner * 2 + order_in
    chosen = jnp.arange(2 * peers, dtype=jnp.int32)[:, None] == target[None, :]
    packed = jnp.dot(
        chosen.astype(jnp.bfloat16),
        prefill_latent.reshape(blocks, block_len * latent),
        preferred_element_type=jnp.float32,
    ).astype(jnp.bfloat16)

    expert_of = jnp.arange(peers, dtype=jnp.int32) // 2
    named = expert_ids[None, :, :] == expert_of[:, None, None]
    share = jnp.sum(jnp.where(named, route_weight[None, :, :], 0.0), axis=2)
    high = lax.reduce_precision(share, 8, 7)
    middle = lax.reduce_precision(share - high, 8, 7)
    low = share - high - middle
    filled = jnp.sum(chosen.astype(jnp.float32), axis=1).reshape(peers, 1, 2)
    side = jnp.zeros((peers, 2 * block_len, max(tok_rows, 2)), jnp.float32)
    side = side.at[:, :3, :tok_rows].set(jnp.stack([high, middle, low], axis=1))
    side = side.at[:, 3:4, :2].set(filled)
    arrived = lax.all_to_all(
        jnp.concatenate(
            [packed.reshape(peers, 2 * block_len, latent), side.astype(jnp.bfloat16)], axis=2
        ),
        "ep",
        split_axis=0,
        concat_axis=0,
        tiled=True,
    )
    side_in = arrived[:, :, latent:].astype(jnp.float32)
    share_in = side_in[:, 0, :tok_rows] + side_in[:, 1, :tok_rows] + side_in[:, 2, :tok_rows]
    present = side_in[:, 3, :2].reshape(peers * 2)
    arrived = arrived[:, :, :latent]
    shard_len = latent_cache.shape[1]
    positions = lax.axis_index("tp") * shard_len + jnp.arange(shard_len, dtype=jnp.int32)
    keys = jnp.concatenate(
        [latent_cache[0], arrived.reshape(peers * 2 * block_len, latent)], axis=0
    )
    valid = jnp.concatenate([positions < cache_length[0], jnp.repeat(present > 0, block_len)])
    peak, total, mixed = attend_keys(query_latent[0], keys, valid, VAL)
    peak, total, mixed = combined_all((peak, total, mixed), "tp", join_parts)
    attn_out = (mixed / total[:, None]).astype(jnp.bfloat16)[None]

    if peers == 32 and lax.axis_size("tp") == 1:
        serve = grid_experts
    else:
        serve = ring_experts
    moe_out = serve(tokens, share_in, gate_weight, up_weight, down_weight)
    return (attn_out, moe_out)


def solution(mesh):
    in_specs = (
        P(("groups", "ep"), None, None),
        P(("groups", "ep"), "tp", None),
        P(("groups", "ep")),
        P(("groups", "ep"), "tp", None, None),
        P(("groups", "ep"), "tp", None),
        P(("groups", "ep"), None),
        P(("groups", "ep"), None),
        P(("groups", "ep"), None),
        P("ep", None, "tp"),
        P("ep", None, "tp"),
        P("ep", None, "tp"),
    )
    out_specs = (P(("groups", "ep"), None, None), P(("groups", "ep"), "tp"))
    return jax.shard_map(
        per_device, mesh=mesh, in_specs=in_specs, out_specs=out_specs, check_vma=False
    )
```

```python
import functools

import jax
import jax.numpy as jnp
from jax import lax
from jax.experimental import pallas as pl
from jax.experimental.pallas import tpu as pltpu
from jax.sharding import PartitionSpec as P

VAL = 512


SCALE = 192.0 ** (-0.5)
NEG = -1e30


def combined_all(x, axis, combine):
    if lax.axis_size(axis) == 1:
        return x
    everything = jax.tree.map(lambda part: lax.all_gather(part, axis), x)
    leading = jax.tree.map(lambda part: part[0], everything)

    def lap(k, so_far):
        return combine(so_far, jax.tree.map(lambda part: part[k], everything))

    return lax.fori_loop(1, lax.axis_size(axis), lap, leading)


def attend_keys(query, keys, valid, value_width):
    scores = (
        lax.dot_general(query, keys, (((1,), (1,)), ((), ())), preferred_element_type=jnp.float32)
        * SCALE
    )
    scores = jnp.where(valid[None, :], scores, NEG)
    peak = jnp.max(scores, axis=1)
    expo = jnp.where(valid[None, :], jnp.exp(scores - peak[:, None]), 0.0)
    total = jnp.sum(expo, axis=1)
    mixed = jnp.dot(
        expo.astype(jnp.bfloat16), keys[:, :value_width], preferred_element_type=jnp.float32
    )
    return (peak, total, mixed)


def join_parts(first, second):
    peak = jnp.maximum(first[0], second[0])
    left = jnp.exp(first[0] - peak)
    right = jnp.exp(second[0] - peak)
    return (
        peak,
        first[1] * left + second[1] * right,
        first[2] * left[:, None] + second[2] * right[:, None],
    )


def ring_experts(tokens, share, gate_weight, up_weight, down_weight):
    rows = lax.all_gather(tokens, "ep", axis=0, tiled=True)
    gate = jnp.dot(rows, gate_weight[0], preferred_element_type=jnp.float32)
    upper = jnp.dot(rows, up_weight[0], preferred_element_type=jnp.float32)
    hidden = (jax.nn.silu(gate) * upper).astype(jnp.bfloat16)
    if lax.axis_size("tp") > 1:
        hidden = lax.all_gather(hidden, "tp", axis=1, tiled=True)
    partial_out = jnp.dot(hidden, down_weight[0], preferred_element_type=jnp.float32)
    scaled = partial_out * share.reshape(-1)[:, None]
    return lax.psum_scatter(scaled, "ep", scatter_dimension=0, tiled=True).astype(jnp.bfloat16)


MIB = 1024 * 1024


def hidden_kernel(places, *refs):
    sources = refs[: len(places)]
    gate_ref, up_ref, gate_other_ref, up_other_ref, hidden_ref, rows_ref = refs[len(places) :]
    step = pl.program_id(0)
    own_steps = pl.num_programs(0) // 2

    @pl.when(step == 0)
    def _():
        at = 0
        for source, (start, stop) in zip(sources, places):
            rows_ref[at : at + stop - start] = source[start:stop]
            at += stop - start

    def units(gate_tile, up_tile):
        rows = rows_ref[...]
        gate = jnp.dot(rows, gate_tile[...], preferred_element_type=jnp.float32)
        upper = jnp.dot(rows, up_tile[...], preferred_element_type=jnp.float32)
        hidden_ref[...] = (gate / (1.0 + jnp.exp(-gate)) * upper).astype(jnp.bfloat16)

    @pl.when(step < own_steps)
    def _():
        units(gate_ref, up_ref)

    @pl.when(step >= own_steps)
    def _():
        units(gate_other_ref, up_other_ref)


def packed_weights(gate, up, down):
    width, units = gate.shape
    blocks = [down[:, at : at + units] for at in range(0, width, units)]
    return jnp.concatenate([gate, up] + blocks, axis=0)


def expert_hidden(pieces, gate, up, other):
    width, units = gate.shape
    count = sum(stop - start for _, start, stop in pieces)
    tile = 256
    steps = units // tile
    own = pl.BlockSpec((width, tile), lambda i: (0, jnp.minimum(i, steps - 1)))
    gate_other = pl.BlockSpec((width, tile), lambda i: (0, jnp.maximum(i - steps, 0)))
    up_other = pl.BlockSpec((width, tile), lambda i: (1, jnp.maximum(i - steps, 0)))
    return pl.pallas_call(
        functools.partial(hidden_kernel, [(start, stop) for _, start, stop in pieces]),
        grid=(2 * steps,),
        in_specs=[pl.BlockSpec(array.shape, lambda i: (0, 0)) for array, _, _ in pieces]
        + [own, own, gate_other, up_other],
        out_specs=pl.BlockSpec((count, tile), lambda i: (0, i)),
        out_shape=jax.ShapeDtypeStruct((count, 2 * units), jnp.bfloat16),
        scratch_shapes=[pltpu.VMEM((count, width), jnp.bfloat16)],
        compiler_params=pltpu.CompilerParams(vmem_limit_bytes=52 * MIB),
        cost_estimate=pl.CostEstimate(
            flops=8 * count * width * units,
            bytes_accessed=2 * (count * width + 4 * width * units + 2 * count * units),
            transcendentals=2 * count * units,
        ),
        name="expert_hidden",
    )(*[array for array, _, _ in pieces], gate, up, other, other)


def output_kernel(scale_ref, hidden_ref, down_ref, down_other_ref, *out_refs):
    units = down_ref.shape[0]
    hidden = hidden_ref[...]
    out = jnp.dot(hidden[:, :units], down_ref[...], preferred_element_type=jnp.float32)
    out += jnp.dot(hidden[:, units:], down_other_ref[...], preferred_element_type=jnp.float32)
    out = out * scale_ref[...]
    unit = out_refs[0].shape[0]
    for at, out_ref in enumerate(out_refs):
        out_ref[...] = out[at * unit : (at + 1) * unit]


def expert_output(unit, scale, hidden, down, other):
    units, width = down.shape
    count = hidden.shape[0]
    slots = count // unit
    steps = width // units
    return pl.pallas_call(
        output_kernel,
        grid=(steps,),
        in_specs=[
            pl.BlockSpec((count, 1), lambda i: (0, 0)),
            pl.BlockSpec((count, 2 * units), lambda i: (0, 0)),
            pl.BlockSpec((units, units), lambda i: (0, i)),
            pl.BlockSpec((units, units), lambda i: (2 * steps + i, 0)),
        ],
        out_specs=[pl.BlockSpec((unit, units), lambda i: (0, i))] * slots,
        out_shape=[jax.ShapeDtypeStruct((unit, width), jnp.float32)] * slots,
        compiler_params=pltpu.CompilerParams(vmem_limit_bytes=44 * MIB),
        cost_estimate=pl.CostEstimate(
            flops=4 * count * width * units,
            bytes_accessed=4 * width * units + 4 * count * width,
            transcendentals=0,
        ),
        name="expert_output",
    )(scale, hidden, down, other)


def whole_call(kernel, operands, out_shape, name, after=()):
    given = len(operands)

    def body(*refs):
        kernel(*refs[:given], *refs[given + len(after) :])

    return pl.pallas_call(
        body,
        in_specs=[pl.BlockSpec(memory_space=pltpu.VMEM)] * given
        + [pl.BlockSpec(memory_space=pl.ANY)] * len(after),
        out_specs=[pl.BlockSpec(memory_space=pltpu.VMEM)] * len(out_shape),
        out_shape=out_shape,
        compiler_params=pltpu.CompilerParams(vmem_limit_bytes=12 * MIB),
        cost_estimate=pl.CostEstimate(
            flops=0,
            bytes_accessed=sum(x.size * x.dtype.itemsize for x in list(operands) + list(out_shape)),
            transcendentals=0,
        ),
        name=name,
    )(*operands, *after)


def gather_round(unit, column, from_x, from_y, extra, after=()):
    width = from_x.shape[1]
    half = unit // 2
    head = unit if column is not None else 0
    operands = [x for x in (from_x, from_y, column, extra) if x is not None]
    message = jax.ShapeDtypeStruct((head + half, width), from_x.dtype)
    out_shape = [message, message] + ([extra] if extra is not None else [])

    def kernel(x_ref, y_ref, *refs):
        refs = list(refs)
        column_ref = refs.pop(0) if column is not None else None
        extra_ref = refs.pop(0) if extra is not None else None
        if column is not None:
            refs[0][:head] = column_ref[...]
            refs[1][:head] = column_ref[...]
        refs[0][head:] = y_ref[:half]
        refs[1][head:] = x_ref[half:unit]
        if extra is not None:
            refs[2][...] = extra_ref[...]

    return whole_call(kernel, operands, out_shape, "gather_round", after)


def scatter_round(received, plane, following, finished, column, base=()):
    unit, width = (plane or following or finished)[0].shape
    half = unit // 2
    operands = list(received) if received is not None else []
    operands += [plane[1], plane[2]] if plane is not None else []
    operands += [following[3]] if following is not None else []
    operands += [finished[0]] if finished is not None else []
    operands += list(column) + list(base)
    length = (unit if plane is not None else 0) + (half if following is not None else 0)
    out_shape = [jax.ShapeDtypeStruct((length, width), jnp.float32)] * 2 if length else []
    if finished is not None:
        out_shape = out_shape + [jax.ShapeDtypeStruct((unit, width), jnp.float32)]
    if base:
        out_shape = out_shape + [jax.ShapeDtypeStruct((unit, width), jnp.float32)]
    head = unit if finished is not None else 0

    def kernel(*refs):
        refs = list(refs)
        from_x, from_y = (refs.pop(0), refs.pop(0)) if received is not None else (None, None)
        at = 0
        slot_x, slot_y = (refs.pop(0), refs.pop(0)) if plane is not None else (None, None)
        slot_d = refs.pop(0) if following is not None else None
        own = refs.pop(0) if finished is not None else None
        more = [refs.pop(0) for _ in column]
        bases = [refs.pop(0) for _ in base]
        if base:
            refs.pop()[...] = bases[0][...] + bases[1][...]
        if plane is not None:
            refs[0][:half] = slot_x[:half]
            refs[0][half:unit] = slot_x[half:] + from_y[head : head + half]
            refs[1][:half] = slot_y[:half] + from_x[head : head + half]
            refs[1][half:unit] = slot_y[half:]
            at = unit
        if following is not None:
            refs[0][at : at + half] = slot_d[:half]
            refs[1][at : at + half] = slot_d[half:]
        if finished is not None:
            total = own[...] + from_x[:head] + from_y[:head]
            for part in more:
                total = total + part[...]
            refs[-1][...] = total

    return list(whole_call(kernel, operands, out_shape, "scatter_round"))


def grid_experts(tokens, share, gate_weight, up_weight, down_weight):
    peers = lax.axis_size("ep")
    chips = peers // 2
    unit = tokens.shape[0]
    half = unit // 2
    me = lax.axis_index("ep")

    def flip(value, chip_bits):
        return lax.ppermute(value, "ep", [(i, i ^ (2 * chip_bits)) for i in range(peers)])

    def swap(value):
        return lax.ppermute(value, "ep", [(i, i ^ 1) for i in range(peers)])

    gate, up, down = gate_weight[0], up_weight[0], down_weight[0]

    other = swap(packed_weights(gate, up, down))
    gathered = [0, 2, 3, 1]
    column = {0: tokens, 2: flip(tokens, 8)}
    by_x, by_y = [flip(tokens, 1)], [flip(tokens, 2)]

    def plane_rows(at):
        tail = unit if at < 3 else 0
        return [
            (column[gathered[at]], 0, unit),
            (by_x[at], 0, unit),
            (by_y[at], 0, unit),
            (by_x[at + 1], tail, tail + half),
            (by_y[at + 1], tail, tail + half),
        ]

    hidden = []
    for at in (1, 2, 3, 4):
        plane = gathered[at] if at < 4 else None
        extra = tokens if at < 3 else None
        to_x, to_y, *passed = gather_round(
            unit, column.get(plane), by_x[-1], by_y[-1], extra, hidden if at == 4 else ()
        )
        by_x.append(flip(to_x, 1))
        by_y.append(flip(to_y, 2))
        if passed:
            column[gathered[at + 1]] = flip(passed[0], 4 * gathered[at + 1])
        if at in (2, 4):
            rows = plane_rows(at - 2) + plane_rows(at - 1)
            hidden.append(expert_hidden(rows, gate, up, other))

    slots = jnp.bitwise_xor(me, 2 * jnp.arange(chips, dtype=jnp.int32))
    picks = slots[:, None] == jnp.arange(peers, dtype=jnp.int32)[None, :]
    scale = jnp.sum(jnp.where(picks[:, :, None], share[None, :, :], 0.0), axis=1)

    outs = {}
    for units, planes in zip(hidden, (gathered[:2], gathered[2:])):
        group_scale = jnp.concatenate([scale[4 * plane : 4 * plane + 4] for plane in planes])
        results = expert_output(unit, group_scale.reshape(8 * unit, 1), units, down, other)
        for place, plane in enumerate(planes):
            outs[plane] = results[4 * place : 4 * place + 4]

    order = [2, 3, 1, 0]
    base, along_z = outs[0][0], None
    received = None
    for at in range(-1, len(order)):
        plane = outs[order[at]] if at >= 0 else None
        following = outs[order[at + 1]] if at + 1 < len(order) else None
        finished = outs[order[at - 1]] if at >= 1 else None
        bases = (base, along_z) if along_z is not None else ()
        results = scatter_round(received, plane, following, finished, [], bases)
        received = (flip(results[0], 1), flip(results[1], 2))
        if bases:
            base = results[3]
        if finished is not None:
            along_z = flip(results[2], 4 * order[at - 1])
    (total,) = scatter_round(received, None, None, (base,), [along_z])
    return total.astype(jnp.bfloat16)


def per_device(
    query_latent,
    latent_cache,
    cache_length,
    prefill_latent,
    block_owner,
    tokens,
    expert_ids,
    route_weight,
    gate_weight,
    up_weight,
    down_weight,
):
    peers = lax.axis_size("ep")
    blocks = prefill_latent.shape[1]
    block_len = prefill_latent.shape[2]
    latent = prefill_latent.shape[3]
    tok_rows, top_k = expert_ids.shape

    owner = block_owner.reshape(blocks)
    same = owner[:, None] == owner[None, :]
    earlier = jnp.arange(blocks)[None, :] < jnp.arange(blocks)[:, None]
    order_in = jnp.sum(jnp.logical_and(same, earlier).astype(jnp.int32), axis=1)
    target = owner * 2 + order_in
    chosen = jnp.arange(2 * peers, dtype=jnp.int32)[:, None] == target[None, :]
    packed = jnp.dot(
        chosen.astype(jnp.bfloat16),
        prefill_latent.reshape(blocks, block_len * latent),
        preferred_element_type=jnp.float32,
    ).astype(jnp.bfloat16)

    expert_of = jnp.arange(peers, dtype=jnp.int32) // 2
    named = expert_ids[None, :, :] == expert_of[:, None, None]
    share = jnp.sum(jnp.where(named, route_weight[None, :, :], 0.0), axis=2)
    high = lax.reduce_precision(share, 8, 7)
    middle = lax.reduce_precision(share - high, 8, 7)
    low = share - high - middle
    filled = jnp.sum(chosen.astype(jnp.float32), axis=1).reshape(peers, 1, 2)
    side = jnp.zeros((peers, 2 * block_len, max(tok_rows, 2)), jnp.float32)
    side = side.at[:, :3, :tok_rows].set(jnp.stack([high, middle, low], axis=1))
    side = side.at[:, 3:4, :2].set(filled)
    arrived = lax.all_to_all(
        jnp.concatenate(
            [packed.reshape(peers, 2 * block_len, latent), side.astype(jnp.bfloat16)], axis=2
        ),
        "ep",
        split_axis=0,
        concat_axis=0,
        tiled=True,
    )
    side_in = arrived[:, :, latent:].astype(jnp.float32)
    share_in = side_in[:, 0, :tok_rows] + side_in[:, 1, :tok_rows] + side_in[:, 2, :tok_rows]
    present = side_in[:, 3, :2].reshape(peers * 2)
    arrived = arrived[:, :, :latent]
    shard_len = latent_cache.shape[1]
    positions = lax.axis_index("tp") * shard_len + jnp.arange(shard_len, dtype=jnp.int32)
    keys = jnp.concatenate(
        [latent_cache[0], arrived.reshape(peers * 2 * block_len, latent)], axis=0
    )
    valid = jnp.concatenate([positions < cache_length[0], jnp.repeat(present > 0, block_len)])
    peak, total, mixed = attend_keys(query_latent[0], keys, valid, VAL)
    peak, total, mixed = combined_all((peak, total, mixed), "tp", join_parts)
    attn_out = (mixed / total[:, None]).astype(jnp.bfloat16)[None]

    if peers == 32 and lax.axis_size("tp") == 1:
        serve = grid_experts
    else:
        serve = ring_experts
    moe_out = serve(tokens, share_in, gate_weight, up_weight, down_weight)
    return (attn_out, moe_out)


def solution(mesh):
    in_specs = (
        P(("groups", "ep"), None, None),
        P(("groups", "ep"), "tp", None),
        P(("groups", "ep")),
        P(("groups", "ep"), "tp", None, None),
        P(("groups", "ep"), "tp", None),
        P(("groups", "ep"), None),
        P(("groups", "ep"), None),
        P(("groups", "ep"), None),
        P("ep", None, "tp"),
        P("ep", None, "tp"),
        P("ep", None, "tp"),
    )
    out_specs = (P(("groups", "ep"), None, None), P(("groups", "ep"), "tp"))
    return jax.shard_map(
        per_device, mesh=mesh, in_specs=in_specs, out_specs=out_specs, check_vma=False
    )
```

```python
import functools

import jax
import jax.numpy as jnp
from jax import lax
from jax.experimental import pallas as pl
from jax.experimental.pallas import tpu as pltpu
from jax.sharding import PartitionSpec as P

VAL = 512


SCALE = 192.0 ** (-0.5)
NEG = -1e30


def combined_all(x, axis, combine):
    if lax.axis_size(axis) == 1:
        return x
    everything = jax.tree.map(lambda part: lax.all_gather(part, axis), x)
    leading = jax.tree.map(lambda part: part[0], everything)

    def lap(k, so_far):
        return combine(so_far, jax.tree.map(lambda part: part[k], everything))

    return lax.fori_loop(1, lax.axis_size(axis), lap, leading)


def attend_keys(query, keys, valid, value_width):
    scores = (
        lax.dot_general(query, keys, (((1,), (1,)), ((), ())), preferred_element_type=jnp.float32)
        * SCALE
    )
    scores = jnp.where(valid[None, :], scores, NEG)
    peak = jnp.max(scores, axis=1)
    expo = jnp.where(valid[None, :], jnp.exp(scores - peak[:, None]), 0.0)
    total = jnp.sum(expo, axis=1)
    mixed = jnp.dot(
        expo.astype(jnp.bfloat16), keys[:, :value_width], preferred_element_type=jnp.float32
    )
    return (peak, total, mixed)


def join_parts(first, second):
    peak = jnp.maximum(first[0], second[0])
    left = jnp.exp(first[0] - peak)
    right = jnp.exp(second[0] - peak)
    return (
        peak,
        first[1] * left + second[1] * right,
        first[2] * left[:, None] + second[2] * right[:, None],
    )


def ring_experts(tokens, share, gate_weight, up_weight, down_weight):
    rows = lax.all_gather(tokens, "ep", axis=0, tiled=True)
    gate = jnp.dot(rows, gate_weight[0], preferred_element_type=jnp.float32)
    upper = jnp.dot(rows, up_weight[0], preferred_element_type=jnp.float32)
    hidden = (jax.nn.silu(gate) * upper).astype(jnp.bfloat16)
    if lax.axis_size("tp") > 1:
        hidden = lax.all_gather(hidden, "tp", axis=1, tiled=True)
    partial_out = jnp.dot(hidden, down_weight[0], preferred_element_type=jnp.float32)
    scaled = partial_out * share.reshape(-1)[:, None]
    return lax.psum_scatter(scaled, "ep", scatter_dimension=0, tiled=True).astype(jnp.bfloat16)


MIB = 1024 * 1024

LINKS = (1, 2, 4, 12)


def across(value, link):
    peers = lax.axis_size("ep")
    return lax.ppermute(value, "ep", [(i, i ^ (2 * LINKS[link])) for i in range(peers)])


def swap_cores(value):
    return lax.ppermute(value, "ep", [(i, i ^ 1) for i in range(lax.axis_size("ep"))])


def slot_of(bits, quarter, top_first):
    count = len(LINKS)
    slot = 0
    for i in range(count):
        at = count - 1 - i if top_first else i
        slot |= ((bits >> at) & 1) << ((quarter + i) % count)
    return slot


def whole_call(kernel, operands, out_shape, name, after=()):
    given = len(operands)

    def body(*refs):
        kernel(*refs[:given], *refs[given + len(after) :])

    return pl.pallas_call(
        body,
        in_specs=[pl.BlockSpec(memory_space=pltpu.VMEM)] * given
        + [pl.BlockSpec(memory_space=pl.ANY)] * len(after),
        out_specs=[pl.BlockSpec(memory_space=pltpu.VMEM)] * len(out_shape),
        out_shape=out_shape,
        compiler_params=pltpu.CompilerParams(vmem_limit_bytes=12 * MIB),
        cost_estimate=pl.CostEstimate(
            flops=0,
            bytes_accessed=sum(x.size * x.dtype.itemsize for x in list(operands) + list(out_shape)),
            transcendentals=0,
        ),
        name=name,
    )(*operands, *after)


def joined(held, got, after):
    count = len(held)
    out_shape = [jax.ShapeDtypeStruct((2 * x.shape[0], x.shape[1]), x.dtype) for x in held]

    def kernel(*refs):
        for first, second, out in zip(refs[:count], refs[count : 2 * count], refs[2 * count :]):
            rows = first.shape[0]
            out[:rows] = first[...]
            out[rows:] = second[...]

    return whole_call(kernel, [*held, *got], out_shape, "joined", after)


def hold_back(array, after):
    def kernel(in_ref, out_ref):
        out_ref[...] = in_ref[...]

    shape = jax.ShapeDtypeStruct(array.shape, array.dtype)
    return whole_call(kernel, [array], [shape], "hold_back", (after,))[0]


def gather_cube(tokens, others):
    count = len(LINKS)
    width = tokens.shape[1] // count
    held = [tokens[:, q * width : (q + 1) * width] for q in range(count)]
    for phase in range(count):
        got = [across(held[q], (q + phase) % count) for q in range(count)]
        if phase < count - 1:
            held = joined(held, got, others if phase == 1 else ())
    return held, got


def hidden_kernel(unit, *refs):
    count = len(LINKS)
    held, got = refs[:count], refs[count : 2 * count]
    gate_ref, up_ref, gate_other_ref, up_other_ref, hidden_ref, rows_ref = refs[2 * count :]
    step = pl.program_id(0)
    own_steps = pl.num_programs(0) // 2

    @pl.when(step == 0)
    def _():
        for quarter in range(count):
            half, width = held[quarter].shape
            columns = slice(quarter * width, (quarter + 1) * width)
            for place in range(2 * half // unit):
                source = held[quarter] if place * unit < half else got[quarter]
                at = place * unit % half
                slot = slot_of(place, quarter, False)
                rows_ref[slot * unit : (slot + 1) * unit, columns] = source[at : at + unit]

    def units(gate_tile, up_tile):
        rows = rows_ref[...]
        gate = jnp.dot(rows, gate_tile[...], preferred_element_type=jnp.float32)
        upper = jnp.dot(rows, up_tile[...], preferred_element_type=jnp.float32)
        hidden_ref[...] = (gate / (1.0 + jnp.exp(-gate)) * upper).astype(jnp.bfloat16)

    @pl.when(step < own_steps)
    def _():
        units(gate_ref, up_ref)

    @pl.when(step >= own_steps)
    def _():
        units(gate_other_ref, up_other_ref)


def expert_hidden(unit, held, got, gate, up, gate_other, up_other):
    width, units = gate.shape
    count = 2 * held[0].shape[0]
    tile = 256
    steps = units // tile
    own = pl.BlockSpec((width, tile), lambda i: (0, jnp.minimum(i, steps - 1)))
    other = pl.BlockSpec((width, tile), lambda i: (0, jnp.maximum(i - steps, 0)))
    return pl.pallas_call(
        functools.partial(hidden_kernel, unit),
        grid=(2 * steps,),
        in_specs=[pl.BlockSpec(array.shape, lambda i: (0, 0)) for array in (*held, *got)]
        + [own, own, other, other],
        out_specs=pl.BlockSpec((count, tile), lambda i: (0, i)),
        out_shape=jax.ShapeDtypeStruct((count, 2 * units), jnp.bfloat16),
        scratch_shapes=[pltpu.VMEM((count, width), jnp.bfloat16)],
        compiler_params=pltpu.CompilerParams(vmem_limit_bytes=48 * MIB),
        cost_estimate=pl.CostEstimate(
            flops=8 * count * width * units,
            bytes_accessed=2 * (count * width + 4 * width * units + 2 * count * units),
            transcendentals=2 * count * units,
        ),
        name="expert_hidden",
    )(*held, *got, gate, up, gate_other, up_other)


def output_kernel(unit, quarter, scale_ref, hidden_ref, down_ref, down_other_ref, keep_ref, send_ref):
    units = down_ref.shape[0]
    places = hidden_ref.shape[0] // unit
    for out_ref, first in ((send_ref, places // 2), (keep_ref, 0)):
        slots = [slot_of(first + at, quarter, True) for at in range(places // 2)]
        rows = [slice(slot * unit, (slot + 1) * unit) for slot in slots]
        hidden = jnp.concatenate([hidden_ref[row] for row in rows], axis=0)
        scale = jnp.concatenate([scale_ref[row] for row in rows], axis=0)
        out = jnp.dot(hidden[:, :units], down_ref[...], preferred_element_type=jnp.float32)
        out += jnp.dot(hidden[:, units:], down_other_ref[...], preferred_element_type=jnp.float32)
        out_ref[...] = out * scale


def expert_output(unit, quarter, scale, hidden, down, down_other):
    units, width = down.shape
    tile = width // len(LINKS)
    count = hidden.shape[0]
    half = jax.ShapeDtypeStruct((count // 2, tile), jnp.float32)
    return pl.pallas_call(
        functools.partial(output_kernel, unit, quarter),
        grid=(1,),
        in_specs=[
            pl.BlockSpec((count, 1), lambda i: (0, 0)),
            pl.BlockSpec((count, 2 * units), lambda i: (0, 0)),
            pl.BlockSpec((units, tile), lambda i: (0, quarter)),
            pl.BlockSpec((units, tile), lambda i: (0, quarter)),
        ],
        out_specs=[pl.BlockSpec((count // 2, tile), lambda i: (0, 0))] * 2,
        out_shape=[half] * 2,
        compiler_params=pltpu.CompilerParams(vmem_limit_bytes=32 * MIB),
        cost_estimate=pl.CostEstimate(
            flops=4 * count * tile * units,
            bytes_accessed=4 * tile * units + 4 * count * (tile + units),
            transcendentals=0,
        ),
        name="expert_output",
    )(scale, hidden, down, down_other)


def halved(keep, got):
    rows, width = keep.shape
    half = jax.ShapeDtypeStruct((rows // 2, width), keep.dtype)

    def kernel(keep_ref, got_ref, first_ref, second_ref):
        second_ref[...] = keep_ref[rows // 2 :] + got_ref[rows // 2 :]
        first_ref[...] = keep_ref[: rows // 2] + got_ref[: rows // 2]

    return whole_call(kernel, [keep, got], [half, half], "halved")


def finished(keep, got):
    count = len(keep)
    rows, width = keep[0].shape

    def kernel(*refs):
        for q in range(count):
            total = refs[q][...] + refs[count + q][...]
            refs[2 * count][:, q * width : (q + 1) * width] = total.astype(jnp.bfloat16)

    shape = jax.ShapeDtypeStruct((rows, count * width), jnp.bfloat16)
    return whole_call(kernel, [*keep, *got], [shape], "finished")[0]


def cube_experts(unit, gathered, share, weights, others):
    count = len(LINKS)
    peers = lax.axis_size("ep")
    gate, up, down = weights
    gate_other, up_other, down_other = others
    steps = []
    for slot in range(peers // 2):
        step = 0
        for link in range(count):
            step ^= LINKS[link] * ((slot >> link) & 1)
        steps.append(2 * step)
    source = jnp.bitwise_xor(lax.axis_index("ep"), jnp.array(steps, jnp.int32))
    picks = source[:, None] == jnp.arange(peers, dtype=jnp.int32)[None, :]
    scale = jnp.sum(jnp.where(picks[:, :, None], share[None, :, :], 0.0), axis=1)
    scale = scale.reshape(peers // 2 * unit, 1)

    hidden = expert_hidden(unit, *gathered, gate, up, gate_other, up_other)
    keep, got = [], []
    for q in range(count):
        mine, send = expert_output(unit, q, scale, hidden, down, down_other)
        keep.append(mine)
        got.append(across(send, q))
    for phase in range(1, count):
        for q in range(count):
            keep[q], send = halved(keep[q], got[q])
            got[q] = across(send, (q + phase) % count)
    return finished(keep, got)


def per_device(
    query_latent,
    latent_cache,
    cache_length,
    prefill_latent,
    block_owner,
    tokens,
    expert_ids,
    route_weight,
    gate_weight,
    up_weight,
    down_weight,
):
    peers = lax.axis_size("ep")
    blocks = prefill_latent.shape[1]
    block_len = prefill_latent.shape[2]
    latent = prefill_latent.shape[3]
    tok_rows, top_k = expert_ids.shape

    owner = block_owner.reshape(blocks)
    same = owner[:, None] == owner[None, :]
    earlier = jnp.arange(blocks)[None, :] < jnp.arange(blocks)[:, None]
    order_in = jnp.sum(jnp.logical_and(same, earlier).astype(jnp.int32), axis=1)
    target = owner * 2 + order_in
    chosen = jnp.arange(2 * peers, dtype=jnp.int32)[:, None] == target[None, :]
    packed = jnp.dot(
        chosen.astype(jnp.bfloat16),
        prefill_latent.reshape(blocks, block_len * latent),
        preferred_element_type=jnp.float32,
    ).astype(jnp.bfloat16)

    expert_of = jnp.arange(peers, dtype=jnp.int32) // 2
    named = expert_ids[None, :, :] == expert_of[:, None, None]
    share = jnp.sum(jnp.where(named, route_weight[None, :, :], 0.0), axis=2)
    high = lax.reduce_precision(share, 8, 7)
    middle = lax.reduce_precision(share - high, 8, 7)
    low = share - high - middle
    filled = jnp.sum(chosen.astype(jnp.float32), axis=1).reshape(peers, 1, 2)
    side = jnp.zeros((peers, 2 * block_len, max(tok_rows, 2)), jnp.float32)
    side = side.at[:, :3, :tok_rows].set(jnp.stack([high, middle, low], axis=1))
    side = side.at[:, 3:4, :2].set(filled)
    leaving = jnp.concatenate(
        [packed.reshape(peers, 2 * block_len, latent), side.astype(jnp.bfloat16)], axis=2
    )
    cube = peers == 2 << len(LINKS) and lax.axis_size("tp") == 1
    weights = (gate_weight[0], up_weight[0], down_weight[0])
    if cube:
        others = [swap_cores(weight) for weight in weights]
        gathered = gather_cube(tokens, others)
        leaving = hold_back(leaving, gathered[0][0])
    arrived = lax.all_to_all(leaving, "ep", split_axis=0, concat_axis=0, tiled=True)
    side_in = arrived[:, :, latent:].astype(jnp.float32)
    share_in = side_in[:, 0, :tok_rows] + side_in[:, 1, :tok_rows] + side_in[:, 2, :tok_rows]
    present = side_in[:, 3, :2].reshape(peers * 2)
    arrived = arrived[:, :, :latent]
    shard_len = latent_cache.shape[1]
    positions = lax.axis_index("tp") * shard_len + jnp.arange(shard_len, dtype=jnp.int32)
    keys = jnp.concatenate(
        [latent_cache[0], arrived.reshape(peers * 2 * block_len, latent)], axis=0
    )
    valid = jnp.concatenate([positions < cache_length[0], jnp.repeat(present > 0, block_len)])
    peak, total, mixed = attend_keys(query_latent[0], keys, valid, VAL)
    peak, total, mixed = combined_all((peak, total, mixed), "tp", join_parts)
    attn_out = (mixed / total[:, None]).astype(jnp.bfloat16)[None]

    if cube:
        moe_out = cube_experts(tok_rows, gathered, share_in, weights, others)
    else:
        moe_out = ring_experts(tokens, share_in, gate_weight, up_weight, down_weight)
    return (attn_out, moe_out)


def solution(mesh):
    in_specs = (
        P(("groups", "ep"), None, None),
        P(("groups", "ep"), "tp", None),
        P(("groups", "ep")),
        P(("groups", "ep"), "tp", None, None),
        P(("groups", "ep"), "tp", None),
        P(("groups", "ep"), None),
        P(("groups", "ep"), None),
        P(("groups", "ep"), None),
        P("ep", None, "tp"),
        P("ep", None, "tp"),
        P("ep", None, "tp"),
    )
    out_specs = (P(("groups", "ep"), None, None), P(("groups", "ep"), "tp"))
    return jax.shard_map(
        per_device, mesh=mesh, in_specs=in_specs, out_specs=out_specs, check_vma=False
    )
```

```python
import functools

import jax
import jax.numpy as jnp
from jax import lax
from jax.experimental import pallas as pl
from jax.experimental.pallas import tpu as pltpu
from jax.sharding import PartitionSpec as P

VAL = 512


SCALE = 192.0 ** (-0.5)
NEG = -1e30


def combined_all(x, axis, combine):
    if lax.axis_size(axis) == 1:
        return x
    everything = jax.tree.map(lambda part: lax.all_gather(part, axis), x)
    leading = jax.tree.map(lambda part: part[0], everything)

    def lap(k, so_far):
        return combine(so_far, jax.tree.map(lambda part: part[k], everything))

    return lax.fori_loop(1, lax.axis_size(axis), lap, leading)


def attend_keys(query, keys, valid, value_width):
    scores = (
        lax.dot_general(query, keys, (((1,), (1,)), ((), ())), preferred_element_type=jnp.float32)
        * SCALE
    )
    scores = jnp.where(valid[None, :], scores, NEG)
    peak = jnp.max(scores, axis=1)
    expo = jnp.where(valid[None, :], jnp.exp(scores - peak[:, None]), 0.0)
    total = jnp.sum(expo, axis=1)
    mixed = jnp.dot(
        expo.astype(jnp.bfloat16), keys[:, :value_width], preferred_element_type=jnp.float32
    )
    return (peak, total, mixed)


def join_parts(first, second):
    peak = jnp.maximum(first[0], second[0])
    left = jnp.exp(first[0] - peak)
    right = jnp.exp(second[0] - peak)
    return (
        peak,
        first[1] * left + second[1] * right,
        first[2] * left[:, None] + second[2] * right[:, None],
    )


def ring_experts(tokens, share, gate_weight, up_weight, down_weight):
    rows = lax.all_gather(tokens, "ep", axis=0, tiled=True)
    gate = jnp.dot(rows, gate_weight[0], preferred_element_type=jnp.float32)
    upper = jnp.dot(rows, up_weight[0], preferred_element_type=jnp.float32)
    hidden = (jax.nn.silu(gate) * upper).astype(jnp.bfloat16)
    if lax.axis_size("tp") > 1:
        hidden = lax.all_gather(hidden, "tp", axis=1, tiled=True)
    partial_out = jnp.dot(hidden, down_weight[0], preferred_element_type=jnp.float32)
    scaled = partial_out * share.reshape(-1)[:, None]
    return lax.psum_scatter(scaled, "ep", scatter_dimension=0, tiled=True).astype(jnp.bfloat16)


MIB = 1024 * 1024

LINKS = (1, 2, 4, 12)
SHARES = (10, 10, 8)
ORDERS = ((1, 0, 3, 2), (0, 2, 1, 3), (2, 1, 0, 3))


def across(value, link):
    peers = lax.axis_size("ep")
    return lax.ppermute(value, "ep", [(i, i ^ (2 * LINKS[link])) for i in range(peers)])


def swap_cores(value):
    return lax.ppermute(value, "ep", [(i, i ^ 1) for i in range(lax.axis_size("ep"))])


def slot_of(place, order):
    slot = 0
    for i, step in enumerate(order):
        slot |= ((place >> (len(order) - 1 - i)) & 1) << step
    return slot


def piece_columns(width):
    share = width // sum(SHARES)
    ends = [share * sum(SHARES[: at + 1]) for at in range(len(SHARES))]
    ends[-1] = width
    return list(zip([0] + ends[:-1], ends))


def whole_call(kernel, operands, out_shape, name, after=()):
    given = len(operands)

    def body(*refs):
        kernel(*refs[:given], *refs[given + len(after) :])

    return pl.pallas_call(
        body,
        in_specs=[pl.BlockSpec(memory_space=pltpu.VMEM)] * given
        + [pl.BlockSpec(memory_space=pl.ANY)] * len(after),
        out_specs=[pl.BlockSpec(memory_space=pltpu.VMEM)] * len(out_shape),
        out_shape=out_shape,
        compiler_params=pltpu.CompilerParams(vmem_limit_bytes=12 * MIB),
        cost_estimate=pl.CostEstimate(
            flops=0,
            bytes_accessed=sum(x.size * x.dtype.itemsize for x in list(operands) + list(out_shape)),
            transcendentals=0,
        ),
        name=name,
    )(*operands, *after)


def joined(held, got, after):
    count = len(held)
    out_shape = [jax.ShapeDtypeStruct((2 * x.shape[0], x.shape[1]), x.dtype) for x in held]

    def kernel(*refs):
        for first, second, out in zip(refs[:count], refs[count : 2 * count], refs[2 * count :]):
            rows = first.shape[0]
            out[:rows] = first[...]
            out[rows:] = second[...]

    return whole_call(kernel, [*held, *got], out_shape, "joined", after)


def hold_back(array, after):
    def kernel(in_ref, out_ref):
        out_ref[...] = in_ref[...]

    shape = jax.ShapeDtypeStruct(array.shape, array.dtype)
    return whole_call(kernel, [array], [shape], "hold_back", (after,))[0]


def gather_cube(tokens, others):
    steps = len(LINKS)
    held = [tokens[:, start:stop] for start, stop in piece_columns(tokens.shape[1])]
    for phase in range(steps):
        got = [across(piece, order[steps - 1 - phase]) for piece, order in zip(held, ORDERS)]
        if phase < steps - 1:
            held = joined(held, got, others if phase == 1 else ())
    return held, got


def hidden_kernel(unit, *refs):
    count = len(ORDERS)
    held, got = refs[:count], refs[count : 2 * count]
    gate_ref, up_ref, gate_other_ref, up_other_ref, hidden_ref, rows_ref = refs[2 * count :]
    step = pl.program_id(0)
    own_steps = pl.num_programs(0) // 2

    @pl.when(step == 0)
    def _():
        for piece, (start, stop) in enumerate(piece_columns(rows_ref.shape[1])):
            half = held[piece].shape[0]
            for place in range(2 * half // unit):
                source = held[piece] if place * unit < half else got[piece]
                at = place * unit % half
                slot = slot_of(place, ORDERS[piece])
                rows_ref[slot * unit : (slot + 1) * unit, start:stop] = source[at : at + unit]

    def units(gate_tile, up_tile):
        rows = rows_ref[...]
        gate = jnp.dot(rows, gate_tile[...], preferred_element_type=jnp.float32)
        upper = jnp.dot(rows, up_tile[...], preferred_element_type=jnp.float32)
        hidden_ref[...] = (gate / (1.0 + jnp.exp(-gate)) * upper).astype(jnp.bfloat16)

    @pl.when(step < own_steps)
    def _():
        units(gate_ref, up_ref)

    @pl.when(step >= own_steps)
    def _():
        units(gate_other_ref, up_other_ref)


def expert_hidden(unit, held, got, gate, up, gate_other, up_other):
    width, units = gate.shape
    count = 2 * held[0].shape[0]
    tile = 256
    steps = units // tile
    own = pl.BlockSpec((width, tile), lambda i: (0, jnp.minimum(i, steps - 1)))
    other = pl.BlockSpec((width, tile), lambda i: (0, jnp.maximum(i - steps, 0)))
    return pl.pallas_call(
        functools.partial(hidden_kernel, unit),
        grid=(2 * steps,),
        in_specs=[pl.BlockSpec(array.shape, lambda i: (0, 0)) for array in (*held, *got)]
        + [own, own, other, other],
        out_specs=pl.BlockSpec((count, tile), lambda i: (0, i)),
        out_shape=jax.ShapeDtypeStruct((count, 2 * units), jnp.bfloat16),
        scratch_shapes=[pltpu.VMEM((count, width), jnp.bfloat16)],
        compiler_params=pltpu.CompilerParams(vmem_limit_bytes=48 * MIB),
        cost_estimate=pl.CostEstimate(
            flops=8 * count * width * units,
            bytes_accessed=2 * (count * width + 4 * width * units + 2 * count * units),
            transcendentals=2 * count * units,
        ),
        name="expert_hidden",
    )(*held, *got, gate, up, gate_other, up_other)


def output_kernel(
    unit, order, scale_ref, hidden_ref, down_ref, down_other_ref, keep_ref, send_ref, rows_ref, factor_ref
):
    units = down_ref.shape[0]
    half = keep_ref.shape[0]

    @pl.when(pl.program_id(0) == 0)
    def _():
        for place in range(2 * half // unit):
            slot = slot_of(place, order)
            to, source = pl.ds(place * unit, unit), pl.ds(slot * unit, unit)
            rows_ref[to, :] = hidden_ref[source, :]
            factor_ref[to, :] = scale_ref[source, :]

    for out_ref, part in ((send_ref, pl.ds(half, half)), (keep_ref, pl.ds(0, half))):
        out = jnp.dot(rows_ref[part, :units], down_ref[...], preferred_element_type=jnp.float32)
        out += jnp.dot(
            rows_ref[part, units:], down_other_ref[...], preferred_element_type=jnp.float32
        )
        out_ref[...] = out * factor_ref[part, :]


def expert_output(unit, order, columns, scale, hidden, down, down_other):
    units = down.shape[0]
    start, stop = columns
    count = hidden.shape[0]
    tile = 256
    half = jax.ShapeDtypeStruct((count // 2, stop - start), jnp.float32)
    return pl.pallas_call(
        functools.partial(output_kernel, unit, order),
        grid=((stop - start) // tile,),
        in_specs=[
            pl.BlockSpec((count, 1), lambda i: (0, 0)),
            pl.BlockSpec((count, 2 * units), lambda i: (0, 0)),
            pl.BlockSpec((units, tile), lambda i: (0, start // tile + i)),
            pl.BlockSpec((units, tile), lambda i: (0, start // tile + i)),
        ],
        out_specs=[pl.BlockSpec((count // 2, tile), lambda i: (0, i))] * 2,
        out_shape=[half] * 2,
        scratch_shapes=[
            pltpu.VMEM((count, 2 * units), jnp.bfloat16),
            pltpu.VMEM((count, 1), jnp.float32),
        ],
        compiler_params=pltpu.CompilerParams(vmem_limit_bytes=40 * MIB),
        cost_estimate=pl.CostEstimate(
            flops=4 * count * (stop - start) * units,
            bytes_accessed=4 * (stop - start) * units + 4 * count * (stop - start + units),
            transcendentals=0,
        ),
        name="expert_output",
    )(scale, hidden, down, down_other)


def halved(keep, got):
    rows, width = keep.shape
    half = jax.ShapeDtypeStruct((rows // 2, width), keep.dtype)

    def kernel(keep_ref, got_ref, first_ref, second_ref):
        second_ref[...] = keep_ref[rows // 2 :] + got_ref[rows // 2 :]
        first_ref[...] = keep_ref[: rows // 2] + got_ref[: rows // 2]

    return whole_call(kernel, [keep, got], [half, half], "halved")


def finished(keep, got):
    count = len(keep)
    width = sum(piece.shape[1] for piece in keep)

    def kernel(*refs):
        for at, (start, stop) in enumerate(piece_columns(width)):
            total = refs[at][...] + refs[count + at][...]
            refs[2 * count][:, start:stop] = total.astype(jnp.bfloat16)

    shape = jax.ShapeDtypeStruct((keep[0].shape[0], width), jnp.bfloat16)
    return whole_call(kernel, [*keep, *got], [shape], "finished")[0]


def cube_experts(unit, gathered, share, weights, others):
    count = len(LINKS)
    peers = lax.axis_size("ep")
    gate, up, down = weights
    gate_other, up_other, down_other = others
    steps = []
    for slot in range(peers // 2):
        step = 0
        for link in range(count):
            step ^= LINKS[link] * ((slot >> link) & 1)
        steps.append(2 * step)
    source = jnp.bitwise_xor(lax.axis_index("ep"), jnp.array(steps, jnp.int32))
    picks = source[:, None] == jnp.arange(peers, dtype=jnp.int32)[None, :]
    scale = jnp.sum(jnp.where(picks[:, :, None], share[None, :, :], 0.0), axis=1)
    scale = scale.reshape(peers // 2 * unit, 1)

    hidden = expert_hidden(unit, *gathered, gate, up, gate_other, up_other)
    keep, got = [], []
    for order, columns in zip(ORDERS, piece_columns(down.shape[1])):
        mine, send = expert_output(unit, order, columns, scale, hidden, down, down_other)
        keep.append(mine)
        got.append(across(send, order[0]))
    for phase in range(1, count):
        for at, order in enumerate(ORDERS):
            keep[at], send = halved(keep[at], got[at])
            got[at] = across(send, order[phase])
    return finished(keep, got)


def per_device(
    query_latent,
    latent_cache,
    cache_length,
    prefill_latent,
    block_owner,
    tokens,
    expert_ids,
    route_weight,
    gate_weight,
    up_weight,
    down_weight,
):
    peers = lax.axis_size("ep")
    blocks = prefill_latent.shape[1]
    block_len = prefill_latent.shape[2]
    latent = prefill_latent.shape[3]
    tok_rows, top_k = expert_ids.shape

    owner = block_owner.reshape(blocks)
    same = owner[:, None] == owner[None, :]
    earlier = jnp.arange(blocks)[None, :] < jnp.arange(blocks)[:, None]
    order_in = jnp.sum(jnp.logical_and(same, earlier).astype(jnp.int32), axis=1)
    target = owner * 2 + order_in
    chosen = jnp.arange(2 * peers, dtype=jnp.int32)[:, None] == target[None, :]
    packed = jnp.dot(
        chosen.astype(jnp.bfloat16),
        prefill_latent.reshape(blocks, block_len * latent),
        preferred_element_type=jnp.float32,
    ).astype(jnp.bfloat16)

    expert_of = jnp.arange(peers, dtype=jnp.int32) // 2
    named = expert_ids[None, :, :] == expert_of[:, None, None]
    share = jnp.sum(jnp.where(named, route_weight[None, :, :], 0.0), axis=2)
    high = lax.reduce_precision(share, 8, 7)
    middle = lax.reduce_precision(share - high, 8, 7)
    low = share - high - middle
    filled = jnp.sum(chosen.astype(jnp.float32), axis=1).reshape(peers, 1, 2)
    side = jnp.zeros((peers, 2 * block_len, max(tok_rows, 2)), jnp.float32)
    side = side.at[:, :3, :tok_rows].set(jnp.stack([high, middle, low], axis=1))
    side = side.at[:, 3:4, :2].set(filled)
    leaving = jnp.concatenate(
        [packed.reshape(peers, 2 * block_len, latent), side.astype(jnp.bfloat16)], axis=2
    )
    cube = peers == 2 << len(LINKS) and lax.axis_size("tp") == 1
    weights = (gate_weight[0], up_weight[0], down_weight[0])
    if cube:
        others = [swap_cores(weight) for weight in weights]
        gathered = gather_cube(tokens, others)
        leaving = hold_back(leaving, gathered[0][0])
    arrived = lax.all_to_all(leaving, "ep", split_axis=0, concat_axis=0, tiled=True)
    side_in = arrived[:, :, latent:].astype(jnp.float32)
    share_in = side_in[:, 0, :tok_rows] + side_in[:, 1, :tok_rows] + side_in[:, 2, :tok_rows]
    present = side_in[:, 3, :2].reshape(peers * 2)
    arrived = arrived[:, :, :latent]
    shard_len = latent_cache.shape[1]
    positions = lax.axis_index("tp") * shard_len + jnp.arange(shard_len, dtype=jnp.int32)
    keys = jnp.concatenate(
        [latent_cache[0], arrived.reshape(peers * 2 * block_len, latent)], axis=0
    )
    valid = jnp.concatenate([positions < cache_length[0], jnp.repeat(present > 0, block_len)])
    peak, total, mixed = attend_keys(query_latent[0], keys, valid, VAL)
    peak, total, mixed = combined_all((peak, total, mixed), "tp", join_parts)
    attn_out = (mixed / total[:, None]).astype(jnp.bfloat16)[None]

    if cube:
        moe_out = cube_experts(tok_rows, gathered, share_in, weights, others)
    else:
        moe_out = ring_experts(tokens, share_in, gate_weight, up_weight, down_weight)
    return (attn_out, moe_out)


def solution(mesh):
    in_specs = (
        P(("groups", "ep"), None, None),
        P(("groups", "ep"), "tp", None),
        P(("groups", "ep")),
        P(("groups", "ep"), "tp", None, None),
        P(("groups", "ep"), "tp", None),
        P(("groups", "ep"), None),
        P(("groups", "ep"), None),
        P(("groups", "ep"), None),
        P("ep", None, "tp"),
        P("ep", None, "tp"),
        P("ep", None, "tp"),
    )
    out_specs = (P(("groups", "ep"), None, None), P(("groups", "ep"), "tp"))
    return jax.shard_map(
        per_device, mesh=mesh, in_specs=in_specs, out_specs=out_specs, check_vma=False
    )
```

```python
import functools

import jax
import jax.numpy as jnp
from jax import lax
from jax.experimental import pallas as pl
from jax.experimental.pallas import tpu as pltpu
from jax.sharding import PartitionSpec as P

VAL = 512


SCALE = 192.0 ** (-0.5)
NEG = -1e30


def combined_all(x, axis, combine):
    if lax.axis_size(axis) == 1:
        return x
    everything = jax.tree.map(lambda part: lax.all_gather(part, axis), x)
    leading = jax.tree.map(lambda part: part[0], everything)

    def lap(k, so_far):
        return combine(so_far, jax.tree.map(lambda part: part[k], everything))

    return lax.fori_loop(1, lax.axis_size(axis), lap, leading)


def attend_keys(query, keys, valid, value_width):
    scores = (
        lax.dot_general(query, keys, (((1,), (1,)), ((), ())), preferred_element_type=jnp.float32)
        * SCALE
    )
    scores = jnp.where(valid[None, :], scores, NEG)
    peak = jnp.max(scores, axis=1)
    expo = jnp.where(valid[None, :], jnp.exp(scores - peak[:, None]), 0.0)
    total = jnp.sum(expo, axis=1)
    mixed = jnp.dot(
        expo.astype(jnp.bfloat16), keys[:, :value_width], preferred_element_type=jnp.float32
    )
    return (peak, total, mixed)


def join_parts(first, second):
    peak = jnp.maximum(first[0], second[0])
    left = jnp.exp(first[0] - peak)
    right = jnp.exp(second[0] - peak)
    return (
        peak,
        first[1] * left + second[1] * right,
        first[2] * left[:, None] + second[2] * right[:, None],
    )


def ring_experts(tokens, share, gate_weight, up_weight, down_weight):
    rows = lax.all_gather(tokens, "ep", axis=0, tiled=True)
    gate = jnp.dot(rows, gate_weight[0], preferred_element_type=jnp.float32)
    upper = jnp.dot(rows, up_weight[0], preferred_element_type=jnp.float32)
    hidden = (jax.nn.silu(gate) * upper).astype(jnp.bfloat16)
    if lax.axis_size("tp") > 1:
        hidden = lax.all_gather(hidden, "tp", axis=1, tiled=True)
    partial_out = jnp.dot(hidden, down_weight[0], preferred_element_type=jnp.float32)
    scaled = partial_out * share.reshape(-1)[:, None]
    return lax.psum_scatter(scaled, "ep", scatter_dimension=0, tiled=True).astype(jnp.bfloat16)


MIB = 1024 * 1024

LINKS = (1, 2, 4, 12)
SHARES = (10, 10, 8)
ORDERS = ((1, 0, 3, 2), (0, 2, 1, 3), (2, 1, 0, 3))


def across(value, link):
    peers = lax.axis_size("ep")
    return lax.ppermute(value, "ep", [(i, i ^ (2 * LINKS[link])) for i in range(peers)])


def swap_cores(value):
    return lax.ppermute(value, "ep", [(i, i ^ 1) for i in range(lax.axis_size("ep"))])


def slot_of(place, order):
    slot = 0
    for i, step in enumerate(order):
        slot |= ((place >> (len(order) - 1 - i)) & 1) << step
    return slot


def piece_columns(width):
    share = width // sum(SHARES)
    ends = [share * sum(SHARES[: at + 1]) for at in range(len(SHARES))]
    ends[-1] = width
    return list(zip([0] + ends[:-1], ends))


def whole_call(kernel, operands, out_shape, name, after=()):
    given = len(operands)

    def body(*refs):
        kernel(*refs[:given], *refs[given + len(after) :])

    return pl.pallas_call(
        body,
        in_specs=[pl.BlockSpec(memory_space=pltpu.VMEM)] * given
        + [pl.BlockSpec(memory_space=pl.ANY)] * len(after),
        out_specs=[pl.BlockSpec(memory_space=pltpu.VMEM)] * len(out_shape),
        out_shape=out_shape,
        compiler_params=pltpu.CompilerParams(vmem_limit_bytes=12 * MIB),
        cost_estimate=pl.CostEstimate(
            flops=0,
            bytes_accessed=sum(x.size * x.dtype.itemsize for x in list(operands) + list(out_shape)),
            transcendentals=0,
        ),
        name=name,
    )(*operands, *after)


def joined(held, got, after):
    count = len(held)
    out_shape = [jax.ShapeDtypeStruct((2 * x.shape[0], x.shape[1]), x.dtype) for x in held]

    def kernel(*refs):
        for first, second, out in zip(refs[:count], refs[count : 2 * count], refs[2 * count :]):
            rows = first.shape[0]
            out[:rows] = first[...]
            out[rows:] = second[...]

    return whole_call(kernel, [*held, *got], out_shape, "joined", after)


def hold_back(array, after):
    def kernel(in_ref, out_ref):
        out_ref[...] = in_ref[...]

    shape = jax.ShapeDtypeStruct(array.shape, array.dtype)
    return whole_call(kernel, [array], [shape], "hold_back", (after,))[0]


def gather_cube(tokens, side, gate, up, down):
    steps = len(LINKS)
    others = [swap_cores(gate), swap_cores(up)]
    held = [tokens[:, start:stop] for start, stop in piece_columns(tokens.shape[1])]
    held[-1] = jnp.concatenate([held[-1], side], axis=1)
    for phase in range(steps):
        got = [across(piece, order[steps - 1 - phase]) for piece, order in zip(held, ORDERS)]
        if phase < steps - 1:
            held = joined(held, got, others if phase == 1 else ())
        if phase == 1:
            others.append(swap_cores(hold_back(down, held[0])))
    return held, got, others


def hidden_kernel(unit, chip_ref, *refs):
    count = len(ORDERS)
    held, got = refs[:count], refs[count : 2 * count]
    gate_ref, up_ref, gate_other_ref, up_other_ref = refs[2 * count : 2 * count + 4]
    hidden_ref, scale_ref, rows_ref, side_ref = refs[2 * count + 4 :]
    step = pl.program_id(0)
    own_steps = pl.num_programs(0) // 2

    @pl.when(step == 0)
    def _():
        for piece, (start, stop) in enumerate(piece_columns(rows_ref.shape[1])):
            half = held[piece].shape[0]
            for place in range(2 * half // unit):
                source = held[piece] if place * unit < half else got[piece]
                at = place * unit % half
                slot = slot_of(place, ORDERS[piece])
                to = slice(slot * unit, (slot + 1) * unit)
                rows_ref[to, start:stop] = source[at : at + unit, : stop - start]
                if piece == count - 1:
                    side_ref[to, :] = source[at : at + unit, stop - start :]
        column = lax.broadcasted_iota(jnp.int32, side_ref.shape, 1)
        experts = 1 << len(LINKS)
        mine = jnp.logical_and(column % experts == chip_ref[0], column < 3 * experts)
        parts = jnp.where(mine, side_ref[...].astype(jnp.float32), 0.0)
        scale_ref[...] = jnp.sum(parts, axis=1, keepdims=True)

    def units(gate_tile, up_tile):
        rows = rows_ref[...]
        gate = jnp.dot(rows, gate_tile[...], preferred_element_type=jnp.float32)
        upper = jnp.dot(rows, up_tile[...], preferred_element_type=jnp.float32)
        hidden_ref[...] = (gate / (1.0 + jnp.exp(-gate)) * upper).astype(jnp.bfloat16)

    @pl.when(step < own_steps)
    def _():
        units(gate_ref, up_ref)

    @pl.when(step >= own_steps)
    def _():
        units(gate_other_ref, up_other_ref)


def expert_hidden(unit, chip, held, got, gate, up, gate_other, up_other):
    width, units = gate.shape
    count = 2 * held[0].shape[0]
    tile = 256
    steps = units // tile
    own = pl.BlockSpec((width, tile), lambda i: (0, jnp.minimum(i, steps - 1)))
    other = pl.BlockSpec((width, tile), lambda i: (0, jnp.maximum(i - steps, 0)))
    return pl.pallas_call(
        functools.partial(hidden_kernel, unit),
        grid=(2 * steps,),
        in_specs=[pl.BlockSpec(memory_space=pltpu.SMEM)]
        + [pl.BlockSpec(array.shape, lambda i: (0, 0)) for array in (*held, *got)]
        + [own, own, other, other],
        out_specs=[
            pl.BlockSpec((count, tile), lambda i: (0, i)),
            pl.BlockSpec((count, 1), lambda i: (0, 0)),
        ],
        out_shape=[
            jax.ShapeDtypeStruct((count, 2 * units), jnp.bfloat16),
            jax.ShapeDtypeStruct((count, 1), jnp.float32),
        ],
        scratch_shapes=[
            pltpu.VMEM((count, width), jnp.bfloat16),
            pltpu.VMEM((count, sum(piece.shape[1] for piece in held) - width), jnp.bfloat16),
        ],
        compiler_params=pltpu.CompilerParams(vmem_limit_bytes=38 * MIB),
        cost_estimate=pl.CostEstimate(
            flops=8 * count * width * units,
            bytes_accessed=2 * (count * width + 4 * width * units + 2 * count * units),
            transcendentals=2 * count * units,
        ),
        name="expert_hidden",
    )(chip, *held, *got, gate, up, gate_other, up_other)


def output_kernel(
    unit, order, scale_ref, hidden_ref, down_ref, down_other_ref, keep_ref, send_ref, rows_ref, factor_ref
):
    units = down_ref.shape[0]
    half = keep_ref.shape[0]

    @pl.when(pl.program_id(0) == 0)
    def _():
        for place in range(2 * half // unit):
            slot = slot_of(place, order)
            to, source = pl.ds(place * unit, unit), pl.ds(slot * unit, unit)
            rows_ref[to, :] = hidden_ref[source, :]
            factor_ref[to, :] = scale_ref[source, :]

    out = jnp.dot(rows_ref[:, :units], down_ref[...], preferred_element_type=jnp.float32)
    out += jnp.dot(rows_ref[:, units:], down_other_ref[...], preferred_element_type=jnp.float32)
    out = out * factor_ref[...]
    keep_ref[...] = out[:half]
    send_ref[...] = out[half:]


def expert_output(unit, order, columns, scale, hidden, down, down_other):
    units = down.shape[0]
    start, stop = columns
    count = hidden.shape[0]
    tile = 256
    half = jax.ShapeDtypeStruct((count // 2, stop - start), jnp.float32)
    return pl.pallas_call(
        functools.partial(output_kernel, unit, order),
        grid=((stop - start) // tile,),
        in_specs=[
            pl.BlockSpec((count, 1), lambda i: (0, 0)),
            pl.BlockSpec((count, 2 * units), lambda i: (0, 0)),
            pl.BlockSpec((units, tile), lambda i: (0, start // tile + i)),
            pl.BlockSpec((units, tile), lambda i: (0, start // tile + i)),
        ],
        out_specs=[pl.BlockSpec((count // 2, tile), lambda i: (0, i))] * 2,
        out_shape=[half] * 2,
        scratch_shapes=[
            pltpu.VMEM((count, 2 * units), jnp.bfloat16),
            pltpu.VMEM((count, 1), jnp.float32),
        ],
        compiler_params=pltpu.CompilerParams(vmem_limit_bytes=40 * MIB),
        cost_estimate=pl.CostEstimate(
            flops=4 * count * (stop - start) * units,
            bytes_accessed=4 * (stop - start) * units + 4 * count * (stop - start + units),
            transcendentals=0,
        ),
        name="expert_output",
    )(scale, hidden, down, down_other)


def halved(keep, got):
    rows, width = keep.shape
    half = jax.ShapeDtypeStruct((rows // 2, width), keep.dtype)

    def kernel(keep_ref, got_ref, first_ref, second_ref):
        second_ref[...] = keep_ref[rows // 2 :] + got_ref[rows // 2 :]
        first_ref[...] = keep_ref[: rows // 2] + got_ref[: rows // 2]

    return whole_call(kernel, [keep, got], [half, half], "halved")


def finished(keep, got):
    count = len(keep)
    width = sum(piece.shape[1] for piece in keep)

    def kernel(*refs):
        for at, (start, stop) in enumerate(piece_columns(width)):
            total = refs[at][...] + refs[count + at][...]
            refs[2 * count][:, start:stop] = total.astype(jnp.bfloat16)

    shape = jax.ShapeDtypeStruct((keep[0].shape[0], width), jnp.bfloat16)
    return whole_call(kernel, [*keep, *got], [shape], "finished")[0]


def cube_outputs(unit, held, got, weights, others):
    gate, up, down = weights
    gate_other, up_other, down_other = others
    chip = (lax.axis_index("ep") // 2).astype(jnp.int32).reshape(1)
    hidden, scale = expert_hidden(unit, chip, held, got, gate, up, gate_other, up_other)
    keep, coming = [], []
    for order, columns in zip(ORDERS, piece_columns(down.shape[1])):
        mine, send = expert_output(unit, order, columns, scale, hidden, down, down_other)
        keep.append(mine)
        coming.append(across(send, order[0]))
    return keep, coming


def cube_sums(keep, got):
    keep, got = list(keep), list(got)
    for phase in range(1, len(LINKS)):
        for at, order in enumerate(ORDERS):
            keep[at], send = halved(keep[at], got[at])
            got[at] = across(send, order[phase])
    return finished(keep, got)


def three_parts(value):
    high = lax.reduce_precision(value, 8, 7)
    middle = lax.reduce_precision(value - high, 8, 7)
    return high, middle, value - high - middle


def per_device(
    query_latent,
    latent_cache,
    cache_length,
    prefill_latent,
    block_owner,
    tokens,
    expert_ids,
    route_weight,
    gate_weight,
    up_weight,
    down_weight,
):
    peers = lax.axis_size("ep")
    blocks = prefill_latent.shape[1]
    block_len = prefill_latent.shape[2]
    latent = prefill_latent.shape[3]
    tok_rows, top_k = expert_ids.shape

    owner = block_owner.reshape(blocks)
    same = owner[:, None] == owner[None, :]
    earlier = jnp.arange(blocks)[None, :] < jnp.arange(blocks)[:, None]
    order_in = jnp.sum(jnp.logical_and(same, earlier).astype(jnp.int32), axis=1)
    target = owner * 2 + order_in
    chosen = jnp.arange(2 * peers, dtype=jnp.int32)[:, None] == target[None, :]
    packed = jnp.dot(
        chosen.astype(jnp.bfloat16),
        prefill_latent.reshape(blocks, block_len * latent),
        preferred_element_type=jnp.float32,
    ).astype(jnp.bfloat16)

    cube = peers == 2 << len(LINKS) and lax.axis_size("tp") == 1
    weights = (gate_weight[0], up_weight[0], down_weight[0])
    filled = jnp.sum(chosen.astype(jnp.float32), axis=1).reshape(peers, 1, 2)
    side = jnp.zeros((peers, 2 * block_len, max(tok_rows, 2)), jnp.float32)
    side = side.at[:, 3:4, :2].set(filled)
    if not cube:
        expert_of = jnp.arange(peers, dtype=jnp.int32) // 2
        named = expert_ids[None, :, :] == expert_of[:, None, None]
        share = jnp.sum(jnp.where(named, route_weight[None, :, :], 0.0), axis=2)
        side = side.at[:, :3, :tok_rows].set(jnp.stack(three_parts(share), axis=1))
    leaving = jnp.concatenate(
        [packed.reshape(peers, 2 * block_len, latent), side.astype(jnp.bfloat16)], axis=2
    )
    if cube:
        experts = jnp.arange(peers // 2, dtype=jnp.int32)
        named = expert_ids[:, :, None] == experts[None, None, :]
        share = jnp.sum(jnp.where(named, route_weight[:, :, None], 0.0), axis=1)
        parts = jnp.concatenate(three_parts(share), axis=1).astype(jnp.bfloat16)
        parts = jnp.pad(parts, ((0, 0), (0, 128 - parts.shape[1])))
        *gathered, others = gather_cube(tokens, parts, *weights)
        keep, coming = cube_outputs(tok_rows, *gathered, weights, others)
        leaving = hold_back(leaving, keep[-1])
    arrived = lax.all_to_all(leaving, "ep", split_axis=0, concat_axis=0, tiled=True)
    side_in = arrived[:, :, latent:].astype(jnp.float32)
    present = side_in[:, 3, :2].reshape(peers * 2)
    arrived = arrived[:, :, :latent]
    shard_len = latent_cache.shape[1]
    positions = lax.axis_index("tp") * shard_len + jnp.arange(shard_len, dtype=jnp.int32)
    keys = jnp.concatenate(
        [latent_cache[0], arrived.reshape(peers * 2 * block_len, latent)], axis=0
    )
    valid = jnp.concatenate([positions < cache_length[0], jnp.repeat(present > 0, block_len)])
    peak, total, mixed = attend_keys(query_latent[0], keys, valid, VAL)
    peak, total, mixed = combined_all((peak, total, mixed), "tp", join_parts)
    attn_out = (mixed / total[:, None]).astype(jnp.bfloat16)[None]

    if cube:
        moe_out = cube_sums(keep, coming)
    else:
        share_in = jnp.sum(side_in[:, :3, :tok_rows], axis=1)
        moe_out = ring_experts(tokens, share_in, gate_weight, up_weight, down_weight)
    return (attn_out, moe_out)


def solution(mesh):
    in_specs = (
        P(("groups", "ep"), None, None),
        P(("groups", "ep"), "tp", None),
        P(("groups", "ep")),
        P(("groups", "ep"), "tp", None, None),
        P(("groups", "ep"), "tp", None),
        P(("groups", "ep"), None),
        P(("groups", "ep"), None),
        P(("groups", "ep"), None),
        P("ep", None, "tp"),
        P("ep", None, "tp"),
        P("ep", None, "tp"),
    )
    out_specs = (P(("groups", "ep"), None, None), P(("groups", "ep"), "tp"))
    return jax.shard_map(
        per_device, mesh=mesh, in_specs=in_specs, out_specs=out_specs, check_vma=False
    )
```

```python
import functools

import jax
import jax.numpy as jnp
from jax import lax
from jax.experimental import pallas as pl
from jax.experimental.pallas import tpu as pltpu
from jax.sharding import PartitionSpec as P

VAL = 512


SCALE = 192.0 ** (-0.5)
NEG = -1e30


def combined_all(x, axis, combine):
    if lax.axis_size(axis) == 1:
        return x
    everything = jax.tree.map(lambda part: lax.all_gather(part, axis), x)
    leading = jax.tree.map(lambda part: part[0], everything)

    def lap(k, so_far):
        return combine(so_far, jax.tree.map(lambda part: part[k], everything))

    return lax.fori_loop(1, lax.axis_size(axis), lap, leading)


def attend_keys(query, keys, valid, value_width):
    scores = (
        lax.dot_general(query, keys, (((1,), (1,)), ((), ())), preferred_element_type=jnp.float32)
        * SCALE
    )
    scores = jnp.where(valid[None, :], scores, NEG)
    peak = jnp.max(scores, axis=1)
    expo = jnp.where(valid[None, :], jnp.exp(scores - peak[:, None]), 0.0)
    total = jnp.sum(expo, axis=1)
    mixed = jnp.dot(
        expo.astype(jnp.bfloat16), keys[:, :value_width], preferred_element_type=jnp.float32
    )
    return (peak, total, mixed)


def join_parts(first, second):
    peak = jnp.maximum(first[0], second[0])
    left = jnp.exp(first[0] - peak)
    right = jnp.exp(second[0] - peak)
    return (
        peak,
        first[1] * left + second[1] * right,
        first[2] * left[:, None] + second[2] * right[:, None],
    )


def ring_experts(tokens, share, gate_weight, up_weight, down_weight):
    rows = lax.all_gather(tokens, "ep", axis=0, tiled=True)
    gate = jnp.dot(rows, gate_weight[0], preferred_element_type=jnp.float32)
    upper = jnp.dot(rows, up_weight[0], preferred_element_type=jnp.float32)
    hidden = (jax.nn.silu(gate) * upper).astype(jnp.bfloat16)
    if lax.axis_size("tp") > 1:
        hidden = lax.all_gather(hidden, "tp", axis=1, tiled=True)
    partial_out = jnp.dot(hidden, down_weight[0], preferred_element_type=jnp.float32)
    scaled = partial_out * share.reshape(-1)[:, None]
    return lax.psum_scatter(scaled, "ep", scatter_dimension=0, tiled=True).astype(jnp.bfloat16)


MIB = 1024 * 1024

LINKS = (1, 2, 4, 12)
OUT = ((5, (1, 0, 3, 2)), (5, (0, 2, 1, 3)), (4, (2, 1, 0, 3)))
BACK = ((5, (1, 0, 2, 3)), (5, (0, 1, 3, 2)), (2, (3, 2, 1, 0)), (2, (2, 3, 0, 1)))


def across(value, link):
    peers = lax.axis_size("ep")
    return lax.ppermute(value, "ep", [(i, i ^ (2 * LINKS[link])) for i in range(peers)])


def swap_cores(value):
    return lax.ppermute(value, "ep", [(i, i ^ 1) for i in range(lax.axis_size("ep"))])


def slot_of(place, order):
    slot = 0
    for i, step in enumerate(order):
        slot |= ((place >> (len(order) - 1 - i)) & 1) << step
    return slot


def orders_of(pieces):
    return [order for _, order in pieces]


def piece_columns(width, pieces):
    shares = [share for share, _ in pieces]
    one = width // sum(shares)
    ends = [one * sum(shares[: at + 1]) for at in range(len(shares))]
    ends[-1] = width
    return list(zip([0] + ends[:-1], ends))


def whole_call(kernel, operands, out_shape, name, after=()):
    given = len(operands)

    def body(*refs):
        kernel(*refs[:given], *refs[given + len(after) :])

    return pl.pallas_call(
        body,
        in_specs=[pl.BlockSpec(memory_space=pltpu.VMEM)] * given
        + [pl.BlockSpec(memory_space=pl.ANY)] * len(after),
        out_specs=[pl.BlockSpec(memory_space=pltpu.VMEM)] * len(out_shape),
        out_shape=out_shape,
        compiler_params=pltpu.CompilerParams(vmem_limit_bytes=12 * MIB),
        cost_estimate=pl.CostEstimate(
            flops=0,
            bytes_accessed=sum(x.size * x.dtype.itemsize for x in list(operands) + list(out_shape)),
            transcendentals=0,
        ),
        name=name,
    )(*operands, *after)


def joined(held, got, after):
    count = len(held)
    out_shape = [jax.ShapeDtypeStruct((2 * x.shape[0], x.shape[1]), x.dtype) for x in held]

    def kernel(*refs):
        for first, second, out in zip(refs[:count], refs[count : 2 * count], refs[2 * count :]):
            rows = first.shape[0]
            out[:rows] = first[...]
            out[rows:] = second[...]

    return whole_call(kernel, [*held, *got], out_shape, "joined", after)


def hold_back(array, after):
    def kernel(in_ref, out_ref):
        out_ref[...] = in_ref[...]

    shape = jax.ShapeDtypeStruct(array.shape, array.dtype)
    return whole_call(kernel, [array], [shape], "hold_back", (after,))[0]


def hold_back_tiles(array, after):
    tile = array.shape[1] // 4

    def kernel(in_ref, after_ref, out_ref):
        out_ref[...] = in_ref[...]

    spec = pl.BlockSpec((array.shape[0], tile), lambda i: (0, i))
    return pl.pallas_call(
        kernel,
        grid=(4,),
        in_specs=[spec, pl.BlockSpec(memory_space=pl.ANY)],
        out_specs=spec,
        out_shape=jax.ShapeDtypeStruct(array.shape, array.dtype),
        compiler_params=pltpu.CompilerParams(vmem_limit_bytes=32 * MIB),
        cost_estimate=pl.CostEstimate(flops=0, bytes_accessed=4 * array.size, transcendentals=0),
        name="hold_back_tiles",
    )(array, after)


def gather_cube(tokens, side, gate, up, down):
    steps = len(LINKS)
    others = [swap_cores(gate), swap_cores(up)]
    held = [tokens[:, start:stop] for start, stop in piece_columns(tokens.shape[1], OUT)]
    held[-1] = jnp.concatenate([held[-1], side], axis=1)
    for phase in range(steps):
        got = [across(piece, order[steps - 1 - phase]) for piece, order in zip(held, orders_of(OUT))]
        if phase < steps - 1:
            held = joined(held, got, others if phase == 1 else ())
        if phase == 1:
            others.append(swap_cores(hold_back_tiles(down, held[0])))
    return held, got, others


def hidden_kernel(unit, chip_ref, *refs):
    count = len(OUT)
    held, got = refs[:count], refs[count : 2 * count]
    gate_ref, up_ref, gate_other_ref, up_other_ref = refs[2 * count : 2 * count + 4]
    hidden_ref, scale_ref, rows_ref, side_ref = refs[2 * count + 4 :]
    step = pl.program_id(0)
    own_steps = pl.num_programs(0) // 2

    @pl.when(step == 0)
    def _():
        for piece, (start, stop) in enumerate(piece_columns(rows_ref.shape[1], OUT)):
            half = held[piece].shape[0]
            for place in range(2 * half // unit):
                source = held[piece] if place * unit < half else got[piece]
                at = place * unit % half
                slot = slot_of(place, OUT[piece][1])
                to = slice(slot * unit, (slot + 1) * unit)
                rows_ref[to, start:stop] = source[at : at + unit, : stop - start]
                if piece == count - 1:
                    side_ref[to, :] = source[at : at + unit, stop - start :]
        column = lax.broadcasted_iota(jnp.int32, side_ref.shape, 1)
        experts = 1 << len(LINKS)
        mine = jnp.logical_and(column % experts == chip_ref[0], column < 3 * experts)
        parts = jnp.where(mine, side_ref[...].astype(jnp.float32), 0.0)
        scale_ref[...] = jnp.sum(parts, axis=1, keepdims=True)

    def units(gate_tile, up_tile):
        rows = rows_ref[...]
        gate = jnp.dot(rows, gate_tile[...], preferred_element_type=jnp.float32)
        upper = jnp.dot(rows, up_tile[...], preferred_element_type=jnp.float32)
        hidden_ref[...] = (gate / (1.0 + jnp.exp(-gate)) * upper).astype(jnp.bfloat16)

    @pl.when(step < own_steps)
    def _():
        units(gate_ref, up_ref)

    @pl.when(step >= own_steps)
    def _():
        units(gate_other_ref, up_other_ref)


def expert_hidden(unit, chip, held, got, gate, up, gate_other, up_other):
    width, units = gate.shape
    count = 2 * held[0].shape[0]
    tile = 256
    steps = units // tile
    own = pl.BlockSpec((width, tile), lambda i: (0, jnp.minimum(i, steps - 1)))
    other = pl.BlockSpec((width, tile), lambda i: (0, jnp.maximum(i - steps, 0)))
    return pl.pallas_call(
        functools.partial(hidden_kernel, unit),
        grid=(2 * steps,),
        in_specs=[pl.BlockSpec(memory_space=pltpu.SMEM)]
        + [pl.BlockSpec(array.shape, lambda i: (0, 0)) for array in (*held, *got)]
        + [own, own, other, other],
        out_specs=[
            pl.BlockSpec((count, tile), lambda i: (0, i)),
            pl.BlockSpec((count, 1), lambda i: (0, 0)),
        ],
        out_shape=[
            jax.ShapeDtypeStruct((count, 2 * units), jnp.bfloat16),
            jax.ShapeDtypeStruct((count, 1), jnp.float32),
        ],
        scratch_shapes=[
            pltpu.VMEM((count, width), jnp.bfloat16),
            pltpu.VMEM((count, sum(piece.shape[1] for piece in held) - width), jnp.bfloat16),
        ],
        compiler_params=pltpu.CompilerParams(vmem_limit_bytes=48 * MIB),
        cost_estimate=pl.CostEstimate(
            flops=8 * count * width * units,
            bytes_accessed=2 * (count * width + 4 * width * units + 2 * count * units),
            transcendentals=2 * count * units,
        ),
        name="expert_hidden",
    )(chip, *held, *got, gate, up, gate_other, up_other)


def output_kernel(unit, order, tiles, scale_ref, hidden_ref, *refs):
    down, down_other = refs[:tiles], refs[tiles : 2 * tiles]
    keep_ref, send_ref = refs[2 * tiles :]
    units, tile = down[0].shape
    places = hidden_ref.shape[0] // unit
    for out_ref, first in ((send_ref, places // 2), (keep_ref, 0)):
        slots = [slot_of(first + at, order) for at in range(places // 2)]
        rows = [slice(slot * unit, (slot + 1) * unit) for slot in slots]
        hidden = jnp.concatenate([hidden_ref[row] for row in rows], axis=0)
        scale = jnp.concatenate([scale_ref[row] for row in rows], axis=0)
        for at in range(tiles):
            out = jnp.dot(hidden[:, :units], down[at][...], preferred_element_type=jnp.float32)
            out += jnp.dot(hidden[:, units:], down_other[at][...], preferred_element_type=jnp.float32)
            out_ref[:, at * tile : (at + 1) * tile] = out * scale


def expert_output(unit, order, columns, scale, hidden, down, down_other):
    units = down.shape[0]
    start, stop = columns
    count = hidden.shape[0]
    tile = 256
    tiles = (stop - start) // tile
    half = jax.ShapeDtypeStruct((count // 2, stop - start), jnp.float32)

    def tile_at(at):
        return pl.BlockSpec((units, tile), lambda i: (0, start // tile + at))

    return pl.pallas_call(
        functools.partial(output_kernel, unit, order, tiles),
        grid=(1,),
        in_specs=[
            pl.BlockSpec((count, 1), lambda i: (0, 0)),
            pl.BlockSpec((count, 2 * units), lambda i: (0, 0)),
        ]
        + [tile_at(at) for at in range(tiles)] * 2,
        out_specs=[pl.BlockSpec((count // 2, stop - start), lambda i: (0, 0))] * 2,
        out_shape=[half] * 2,
        compiler_params=pltpu.CompilerParams(vmem_limit_bytes=24 * MIB),
        cost_estimate=pl.CostEstimate(
            flops=4 * count * (stop - start) * units,
            bytes_accessed=4 * (stop - start) * units + 4 * count * (stop - start + units),
            transcendentals=0,
        ),
        name="expert_output",
    )(scale, hidden, *[down] * tiles, *[down_other] * tiles)


def halved(keep, got):
    rows, width = keep.shape
    half = jax.ShapeDtypeStruct((rows // 2, width), keep.dtype)

    def kernel(keep_ref, got_ref, first_ref, second_ref):
        second_ref[...] = keep_ref[rows // 2 :] + got_ref[rows // 2 :]
        first_ref[...] = keep_ref[: rows // 2] + got_ref[: rows // 2]

    return whole_call(kernel, [keep, got], [half, half], "halved")


def finished(keep, got):
    count = len(keep)
    width = sum(piece.shape[1] for piece in keep)

    def kernel(*refs):
        for at, (start, stop) in enumerate(piece_columns(width, BACK)):
            total = refs[at][...] + refs[count + at][...]
            refs[2 * count][:, start:stop] = total.astype(jnp.bfloat16)

    shape = jax.ShapeDtypeStruct((keep[0].shape[0], width), jnp.bfloat16)
    return whole_call(kernel, [*keep, *got], [shape], "finished")[0]


def cube_outputs(unit, held, got, weights, others):
    gate, up, down = weights
    gate_other, up_other, down_other = others
    chip = (lax.axis_index("ep") // 2).astype(jnp.int32).reshape(1)
    hidden, scale = expert_hidden(unit, chip, held, got, gate, up, gate_other, up_other)
    keep, coming = [], []
    for order, columns in zip(orders_of(BACK), piece_columns(down.shape[1], BACK)):
        mine, send = expert_output(unit, order, columns, scale, hidden, down, down_other)
        keep.append(mine)
        coming.append(across(send, order[0]))
    return keep, coming


def cube_sums(keep, got):
    keep, got = list(keep), list(got)
    for phase in range(1, len(LINKS)):
        for at, order in enumerate(orders_of(BACK)):
            keep[at], send = halved(keep[at], got[at])
            got[at] = across(send, order[phase])
    return finished(keep, got)


def three_parts(value):
    high = lax.reduce_precision(value, 8, 7)
    middle = lax.reduce_precision(value - high, 8, 7)
    return high, middle, value - high - middle


def per_device(
    query_latent,
    latent_cache,
    cache_length,
    prefill_latent,
    block_owner,
    tokens,
    expert_ids,
    route_weight,
    gate_weight,
    up_weight,
    down_weight,
):
    peers = lax.axis_size("ep")
    blocks = prefill_latent.shape[1]
    block_len = prefill_latent.shape[2]
    latent = prefill_latent.shape[3]
    tok_rows, top_k = expert_ids.shape

    owner = block_owner.reshape(blocks)
    same = owner[:, None] == owner[None, :]
    earlier = jnp.arange(blocks)[None, :] < jnp.arange(blocks)[:, None]
    order_in = jnp.sum(jnp.logical_and(same, earlier).astype(jnp.int32), axis=1)
    target = owner * 2 + order_in
    chosen = jnp.arange(2 * peers, dtype=jnp.int32)[:, None] == target[None, :]
    packed = jnp.dot(
        chosen.astype(jnp.bfloat16),
        prefill_latent.reshape(blocks, block_len * latent),
        preferred_element_type=jnp.float32,
    ).astype(jnp.bfloat16)

    cube = peers == 2 << len(LINKS) and lax.axis_size("tp") == 1
    weights = (gate_weight[0], up_weight[0], down_weight[0])
    filled = jnp.sum(chosen.astype(jnp.float32), axis=1).reshape(peers, 1, 2)
    side = jnp.zeros((peers, 2 * block_len, max(tok_rows, 2)), jnp.float32)
    side = side.at[:, 3:4, :2].set(filled)
    if not cube:
        expert_of = jnp.arange(peers, dtype=jnp.int32) // 2
        named = expert_ids[None, :, :] == expert_of[:, None, None]
        share = jnp.sum(jnp.where(named, route_weight[None, :, :], 0.0), axis=2)
        side = side.at[:, :3, :tok_rows].set(jnp.stack(three_parts(share), axis=1))
    leaving = jnp.concatenate(
        [packed.reshape(peers, 2 * block_len, latent), side.astype(jnp.bfloat16)], axis=2
    )
    if cube:
        experts = jnp.arange(peers // 2, dtype=jnp.int32)
        named = expert_ids[:, :, None] == experts[None, None, :]
        share = jnp.sum(jnp.where(named, route_weight[:, :, None], 0.0), axis=1)
        parts = jnp.concatenate(three_parts(share), axis=1).astype(jnp.bfloat16)
        parts = jnp.pad(parts, ((0, 0), (0, 128 - parts.shape[1])))
        *gathered, others = gather_cube(tokens, parts, *weights)
        keep, coming = cube_outputs(tok_rows, *gathered, weights, others)
        leaving = hold_back(leaving, keep[-1])
    arrived = lax.all_to_all(leaving, "ep", split_axis=0, concat_axis=0, tiled=True)
    side_in = arrived[:, :, latent:].astype(jnp.float32)
    present = side_in[:, 3, :2].reshape(peers * 2)
    arrived = arrived[:, :, :latent]
    shard_len = latent_cache.shape[1]
    positions = lax.axis_index("tp") * shard_len + jnp.arange(shard_len, dtype=jnp.int32)
    keys = jnp.concatenate(
        [latent_cache[0], arrived.reshape(peers * 2 * block_len, latent)], axis=0
    )
    valid = jnp.concatenate([positions < cache_length[0], jnp.repeat(present > 0, block_len)])
    peak, total, mixed = attend_keys(query_latent[0], keys, valid, VAL)
    peak, total, mixed = combined_all((peak, total, mixed), "tp", join_parts)
    attn_out = (mixed / total[:, None]).astype(jnp.bfloat16)[None]

    if cube:
        moe_out = cube_sums(keep, coming)
    else:
        share_in = jnp.sum(side_in[:, :3, :tok_rows], axis=1)
        moe_out = ring_experts(tokens, share_in, gate_weight, up_weight, down_weight)
    return (attn_out, moe_out)


def solution(mesh):
    in_specs = (
        P(("groups", "ep"), None, None),
        P(("groups", "ep"), "tp", None),
        P(("groups", "ep")),
        P(("groups", "ep"), "tp", None, None),
        P(("groups", "ep"), "tp", None),
        P(("groups", "ep"), None),
        P(("groups", "ep"), None),
        P(("groups", "ep"), None),
        P("ep", None, "tp"),
        P("ep", None, "tp"),
        P("ep", None, "tp"),
    )
    out_specs = (P(("groups", "ep"), None, None), P(("groups", "ep"), "tp"))
    return jax.shard_map(
        per_device, mesh=mesh, in_specs=in_specs, out_specs=out_specs, check_vma=False
    )
```

```python
import functools

import jax
import jax.numpy as jnp
from jax import lax
from jax.experimental import pallas as pl
from jax.experimental.pallas import tpu as pltpu
from jax.sharding import PartitionSpec as P

VAL = 512


SCALE = 192.0 ** (-0.5)
NEG = -1e30


def combined_all(x, axis, combine):
    if lax.axis_size(axis) == 1:
        return x
    everything = jax.tree.map(lambda part: lax.all_gather(part, axis), x)
    leading = jax.tree.map(lambda part: part[0], everything)

    def lap(k, so_far):
        return combine(so_far, jax.tree.map(lambda part: part[k], everything))

    return lax.fori_loop(1, lax.axis_size(axis), lap, leading)


def attend_keys(query, keys, valid, value_width):
    scores = (
        lax.dot_general(query, keys, (((1,), (1,)), ((), ())), preferred_element_type=jnp.float32)
        * SCALE
    )
    scores = jnp.where(valid[None, :], scores, NEG)
    peak = jnp.max(scores, axis=1)
    expo = jnp.where(valid[None, :], jnp.exp(scores - peak[:, None]), 0.0)
    total = jnp.sum(expo, axis=1)
    mixed = jnp.dot(
        expo.astype(jnp.bfloat16), keys[:, :value_width], preferred_element_type=jnp.float32
    )
    return (peak, total, mixed)


def join_parts(first, second):
    peak = jnp.maximum(first[0], second[0])
    left = jnp.exp(first[0] - peak)
    right = jnp.exp(second[0] - peak)
    return (
        peak,
        first[1] * left + second[1] * right,
        first[2] * left[:, None] + second[2] * right[:, None],
    )


def ring_experts(tokens, share, gate_weight, up_weight, down_weight):
    rows = lax.all_gather(tokens, "ep", axis=0, tiled=True)
    gate = jnp.dot(rows, gate_weight[0], preferred_element_type=jnp.float32)
    upper = jnp.dot(rows, up_weight[0], preferred_element_type=jnp.float32)
    hidden = (jax.nn.silu(gate) * upper).astype(jnp.bfloat16)
    if lax.axis_size("tp") > 1:
        hidden = lax.all_gather(hidden, "tp", axis=1, tiled=True)
    partial_out = jnp.dot(hidden, down_weight[0], preferred_element_type=jnp.float32)
    scaled = partial_out * share.reshape(-1)[:, None]
    return lax.psum_scatter(scaled, "ep", scatter_dimension=0, tiled=True).astype(jnp.bfloat16)


MIB = 1024 * 1024

LINKS = (1, 2, 4, 12)
PIECES = ((5, (1, 0, 3, 2)), (5, (0, 2, 1, 3)), (4, (2, 1, 0, 3)))
TURNS = (0, 2, 1)


def across(value, link):
    peers = lax.axis_size("ep")
    return lax.ppermute(value, "ep", [(i, i ^ (2 * LINKS[link])) for i in range(peers)])


def swap_cores(value):
    return lax.ppermute(value, "ep", [(i, i ^ 1) for i in range(lax.axis_size("ep"))])


def slot_of(place, order):
    slot = 0
    for i, step in enumerate(order):
        slot |= ((place >> (len(order) - 1 - i)) & 1) << step
    return slot


ORDERS = [order for _, order in PIECES]


def piece_columns(width):
    shares = [share for share, _ in PIECES]
    one = width // sum(shares)
    ends = [one * sum(shares[: at + 1]) for at in range(len(shares))]
    ends[-1] = width
    return list(zip([0] + ends[:-1], ends))


def whole_call(kernel, operands, out_shape, name, after=()):
    given = len(operands)

    def body(*refs):
        kernel(*refs[:given], *refs[given + len(after) :])

    return pl.pallas_call(
        body,
        in_specs=[pl.BlockSpec(memory_space=pltpu.VMEM)] * given
        + [pl.BlockSpec(memory_space=pl.ANY)] * len(after),
        out_specs=[pl.BlockSpec(memory_space=pltpu.VMEM)] * len(out_shape),
        out_shape=out_shape,
        compiler_params=pltpu.CompilerParams(vmem_limit_bytes=12 * MIB),
        cost_estimate=pl.CostEstimate(
            flops=0,
            bytes_accessed=sum(x.size * x.dtype.itemsize for x in list(operands) + list(out_shape)),
            transcendentals=0,
        ),
        name=name,
    )(*operands, *after)


def joined(held, got, after):
    count = len(held)
    out_shape = [jax.ShapeDtypeStruct((2 * x.shape[0], x.shape[1]), x.dtype) for x in held]

    def kernel(*refs):
        for first, second, out in zip(refs[:count], refs[count : 2 * count], refs[2 * count :]):
            rows = first.shape[0]
            out[:rows] = first[...]
            out[rows:] = second[...]

    return whole_call(kernel, [*held, *got], out_shape, "joined", after)


def hold_back(array, after):
    def kernel(in_ref, out_ref):
        out_ref[...] = in_ref[...]

    shape = jax.ShapeDtypeStruct(array.shape, array.dtype)
    return whole_call(kernel, [array], [shape], "hold_back", (after,))[0]


def gather_cube(tokens, side, gate, up, down):
    steps = len(LINKS)
    others = [swap_cores(weight) for weight in (gate, up, down)]
    held = [tokens[:, start:stop] for start, stop in piece_columns(tokens.shape[1])]
    held[-1] = jnp.concatenate([held[-1], side], axis=1)
    for phase in range(steps):
        got = [across(piece, order[steps - 1 - phase]) for piece, order in zip(held, ORDERS)]
        if phase < steps - 1:
            held = joined(held, got, (others[2:], others[:2], ())[phase])
    return held, got, others


def hidden_kernel(unit, chip_ref, *refs):
    count = len(ORDERS)
    held, got = refs[:count], refs[count : 2 * count]
    gate_ref, up_ref, gate_other_ref, up_other_ref = refs[2 * count : 2 * count + 4]
    hidden_ref, scale_ref, rows_ref, side_ref = refs[2 * count + 4 :]
    step = pl.program_id(0)
    own_steps = pl.num_programs(0) // 2

    @pl.when(step == 0)
    def _():
        for piece, (start, stop) in enumerate(piece_columns(rows_ref.shape[1])):
            half = held[piece].shape[0]
            for place in range(2 * half // unit):
                source = held[piece] if place * unit < half else got[piece]
                at = place * unit % half
                slot = slot_of(place, ORDERS[piece])
                to = slice(slot * unit, (slot + 1) * unit)
                rows_ref[to, start:stop] = source[at : at + unit, : stop - start]
                if piece == count - 1:
                    side_ref[to, :] = source[at : at + unit, stop - start :]
        column = lax.broadcasted_iota(jnp.int32, side_ref.shape, 1)
        experts = 1 << len(LINKS)
        mine = jnp.logical_and(column % experts == chip_ref[0], column < 3 * experts)
        parts = jnp.where(mine, side_ref[...].astype(jnp.float32), 0.0)
        scale_ref[...] = jnp.sum(parts, axis=1, keepdims=True)

    def units(gate_tile, up_tile):
        rows = rows_ref[...]
        gate = jnp.dot(rows, gate_tile[...], preferred_element_type=jnp.float32)
        upper = jnp.dot(rows, up_tile[...], preferred_element_type=jnp.float32)
        hidden_ref[...] = (gate / (1.0 + jnp.exp(-gate)) * upper).astype(jnp.bfloat16)

    @pl.when(step < own_steps)
    def _():
        units(gate_ref, up_ref)

    @pl.when(step >= own_steps)
    def _():
        units(gate_other_ref, up_other_ref)


def expert_hidden(unit, chip, held, got, gate, up, gate_other, up_other):
    width, units = gate.shape
    count = 2 * held[0].shape[0]
    tile = 256
    steps = units // tile
    own = pl.BlockSpec((width, tile), lambda i: (0, jnp.minimum(i, steps - 1)))
    other = pl.BlockSpec((width, tile), lambda i: (0, jnp.maximum(i - steps, 0)))
    return pl.pallas_call(
        functools.partial(hidden_kernel, unit),
        grid=(2 * steps,),
        in_specs=[pl.BlockSpec(memory_space=pltpu.SMEM)]
        + [pl.BlockSpec(array.shape, lambda i: (0, 0)) for array in (*held, *got)]
        + [own, own, other, other],
        out_specs=[
            pl.BlockSpec((count, tile), lambda i: (0, i)),
            pl.BlockSpec((count, 1), lambda i: (0, 0)),
        ],
        out_shape=[
            jax.ShapeDtypeStruct((count, 2 * units), jnp.bfloat16),
            jax.ShapeDtypeStruct((count, 1), jnp.float32),
        ],
        scratch_shapes=[
            pltpu.VMEM((count, width), jnp.bfloat16),
            pltpu.VMEM((count, sum(piece.shape[1] for piece in held) - width), jnp.bfloat16),
        ],
        compiler_params=pltpu.CompilerParams(vmem_limit_bytes=48 * MIB),
        cost_estimate=pl.CostEstimate(
            flops=8 * count * width * units,
            bytes_accessed=2 * (count * width + 4 * width * units + 2 * count * units),
            transcendentals=2 * count * units,
        ),
        name="expert_hidden",
    )(chip, *held, *got, gate, up, gate_other, up_other)


def output_kernel(unit, order, tiles, scale_ref, hidden_ref, *refs):
    down, down_other = refs[:tiles], refs[tiles : 2 * tiles]
    keep_ref, send_ref = refs[-2:]
    units, tile = down[0].shape
    places = hidden_ref.shape[0] // unit
    for out_ref, first in ((send_ref, places // 2), (keep_ref, 0)):
        slots = [slot_of(first + at, order) for at in range(places // 2)]
        rows = [slice(slot * unit, (slot + 1) * unit) for slot in slots]
        hidden = jnp.concatenate([hidden_ref[row] for row in rows], axis=0)
        scale = jnp.concatenate([scale_ref[row] for row in rows], axis=0)
        for at in range(tiles):
            out = jnp.dot(hidden[:, :units], down[at][...], preferred_element_type=jnp.float32)
            out += jnp.dot(hidden[:, units:], down_other[at][...], preferred_element_type=jnp.float32)
            out_ref[:, at * tile : (at + 1) * tile] = out * scale


def expert_output(unit, order, columns, scale, hidden, down, down_other, after):
    units = down.shape[0]
    start, stop = columns
    count = hidden.shape[0]
    tile = 256
    tiles = (stop - start) // tile
    half = jax.ShapeDtypeStruct((count // 2, stop - start), jnp.float32)

    def tile_at(at):
        return pl.BlockSpec((units, tile), lambda i: (0, start // tile + at))

    return pl.pallas_call(
        functools.partial(output_kernel, unit, order, tiles),
        grid=(1,),
        in_specs=[
            pl.BlockSpec((count, 1), lambda i: (0, 0)),
            pl.BlockSpec((count, 2 * units), lambda i: (0, 0)),
        ]
        + [tile_at(at) for at in range(tiles)] * 2
        + [pl.BlockSpec(memory_space=pl.ANY)] * len(after),
        out_specs=[pl.BlockSpec((count // 2, stop - start), lambda i: (0, 0))] * 2,
        out_shape=[half] * 2,
        compiler_params=pltpu.CompilerParams(vmem_limit_bytes=24 * MIB),
        cost_estimate=pl.CostEstimate(
            flops=4 * count * (stop - start) * units,
            bytes_accessed=4 * (stop - start) * units + 4 * count * (stop - start + units),
            transcendentals=0,
        ),
        name="expert_output",
    )(scale, hidden, *[down] * tiles, *[down_other] * tiles, *after)


def halved(keep, got, after):
    rows, width = keep.shape
    half = jax.ShapeDtypeStruct((rows // 2, width), keep.dtype)

    def kernel(keep_ref, got_ref, first_ref, second_ref):
        second_ref[...] = keep_ref[rows // 2 :] + got_ref[rows // 2 :]
        first_ref[...] = keep_ref[: rows // 2] + got_ref[: rows // 2]

    return whole_call(kernel, [keep, got], [half, half], "halved", after)


def finished(keep, got):
    count = len(keep)
    width = sum(piece.shape[1] for piece in keep)

    def kernel(*refs):
        for at, (start, stop) in enumerate(piece_columns(width)):
            total = refs[at][...] + refs[count + at][...]
            refs[2 * count][:, start:stop] = total.astype(jnp.bfloat16)

    shape = jax.ShapeDtypeStruct((keep[0].shape[0], width), jnp.bfloat16)
    return whole_call(kernel, [*keep, *got], [shape], "finished")[0]


def cube_outputs(unit, held, got, weights, others):
    gate, up, down = weights
    gate_other, up_other, down_other = others
    chip = (lax.axis_index("ep") // 2).astype(jnp.int32).reshape(1)
    hidden, scale = expert_hidden(unit, chip, held, got, gate, up, gate_other, up_other)
    keep, coming = [], []
    for order, columns in zip(ORDERS, piece_columns(down.shape[1])):
        after = keep[-1:]
        mine, send = expert_output(unit, order, columns, scale, hidden, down, down_other, after)
        keep.append(mine)
        coming.append(across(send, order[0]))
    return keep, coming


def cube_sums(keep, got):
    keep, got, after = list(keep), list(got), ()
    for phase in range(1, len(LINKS)):
        for at in TURNS:
            keep[at], send = halved(keep[at], got[at], after)
            got[at] = across(send, ORDERS[at][phase])
            after = (keep[at],)
    return finished(keep, got)


def three_parts(value):
    high = lax.reduce_precision(value, 8, 7)
    middle = lax.reduce_precision(value - high, 8, 7)
    return high, middle, value - high - middle


def per_device(
    query_latent,
    latent_cache,
    cache_length,
    prefill_latent,
    block_owner,
    tokens,
    expert_ids,
    route_weight,
    gate_weight,
    up_weight,
    down_weight,
):
    peers = lax.axis_size("ep")
    blocks = prefill_latent.shape[1]
    block_len = prefill_latent.shape[2]
    latent = prefill_latent.shape[3]
    tok_rows, top_k = expert_ids.shape

    cube = peers == 2 << len(LINKS) and lax.axis_size("tp") == 1
    weights = (gate_weight[0], up_weight[0], down_weight[0])
    if cube:
        experts = jnp.arange(peers // 2, dtype=jnp.int32)
        named = expert_ids[:, :, None] == experts[None, None, :]
        share = jnp.sum(jnp.where(named, route_weight[:, :, None], 0.0), axis=1)
        parts = jnp.concatenate(three_parts(share), axis=1).astype(jnp.bfloat16)
        parts = jnp.pad(parts, ((0, 0), (0, 128 - parts.shape[1])))
        *gathered, others = gather_cube(tokens, parts, *weights)
        keep, coming = cube_outputs(tok_rows, *gathered, weights, others)
        prefill_latent = hold_back(prefill_latent, keep[-1])

    owner = block_owner.reshape(blocks)
    same = owner[:, None] == owner[None, :]
    earlier = jnp.arange(blocks)[None, :] < jnp.arange(blocks)[:, None]
    order_in = jnp.sum(jnp.logical_and(same, earlier).astype(jnp.int32), axis=1)
    target = owner * 2 + order_in
    chosen = jnp.arange(2 * peers, dtype=jnp.int32)[:, None] == target[None, :]
    packed = jnp.dot(
        chosen.astype(jnp.bfloat16),
        prefill_latent.reshape(blocks, block_len * latent),
        preferred_element_type=jnp.float32,
    ).astype(jnp.bfloat16)

    filled = jnp.sum(chosen.astype(jnp.float32), axis=1).reshape(peers, 1, 2)
    side = jnp.zeros((peers, 2 * block_len, max(tok_rows, 2)), jnp.float32)
    side = side.at[:, 3:4, :2].set(filled)
    if not cube:
        expert_of = jnp.arange(peers, dtype=jnp.int32) // 2
        named = expert_ids[None, :, :] == expert_of[:, None, None]
        share = jnp.sum(jnp.where(named, route_weight[None, :, :], 0.0), axis=2)
        side = side.at[:, :3, :tok_rows].set(jnp.stack(three_parts(share), axis=1))
    leaving = jnp.concatenate(
        [packed.reshape(peers, 2 * block_len, latent), side.astype(jnp.bfloat16)], axis=2
    )
    arrived = lax.all_to_all(leaving, "ep", split_axis=0, concat_axis=0, tiled=True)
    side_in = arrived[:, :, latent:].astype(jnp.float32)
    present = side_in[:, 3, :2].reshape(peers * 2)
    arrived = arrived[:, :, :latent]
    shard_len = latent_cache.shape[1]
    positions = lax.axis_index("tp") * shard_len + jnp.arange(shard_len, dtype=jnp.int32)
    keys = jnp.concatenate(
        [latent_cache[0], arrived.reshape(peers * 2 * block_len, latent)], axis=0
    )
    valid = jnp.concatenate([positions < cache_length[0], jnp.repeat(present > 0, block_len)])
    peak, total, mixed = attend_keys(query_latent[0], keys, valid, VAL)
    peak, total, mixed = combined_all((peak, total, mixed), "tp", join_parts)
    attn_out = (mixed / total[:, None]).astype(jnp.bfloat16)[None]

    if cube:
        moe_out = cube_sums(keep, coming)
    else:
        share_in = jnp.sum(side_in[:, :3, :tok_rows], axis=1)
        moe_out = ring_experts(tokens, share_in, gate_weight, up_weight, down_weight)
    return (attn_out, moe_out)


def solution(mesh):
    in_specs = (
        P(("groups", "ep"), None, None),
        P(("groups", "ep"), "tp", None),
        P(("groups", "ep")),
        P(("groups", "ep"), "tp", None, None),
        P(("groups", "ep"), "tp", None),
        P(("groups", "ep"), None),
        P(("groups", "ep"), None),
        P(("groups", "ep"), None),
        P("ep", None, "tp"),
        P("ep", None, "tp"),
        P("ep", None, "tp"),
    )
    out_specs = (P(("groups", "ep"), None, None), P(("groups", "ep"), "tp"))
    return jax.shard_map(
        per_device, mesh=mesh, in_specs=in_specs, out_specs=out_specs, check_vma=False
    )
```

```python
import functools

import jax
import jax.numpy as jnp
from jax import lax
from jax.experimental import pallas as pl
from jax.experimental.pallas import tpu as pltpu
from jax.sharding import PartitionSpec as P

VAL = 512


SCALE = 192.0 ** (-0.5)
NEG = -1e30


def combined_all(x, axis, combine):
    if lax.axis_size(axis) == 1:
        return x
    everything = jax.tree.map(lambda part: lax.all_gather(part, axis), x)
    leading = jax.tree.map(lambda part: part[0], everything)

    def lap(k, so_far):
        return combine(so_far, jax.tree.map(lambda part: part[k], everything))

    return lax.fori_loop(1, lax.axis_size(axis), lap, leading)


def attend_keys(query, keys, valid, value_width):
    scores = (
        lax.dot_general(query, keys, (((1,), (1,)), ((), ())), preferred_element_type=jnp.float32)
        * SCALE
    )
    scores = jnp.where(valid[None, :], scores, NEG)
    peak = jnp.max(scores, axis=1)
    expo = jnp.where(valid[None, :], jnp.exp(scores - peak[:, None]), 0.0)
    total = jnp.sum(expo, axis=1)
    mixed = jnp.dot(
        expo.astype(jnp.bfloat16), keys[:, :value_width], preferred_element_type=jnp.float32
    )
    return (peak, total, mixed)


def join_parts(first, second):
    peak = jnp.maximum(first[0], second[0])
    left = jnp.exp(first[0] - peak)
    right = jnp.exp(second[0] - peak)
    return (
        peak,
        first[1] * left + second[1] * right,
        first[2] * left[:, None] + second[2] * right[:, None],
    )


def ring_experts(tokens, share, gate_weight, up_weight, down_weight):
    rows = lax.all_gather(tokens, "ep", axis=0, tiled=True)
    gate = jnp.dot(rows, gate_weight[0], preferred_element_type=jnp.float32)
    upper = jnp.dot(rows, up_weight[0], preferred_element_type=jnp.float32)
    hidden = (jax.nn.silu(gate) * upper).astype(jnp.bfloat16)
    if lax.axis_size("tp") > 1:
        hidden = lax.all_gather(hidden, "tp", axis=1, tiled=True)
    partial_out = jnp.dot(hidden, down_weight[0], preferred_element_type=jnp.float32)
    scaled = partial_out * share.reshape(-1)[:, None]
    return lax.psum_scatter(scaled, "ep", scatter_dimension=0, tiled=True).astype(jnp.bfloat16)


MIB = 1024 * 1024

LINKS = (1, 2, 4, 12)
PIECES = ((5, (1, 0, 3, 2)), (5, (0, 2, 1, 3)), (4, (2, 1, 0, 3)))
TURNS = (0, 2, 1)


def across(value, link):
    peers = lax.axis_size("ep")
    return lax.ppermute(value, "ep", [(i, i ^ (2 * LINKS[link])) for i in range(peers)])


def swap_cores(value):
    return lax.ppermute(value, "ep", [(i, i ^ 1) for i in range(lax.axis_size("ep"))])


def slot_of(place, order):
    slot = 0
    for i, step in enumerate(order):
        slot |= ((place >> (len(order) - 1 - i)) & 1) << step
    return slot


ORDERS = [order for _, order in PIECES]


def piece_columns(width):
    shares = [share for share, _ in PIECES]
    one = width // sum(shares)
    ends = [one * sum(shares[: at + 1]) for at in range(len(shares))]
    ends[-1] = width
    return list(zip([0] + ends[:-1], ends))


def whole_call(kernel, operands, out_shape, name, after=()):
    given = len(operands)

    def body(*refs):
        kernel(*refs[:given], *refs[given + len(after) :])

    return pl.pallas_call(
        body,
        in_specs=[pl.BlockSpec(memory_space=pltpu.VMEM)] * given
        + [pl.BlockSpec(memory_space=pl.ANY)] * len(after),
        out_specs=[pl.BlockSpec(memory_space=pltpu.VMEM)] * len(out_shape),
        out_shape=out_shape,
        compiler_params=pltpu.CompilerParams(vmem_limit_bytes=12 * MIB),
        cost_estimate=pl.CostEstimate(
            flops=0,
            bytes_accessed=sum(x.size * x.dtype.itemsize for x in list(operands) + list(out_shape)),
            transcendentals=0,
        ),
        name=name,
    )(*operands, *after)


def joined(held, got, after):
    count = len(held)
    out_shape = [jax.ShapeDtypeStruct((2 * x.shape[0], x.shape[1]), x.dtype) for x in held]

    def kernel(*refs):
        for first, second, out in zip(refs[:count], refs[count : 2 * count], refs[2 * count :]):
            rows = first.shape[0]
            out[:rows] = first[...]
            out[rows:] = second[...]

    return whole_call(kernel, [*held, *got], out_shape, "joined", after)


def hold_back(array, after):
    def kernel(in_ref, out_ref):
        out_ref[...] = in_ref[...]

    shape = jax.ShapeDtypeStruct(array.shape, array.dtype)
    return whole_call(kernel, [array], [shape], "hold_back", (after,))[0]


def first_joined(held, got, widths, after):
    rows = held[0].shape[0]
    out_shape = [jax.ShapeDtypeStruct((2 * rows, width), held[0].dtype) for width in widths]

    def kernel(first, rest, got_first, got_rest, *outs):
        outs[0][:rows] = first[...]
        outs[0][rows:] = got_first[...]
        start = 0
        for out, width in zip(outs[1:], widths[1:]):
            out[:rows] = rest[:, start : start + width]
            out[rows:] = got_rest[:, start : start + width]
            start += width

    return whole_call(kernel, [*held, *got], out_shape, "first_joined", after)


def gather_cube(tokens, side, gate, up, down):
    steps = len(LINKS)
    others = [swap_cores(weight) for weight in (gate, up, down)]
    columns = piece_columns(tokens.shape[1])
    widths = [stop - start for start, stop in columns]
    widths[-1] += side.shape[1]
    cut = columns[0][1]
    held = [tokens[:, :cut], jnp.concatenate([tokens[:, cut:], side], axis=1)]
    got = [across(piece, order[-1]) for piece, order in zip(held, ORDERS)]
    held = first_joined(held, got, widths, others[2:])
    for phase in range(1, steps):
        got = [across(piece, order[steps - 1 - phase]) for piece, order in zip(held, ORDERS)]
        if phase < steps - 1:
            held = joined(held, got, others[:2] if phase == 1 else ())
    return held, got, others


def hidden_kernel(unit, chip_ref, *refs):
    count = len(ORDERS)
    held, got = refs[:count], refs[count : 2 * count]
    gate_ref, up_ref, gate_other_ref, up_other_ref = refs[2 * count : 2 * count + 4]
    hidden_ref, scale_ref, rows_ref, side_ref = refs[2 * count + 4 :]
    step = pl.program_id(0)
    own_steps = pl.num_programs(0) // 2

    @pl.when(step == 0)
    def _():
        for piece, (start, stop) in enumerate(piece_columns(rows_ref.shape[1])):
            half = held[piece].shape[0]
            for place in range(2 * half // unit):
                source = held[piece] if place * unit < half else got[piece]
                at = place * unit % half
                slot = slot_of(place, ORDERS[piece])
                to = slice(slot * unit, (slot + 1) * unit)
                rows_ref[to, start:stop] = source[at : at + unit, : stop - start]
                if piece == count - 1:
                    side_ref[to, :] = source[at : at + unit, stop - start :]
        column = lax.broadcasted_iota(jnp.int32, side_ref.shape, 1)
        experts = 1 << len(LINKS)
        mine = jnp.logical_and(column % experts == chip_ref[0], column < 3 * experts)
        parts = jnp.where(mine, side_ref[...].astype(jnp.float32), 0.0)
        scale_ref[...] = jnp.sum(parts, axis=1, keepdims=True)

    def units(gate_tile, up_tile):
        rows = rows_ref[...]
        gate = jnp.dot(rows, gate_tile[...], preferred_element_type=jnp.float32)
        upper = jnp.dot(rows, up_tile[...], preferred_element_type=jnp.float32)
        hidden_ref[...] = (gate / (1.0 + jnp.exp(-gate)) * upper).astype(jnp.bfloat16)

    @pl.when(step < own_steps)
    def _():
        units(gate_ref, up_ref)

    @pl.when(step >= own_steps)
    def _():
        units(gate_other_ref, up_other_ref)


def expert_hidden(unit, chip, held, got, gate, up, gate_other, up_other):
    width, units = gate.shape
    count = 2 * held[0].shape[0]
    tile = 256
    steps = units // tile
    own = pl.BlockSpec((width, tile), lambda i: (0, jnp.minimum(i, steps - 1)))
    other = pl.BlockSpec((width, tile), lambda i: (0, jnp.maximum(i - steps, 0)))
    return pl.pallas_call(
        functools.partial(hidden_kernel, unit),
        grid=(2 * steps,),
        in_specs=[pl.BlockSpec(memory_space=pltpu.SMEM)]
        + [pl.BlockSpec(array.shape, lambda i: (0, 0)) for array in (*held, *got)]
        + [own, own, other, other],
        out_specs=[
            pl.BlockSpec((count, tile), lambda i: (0, i)),
            pl.BlockSpec((count, 1), lambda i: (0, 0)),
        ],
        out_shape=[
            jax.ShapeDtypeStruct((count, 2 * units), jnp.bfloat16),
            jax.ShapeDtypeStruct((count, 1), jnp.float32),
        ],
        scratch_shapes=[
            pltpu.VMEM((count, width), jnp.bfloat16),
            pltpu.VMEM((count, sum(piece.shape[1] for piece in held) - width), jnp.bfloat16),
        ],
        compiler_params=pltpu.CompilerParams(vmem_limit_bytes=48 * MIB),
        cost_estimate=pl.CostEstimate(
            flops=8 * count * width * units,
            bytes_accessed=2 * (count * width + 4 * width * units + 2 * count * units),
            transcendentals=2 * count * units,
        ),
        name="expert_hidden",
    )(chip, *held, *got, gate, up, gate_other, up_other)


def output_kernel(unit, order, tiles, scale_ref, hidden_ref, *refs):
    down, down_other = refs[:tiles], refs[tiles : 2 * tiles]
    keep_ref, send_ref = refs[-2:]
    units, tile = down[0].shape
    places = hidden_ref.shape[0] // unit
    for out_ref, first in ((send_ref, places // 2), (keep_ref, 0)):
        slots = [slot_of(first + at, order) for at in range(places // 2)]
        rows = [slice(slot * unit, (slot + 1) * unit) for slot in slots]
        hidden = jnp.concatenate([hidden_ref[row] for row in rows], axis=0)
        scale = jnp.concatenate([scale_ref[row] for row in rows], axis=0)
        for at in range(tiles):
            out = jnp.dot(hidden[:, :units], down[at][...], preferred_element_type=jnp.float32)
            out += jnp.dot(hidden[:, units:], down_other[at][...], preferred_element_type=jnp.float32)
            out_ref[:, at * tile : (at + 1) * tile] = out * scale


def expert_output(unit, order, columns, scale, hidden, down, down_other, after):
    units = down.shape[0]
    start, stop = columns
    count = hidden.shape[0]
    tile = 256
    tiles = (stop - start) // tile
    half = jax.ShapeDtypeStruct((count // 2, stop - start), jnp.float32)

    def tile_at(at):
        return pl.BlockSpec((units, tile), lambda i: (0, start // tile + at))

    return pl.pallas_call(
        functools.partial(output_kernel, unit, order, tiles),
        grid=(1,),
        in_specs=[
            pl.BlockSpec((count, 1), lambda i: (0, 0)),
            pl.BlockSpec((count, 2 * units), lambda i: (0, 0)),
        ]
        + [tile_at(at) for at in range(tiles)] * 2
        + [pl.BlockSpec(memory_space=pl.ANY)] * len(after),
        out_specs=[pl.BlockSpec((count // 2, stop - start), lambda i: (0, 0))] * 2,
        out_shape=[half] * 2,
        compiler_params=pltpu.CompilerParams(vmem_limit_bytes=24 * MIB),
        cost_estimate=pl.CostEstimate(
            flops=4 * count * (stop - start) * units,
            bytes_accessed=4 * (stop - start) * units + 4 * count * (stop - start + units),
            transcendentals=0,
        ),
        name="expert_output",
    )(scale, hidden, *[down] * tiles, *[down_other] * tiles, *after)


def summed(pieces, after):
    rows = pieces[0][-1].shape[0] // 2
    widths = [arrays[0].shape[1] for arrays in pieces]
    operands = [array for arrays in pieces for array in arrays]

    def kernel(*refs):
        out_ref = refs[-1]
        refs, start = list(refs), 0
        for arrays, width in zip(pieces, widths):
            total = refs.pop(0)[...]
            for _ in arrays[1:]:
                total = total + refs.pop(0)[...]
            out_ref[:, start : start + width] = total
            start += width

    return pl.pallas_call(
        kernel,
        grid=(1,),
        in_specs=[pl.BlockSpec((rows, array.shape[1]), lambda i: (1, 0)) for array in operands]
        + [pl.BlockSpec(memory_space=pl.ANY)] * len(after),
        out_specs=pl.BlockSpec((rows, sum(widths)), lambda i: (0, 0)),
        out_shape=jax.ShapeDtypeStruct((rows, sum(widths)), jnp.float32),
        compiler_params=pltpu.CompilerParams(vmem_limit_bytes=14 * MIB),
        cost_estimate=pl.CostEstimate(
            flops=len(operands) * rows * widths[0],
            bytes_accessed=4 * rows * (sum(array.shape[1] for array in operands) + sum(widths)),
            transcendentals=0,
        ),
        name="summed",
    )(*operands, *after)


def finished(pieces, last):
    rows = last[0].shape[0]
    columns = piece_columns(sum(arrays[0].shape[1] for arrays in pieces))
    operands = [array for arrays in pieces for array in arrays]

    def kernel(*refs):
        first, rest, out_ref = refs[-3:]
        refs, cut = list(refs), columns[0][1]
        for at, (start, stop) in enumerate(columns):
            total = refs.pop(0)[...]
            for _ in pieces[at][1:]:
                total = total + refs.pop(0)[...]
            total = total + (first[...] if at == 0 else rest[:, start - cut : stop - cut])
            out_ref[:, start:stop] = total.astype(jnp.bfloat16)

    def top(array):
        return pl.BlockSpec((rows, array.shape[1]), lambda i: (0, 0))

    width = columns[-1][1]
    return pl.pallas_call(
        kernel,
        grid=(1,),
        in_specs=[top(array) for array in (*operands, *last)],
        out_specs=pl.BlockSpec((rows, width), lambda i: (0, 0)),
        out_shape=jax.ShapeDtypeStruct((rows, width), jnp.bfloat16),
        compiler_params=pltpu.CompilerParams(vmem_limit_bytes=14 * MIB),
        cost_estimate=pl.CostEstimate(
            flops=5 * rows * width, bytes_accessed=22 * rows * width, transcendentals=0
        ),
        name="finished",
    )(*operands, *last)


def cube_outputs(unit, held, got, weights, others):
    gate, up, down = weights
    gate_other, up_other, down_other = others
    chip = (lax.axis_index("ep") // 2).astype(jnp.int32).reshape(1)
    hidden, scale = expert_hidden(unit, chip, held, got, gate, up, gate_other, up_other)
    keep, coming = [], []
    for order, columns in zip(ORDERS, piece_columns(down.shape[1])):
        after = keep[-1:]
        mine, send = expert_output(unit, order, columns, scale, hidden, down, down_other, after)
        keep.append(mine)
        coming.append(across(send, order[0]))
    return keep, coming


def cube_sums(keep, got):
    pieces, after = [list(pair) for pair in zip(keep, got)], ()
    for phase in range(1, len(LINKS) - 1):
        for at in TURNS:
            send = summed([pieces[at]], after)
            pieces[at].append(across(send, ORDERS[at][phase]))
            after = (send,)
    first = summed(pieces[:1], after)
    rest = summed(pieces[1:], (first,))
    return finished(pieces, [across(first, ORDERS[0][-1]), across(rest, ORDERS[1][-1])])


def three_parts(value):
    high = lax.reduce_precision(value, 8, 7)
    middle = lax.reduce_precision(value - high, 8, 7)
    return high, middle, value - high - middle


def per_device(
    query_latent,
    latent_cache,
    cache_length,
    prefill_latent,
    block_owner,
    tokens,
    expert_ids,
    route_weight,
    gate_weight,
    up_weight,
    down_weight,
):
    peers = lax.axis_size("ep")
    blocks = prefill_latent.shape[1]
    block_len = prefill_latent.shape[2]
    latent = prefill_latent.shape[3]
    tok_rows, top_k = expert_ids.shape

    cube = peers == 2 << len(LINKS) and lax.axis_size("tp") == 1
    weights = (gate_weight[0], up_weight[0], down_weight[0])
    if cube:
        experts = jnp.arange(peers // 2, dtype=jnp.int32)
        named = expert_ids[:, :, None] == experts[None, None, :]
        share = jnp.sum(jnp.where(named, route_weight[:, :, None], 0.0), axis=1)
        parts = jnp.concatenate(three_parts(share), axis=1).astype(jnp.bfloat16)
        parts = jnp.pad(parts, ((0, 0), (0, 128 - parts.shape[1])))
        *gathered, others = gather_cube(tokens, parts, *weights)
        keep, coming = cube_outputs(tok_rows, *gathered, weights, others)
        prefill_latent = hold_back(prefill_latent, keep[-1])

    owner = block_owner.reshape(blocks)
    same = owner[:, None] == owner[None, :]
    earlier = jnp.arange(blocks)[None, :] < jnp.arange(blocks)[:, None]
    order_in = jnp.sum(jnp.logical_and(same, earlier).astype(jnp.int32), axis=1)
    target = owner * 2 + order_in
    chosen = jnp.arange(2 * peers, dtype=jnp.int32)[:, None] == target[None, :]
    packed = jnp.dot(
        chosen.astype(jnp.bfloat16),
        prefill_latent.reshape(blocks, block_len * latent),
        preferred_element_type=jnp.float32,
    ).astype(jnp.bfloat16)

    filled = jnp.sum(chosen.astype(jnp.float32), axis=1).reshape(peers, 1, 2)
    side = jnp.zeros((peers, 2 * block_len, max(tok_rows, 2)), jnp.float32)
    side = side.at[:, 3:4, :2].set(filled)
    if not cube:
        expert_of = jnp.arange(peers, dtype=jnp.int32) // 2
        named = expert_ids[None, :, :] == expert_of[:, None, None]
        share = jnp.sum(jnp.where(named, route_weight[None, :, :], 0.0), axis=2)
        side = side.at[:, :3, :tok_rows].set(jnp.stack(three_parts(share), axis=1))
    leaving = jnp.concatenate(
        [packed.reshape(peers, 2 * block_len, latent), side.astype(jnp.bfloat16)], axis=2
    )
    arrived = lax.all_to_all(leaving, "ep", split_axis=0, concat_axis=0, tiled=True)
    side_in = arrived[:, :, latent:].astype(jnp.float32)
    present = side_in[:, 3, :2].reshape(peers * 2)
    arrived = arrived[:, :, :latent]
    shard_len = latent_cache.shape[1]
    positions = lax.axis_index("tp") * shard_len + jnp.arange(shard_len, dtype=jnp.int32)
    keys = jnp.concatenate(
        [latent_cache[0], arrived.reshape(peers * 2 * block_len, latent)], axis=0
    )
    valid = jnp.concatenate([positions < cache_length[0], jnp.repeat(present > 0, block_len)])
    peak, total, mixed = attend_keys(query_latent[0], keys, valid, VAL)
    peak, total, mixed = combined_all((peak, total, mixed), "tp", join_parts)
    attn_out = (mixed / total[:, None]).astype(jnp.bfloat16)[None]

    if cube:
        moe_out = cube_sums(keep, coming)
    else:
        share_in = jnp.sum(side_in[:, :3, :tok_rows], axis=1)
        moe_out = ring_experts(tokens, share_in, gate_weight, up_weight, down_weight)
    return (attn_out, moe_out)


def solution(mesh):
    in_specs = (
        P(("groups", "ep"), None, None),
        P(("groups", "ep"), "tp", None),
        P(("groups", "ep")),
        P(("groups", "ep"), "tp", None, None),
        P(("groups", "ep"), "tp", None),
        P(("groups", "ep"), None),
        P(("groups", "ep"), None),
        P(("groups", "ep"), None),
        P("ep", None, "tp"),
        P("ep", None, "tp"),
        P("ep", None, "tp"),
    )
    out_specs = (P(("groups", "ep"), None, None), P(("groups", "ep"), "tp"))
    return jax.shard_map(
        per_device, mesh=mesh, in_specs=in_specs, out_specs=out_specs, check_vma=False
    )
```

```python
import functools

import jax
import jax.numpy as jnp
from jax import lax
from jax.experimental import pallas as pl
from jax.experimental.pallas import tpu as pltpu
from jax.sharding import PartitionSpec as P

VAL = 512


SCALE = 192.0 ** (-0.5)
NEG = -1e30


def combined_all(x, axis, combine):
    if lax.axis_size(axis) == 1:
        return x
    everything = jax.tree.map(lambda part: lax.all_gather(part, axis), x)
    leading = jax.tree.map(lambda part: part[0], everything)

    def lap(k, so_far):
        return combine(so_far, jax.tree.map(lambda part: part[k], everything))

    return lax.fori_loop(1, lax.axis_size(axis), lap, leading)


def attend_keys(query, keys, valid, value_width):
    scores = (
        lax.dot_general(query, keys, (((1,), (1,)), ((), ())), preferred_element_type=jnp.float32)
        * SCALE
    )
    scores = jnp.where(valid[None, :], scores, NEG)
    peak = jnp.max(scores, axis=1)
    expo = jnp.where(valid[None, :], jnp.exp(scores - peak[:, None]), 0.0)
    total = jnp.sum(expo, axis=1)
    mixed = jnp.dot(
        expo.astype(jnp.bfloat16), keys[:, :value_width], preferred_element_type=jnp.float32
    )
    return (peak, total, mixed)


def join_parts(first, second):
    peak = jnp.maximum(first[0], second[0])
    left = jnp.exp(first[0] - peak)
    right = jnp.exp(second[0] - peak)
    return (
        peak,
        first[1] * left + second[1] * right,
        first[2] * left[:, None] + second[2] * right[:, None],
    )


def ring_experts(tokens, share, gate_weight, up_weight, down_weight):
    rows = lax.all_gather(tokens, "ep", axis=0, tiled=True)
    gate = jnp.dot(rows, gate_weight[0], preferred_element_type=jnp.float32)
    upper = jnp.dot(rows, up_weight[0], preferred_element_type=jnp.float32)
    hidden = (jax.nn.silu(gate) * upper).astype(jnp.bfloat16)
    if lax.axis_size("tp") > 1:
        hidden = lax.all_gather(hidden, "tp", axis=1, tiled=True)
    partial_out = jnp.dot(hidden, down_weight[0], preferred_element_type=jnp.float32)
    scaled = partial_out * share.reshape(-1)[:, None]
    return lax.psum_scatter(scaled, "ep", scatter_dimension=0, tiled=True).astype(jnp.bfloat16)


MIB = 1024 * 1024

LINKS = (1, 2, 4, 12)
PIECES = ((5, (1, 0, 3, 2)), (5, (0, 2, 1, 3)), (4, (2, 1, 0, 3)))
TURNS = (0, 2, 1)


def across(value, link):
    peers = lax.axis_size("ep")
    return lax.ppermute(value, "ep", [(i, i ^ (2 * LINKS[link])) for i in range(peers)])


def swap_cores(value):
    return lax.ppermute(value, "ep", [(i, i ^ 1) for i in range(lax.axis_size("ep"))])


def slot_of(place, order):
    slot = 0
    for i, step in enumerate(order):
        slot |= ((place >> (len(order) - 1 - i)) & 1) << step
    return slot


ORDERS = [order for _, order in PIECES]


def piece_columns(width):
    shares = [share for share, _ in PIECES]
    one = width // sum(shares)
    ends = [one * sum(shares[: at + 1]) for at in range(len(shares))]
    ends[-1] = width
    return list(zip([0] + ends[:-1], ends))


def whole_call(kernel, operands, out_shape, name, after=()):
    given = len(operands)

    def body(*refs):
        kernel(*refs[:given], *refs[given + len(after) :])

    return pl.pallas_call(
        body,
        in_specs=[pl.BlockSpec(memory_space=pltpu.VMEM)] * given
        + [pl.BlockSpec(memory_space=pl.ANY)] * len(after),
        out_specs=[pl.BlockSpec(memory_space=pltpu.VMEM)] * len(out_shape),
        out_shape=out_shape,
        compiler_params=pltpu.CompilerParams(vmem_limit_bytes=12 * MIB),
        cost_estimate=pl.CostEstimate(
            flops=0,
            bytes_accessed=sum(x.size * x.dtype.itemsize for x in list(operands) + list(out_shape)),
            transcendentals=0,
        ),
        name=name,
    )(*operands, *after)


def joined(held, got, after):
    count = len(held)
    out_shape = [jax.ShapeDtypeStruct((2 * x.shape[0], x.shape[1]), x.dtype) for x in held]

    def kernel(*refs):
        for first, second, out in zip(refs[:count], refs[count : 2 * count], refs[2 * count :]):
            rows = first.shape[0]
            out[:rows] = first[...]
            out[rows:] = second[...]

    return whole_call(kernel, [*held, *got], out_shape, "joined", after)


def hold_back(array, after):
    def kernel(in_ref, out_ref):
        out_ref[...] = in_ref[...]

    shape = jax.ShapeDtypeStruct(array.shape, array.dtype)
    return whole_call(kernel, [array], [shape], "hold_back", (after,))[0]


def first_joined(held, got, widths, after):
    rows = held[0].shape[0]
    out_shape = [jax.ShapeDtypeStruct((2 * rows, width), held[0].dtype) for width in widths]

    def kernel(first, rest, got_first, got_rest, *outs):
        outs[0][:rows] = first[...]
        outs[0][rows:] = got_first[...]
        start = 0
        for out, width in zip(outs[1:], widths[1:]):
            out[:rows] = rest[:, start : start + width]
            out[rows:] = got_rest[:, start : start + width]
            start += width

    return whole_call(kernel, [*held, *got], out_shape, "first_joined", after)


def gather_cube(unit, chip, tokens, side, gate, up, down):
    steps = len(LINKS)
    others = [swap_cores(weight) for weight in (gate, up, down)]
    columns = piece_columns(tokens.shape[1])
    widths = [stop - start for start, stop in columns]
    widths[-1] += side.shape[1]
    cut = columns[0][1]
    held = [tokens[:, :cut], jnp.concatenate([tokens[:, cut:], side], axis=1)]
    got = [across(piece, order[-1]) for piece, order in zip(held, ORDERS)]
    held = first_joined(held, got, widths, others[2:])
    for phase in range(1, steps):
        got = [across(piece, order[steps - 1 - phase]) for piece, order in zip(held, ORDERS)]
        if phase < steps - 1:
            held = joined(held, got, others[:2] if phase == 1 else ())
    weights = (gate, up, *others[:2])
    so_far = expert_part(unit, chip, held, weights)
    return expert_part(unit, chip, got, weights, so_far), others


def part_kernel(unit, last, chip_ref, *refs):
    count = len(ORDERS)
    pieces = refs[:count]
    gate_ref, up_ref, gate_other_ref, up_other_ref = refs[count : count + 4]
    if last:
        gate_part, up_part, scale_part, hidden_ref, scale_ref, gate_sum, up_sum = refs[count + 4 :]
    else:
        gate_sum, up_sum, scale_ref = refs[count + 4 :]
    step = pl.program_id(0)
    own_steps = pl.num_programs(0) // 2
    columns = piece_columns(gate_ref.shape[0])
    places = pieces[0].shape[0] // unit

    def slots(order):
        for at in range(places):
            slot = slot_of(at + (places if last else 0), order)
            yield slice(slot * unit, (slot + 1) * unit), slice(at * unit, (at + 1) * unit)

    @pl.when(step == 0)
    def _():
        scale_ref[...] = scale_part[...] if last else jnp.zeros_like(scale_ref)
        start, stop = columns[-1]
        side = pieces[-1][:, stop - start :].astype(jnp.float32)
        column = lax.broadcasted_iota(jnp.int32, side.shape, 1)
        experts = 1 << len(LINKS)
        mine = jnp.logical_and(column % experts == chip_ref[0], column < 3 * experts)
        scale = jnp.sum(jnp.where(mine, side, 0.0), axis=1, keepdims=True)
        for to, source in slots(ORDERS[-1]):
            scale_ref[to, :] = scale[source]

    def add_up(tile, total, so_far):
        total[...] = so_far[...] if last else jnp.zeros_like(total)
        for piece, (start, stop) in enumerate(columns):
            part = jnp.dot(
                pieces[piece][:, : stop - start],
                tile[start:stop, :],
                preferred_element_type=jnp.float32,
            )
            for to, source in slots(ORDERS[piece]):
                total[to, :] += part[source]

    def units(gate_tile, up_tile):
        add_up(gate_tile, gate_sum, gate_part if last else None)
        add_up(up_tile, up_sum, up_part if last else None)
        if last:
            gate = gate_sum[...]
            hidden_ref[...] = (gate / (1.0 + jnp.exp(-gate)) * up_sum[...]).astype(jnp.bfloat16)

    @pl.when(step < own_steps)
    def _():
        units(gate_ref, up_ref)

    @pl.when(step >= own_steps)
    def _():
        units(gate_other_ref, up_other_ref)


def expert_part(unit, chip, pieces, weights, so_far=()):
    width, units = weights[0].shape
    rows = pieces[0].shape[0]
    tile = 256
    steps = units // tile
    own = pl.BlockSpec((width, tile), lambda i: (0, jnp.minimum(i, steps - 1)))
    other = pl.BlockSpec((width, tile), lambda i: (0, jnp.maximum(i - steps, 0)))
    tiled = pl.BlockSpec((2 * rows, tile), lambda i: (0, i))
    single = pl.BlockSpec((2 * rows, 1), lambda i: (0, 0))
    total = jax.ShapeDtypeStruct((2 * rows, 2 * units), jnp.float32)
    scale = jax.ShapeDtypeStruct((2 * rows, 1), jnp.float32)
    hidden = jax.ShapeDtypeStruct((2 * rows, 2 * units), jnp.bfloat16)
    last = len(so_far) > 0
    return pl.pallas_call(
        functools.partial(part_kernel, unit, last),
        grid=(2 * steps,),
        in_specs=[pl.BlockSpec(memory_space=pltpu.SMEM)]
        + [pl.BlockSpec(array.shape, lambda i: (0, 0)) for array in pieces]
        + [own, own, other, other]
        + ([tiled, tiled, single] if last else []),
        out_specs=[tiled, single] if last else [tiled, tiled, single],
        out_shape=[hidden, scale] if last else [total, total, scale],
        scratch_shapes=[pltpu.VMEM((2 * rows, tile), jnp.float32)] * (2 if last else 0),
        compiler_params=pltpu.CompilerParams(vmem_limit_bytes=48 * MIB),
        cost_estimate=pl.CostEstimate(
            flops=8 * rows * width * units,
            bytes_accessed=8 * width * units + 2 * rows * width + 24 * rows * units,
            transcendentals=4 * rows * units if last else 0,
        ),
        name="expert_part",
    )(chip, *pieces, *weights, *so_far)


def output_kernel(unit, order, tiles, scale_ref, hidden_ref, *refs):
    down, down_other = refs[:tiles], refs[tiles : 2 * tiles]
    keep_ref, send_ref = refs[-2:]
    units, tile = down[0].shape
    places = hidden_ref.shape[0] // unit
    for out_ref, first in ((send_ref, places // 2), (keep_ref, 0)):
        slots = [slot_of(first + at, order) for at in range(places // 2)]
        rows = [slice(slot * unit, (slot + 1) * unit) for slot in slots]
        hidden = jnp.concatenate([hidden_ref[row] for row in rows], axis=0)
        scale = jnp.concatenate([scale_ref[row] for row in rows], axis=0)
        for at in range(tiles):
            out = jnp.dot(hidden[:, :units], down[at][...], preferred_element_type=jnp.float32)
            out += jnp.dot(hidden[:, units:], down_other[at][...], preferred_element_type=jnp.float32)
            out_ref[:, at * tile : (at + 1) * tile] = out * scale


def expert_output(unit, order, columns, scale, hidden, down, down_other, after):
    units = down.shape[0]
    start, stop = columns
    count = hidden.shape[0]
    tile = 256
    tiles = (stop - start) // tile
    half = jax.ShapeDtypeStruct((count // 2, stop - start), jnp.float32)

    def tile_at(at):
        return pl.BlockSpec((units, tile), lambda i: (0, start // tile + at))

    return pl.pallas_call(
        functools.partial(output_kernel, unit, order, tiles),
        grid=(1,),
        in_specs=[
            pl.BlockSpec((count, 1), lambda i: (0, 0)),
            pl.BlockSpec((count, 2 * units), lambda i: (0, 0)),
        ]
        + [tile_at(at) for at in range(tiles)] * 2
        + [pl.BlockSpec(memory_space=pl.ANY)] * len(after),
        out_specs=[pl.BlockSpec((count // 2, stop - start), lambda i: (0, 0))] * 2,
        out_shape=[half] * 2,
        compiler_params=pltpu.CompilerParams(vmem_limit_bytes=24 * MIB),
        cost_estimate=pl.CostEstimate(
            flops=4 * count * (stop - start) * units,
            bytes_accessed=4 * (stop - start) * units + 4 * count * (stop - start + units),
            transcendentals=0,
        ),
        name="expert_output",
    )(scale, hidden, *[down] * tiles, *[down_other] * tiles, *after)


def halved(keep, got, after):
    rows, width = keep.shape
    half = jax.ShapeDtypeStruct((rows // 2, width), keep.dtype)

    def kernel(keep_ref, got_ref, first_ref, second_ref):
        second_ref[...] = keep_ref[rows // 2 :] + got_ref[rows // 2 :]
        first_ref[...] = keep_ref[: rows // 2] + got_ref[: rows // 2]

    return whole_call(kernel, [keep, got], [half, half], "halved", after)


def finished(keep, got):
    count = len(keep)
    width = sum(piece.shape[1] for piece in keep)

    def kernel(*refs):
        for at, (start, stop) in enumerate(piece_columns(width)):
            total = refs[at][...] + refs[count + at][...]
            refs[2 * count][:, start:stop] = total.astype(jnp.bfloat16)

    shape = jax.ShapeDtypeStruct((keep[0].shape[0], width), jnp.bfloat16)
    return whole_call(kernel, [*keep, *got], [shape], "finished")[0]


def cube_outputs(unit, hidden, scale, down, down_other):
    keep, coming = [], []
    for order, columns in zip(ORDERS, piece_columns(down.shape[1])):
        after = keep[-1:]
        mine, send = expert_output(unit, order, columns, scale, hidden, down, down_other, after)
        keep.append(mine)
        coming.append(across(send, order[0]))
    return keep, coming


def cube_sums(keep, got):
    keep, got, after = list(keep), list(got), ()
    for phase in range(1, len(LINKS)):
        for at in TURNS:
            keep[at], send = halved(keep[at], got[at], after)
            got[at] = across(send, ORDERS[at][phase])
            after = (keep[at],)
    return finished(keep, got)


def three_parts(value):
    high = lax.reduce_precision(value, 8, 7)
    middle = lax.reduce_precision(value - high, 8, 7)
    return high, middle, value - high - middle


def per_device(
    query_latent,
    latent_cache,
    cache_length,
    prefill_latent,
    block_owner,
    tokens,
    expert_ids,
    route_weight,
    gate_weight,
    up_weight,
    down_weight,
):
    peers = lax.axis_size("ep")
    blocks = prefill_latent.shape[1]
    block_len = prefill_latent.shape[2]
    latent = prefill_latent.shape[3]
    tok_rows, top_k = expert_ids.shape

    cube = peers == 2 << len(LINKS) and lax.axis_size("tp") == 1
    weights = (gate_weight[0], up_weight[0], down_weight[0])
    if cube:
        experts = jnp.arange(peers // 2, dtype=jnp.int32)
        named = expert_ids[:, :, None] == experts[None, None, :]
        share = jnp.sum(jnp.where(named, route_weight[:, :, None], 0.0), axis=1)
        parts = jnp.concatenate(three_parts(share), axis=1).astype(jnp.bfloat16)
        parts = jnp.pad(parts, ((0, 0), (0, 128 - parts.shape[1])))
        chip = (lax.axis_index("ep") // 2).astype(jnp.int32).reshape(1)
        (hidden, scale), others = gather_cube(tok_rows, chip, tokens, parts, *weights)
        keep, coming = cube_outputs(tok_rows, hidden, scale, weights[2], others[2])
        prefill_latent = hold_back(prefill_latent, keep[-1])

    owner = block_owner.reshape(blocks)
    same = owner[:, None] == owner[None, :]
    earlier = jnp.arange(blocks)[None, :] < jnp.arange(blocks)[:, None]
    order_in = jnp.sum(jnp.logical_and(same, earlier).astype(jnp.int32), axis=1)
    target = owner * 2 + order_in
    chosen = jnp.arange(2 * peers, dtype=jnp.int32)[:, None] == target[None, :]
    packed = jnp.dot(
        chosen.astype(jnp.bfloat16),
        prefill_latent.reshape(blocks, block_len * latent),
        preferred_element_type=jnp.float32,
    ).astype(jnp.bfloat16)

    filled = jnp.sum(chosen.astype(jnp.float32), axis=1).reshape(peers, 1, 2)
    side = jnp.zeros((peers, 2 * block_len, max(tok_rows, 2)), jnp.float32)
    side = side.at[:, 3:4, :2].set(filled)
    if not cube:
        expert_of = jnp.arange(peers, dtype=jnp.int32) // 2
        named = expert_ids[None, :, :] == expert_of[:, None, None]
        share = jnp.sum(jnp.where(named, route_weight[None, :, :], 0.0), axis=2)
        side = side.at[:, :3, :tok_rows].set(jnp.stack(three_parts(share), axis=1))
    leaving = jnp.concatenate(
        [packed.reshape(peers, 2 * block_len, latent), side.astype(jnp.bfloat16)], axis=2
    )
    arrived = lax.all_to_all(leaving, "ep", split_axis=0, concat_axis=0, tiled=True)
    side_in = arrived[:, :, latent:].astype(jnp.float32)
    present = side_in[:, 3, :2].reshape(peers * 2)
    arrived = arrived[:, :, :latent]
    shard_len = latent_cache.shape[1]
    positions = lax.axis_index("tp") * shard_len + jnp.arange(shard_len, dtype=jnp.int32)
    keys = jnp.concatenate(
        [latent_cache[0], arrived.reshape(peers * 2 * block_len, latent)], axis=0
    )
    valid = jnp.concatenate([positions < cache_length[0], jnp.repeat(present > 0, block_len)])
    peak, total, mixed = attend_keys(query_latent[0], keys, valid, VAL)
    peak, total, mixed = combined_all((peak, total, mixed), "tp", join_parts)
    attn_out = (mixed / total[:, None]).astype(jnp.bfloat16)[None]

    if cube:
        moe_out = cube_sums(keep, coming)
    else:
        share_in = jnp.sum(side_in[:, :3, :tok_rows], axis=1)
        moe_out = ring_experts(tokens, share_in, gate_weight, up_weight, down_weight)
    return (attn_out, moe_out)


def solution(mesh):
    in_specs = (
        P(("groups", "ep"), None, None),
        P(("groups", "ep"), "tp", None),
        P(("groups", "ep")),
        P(("groups", "ep"), "tp", None, None),
        P(("groups", "ep"), "tp", None),
        P(("groups", "ep"), None),
        P(("groups", "ep"), None),
        P(("groups", "ep"), None),
        P("ep", None, "tp"),
        P("ep", None, "tp"),
        P("ep", None, "tp"),
    )
    out_specs = (P(("groups", "ep"), None, None), P(("groups", "ep"), "tp"))
    return jax.shard_map(
        per_device, mesh=mesh, in_specs=in_specs, out_specs=out_specs, check_vma=False
    )
```

```python
import functools

import jax
import jax.numpy as jnp
from jax import lax
from jax.experimental import pallas as pl
from jax.experimental.pallas import tpu as pltpu
from jax.sharding import PartitionSpec as P

VAL = 512


SCALE = 192.0 ** (-0.5)
NEG = -1e30


def combined_all(x, axis, combine):
    if lax.axis_size(axis) == 1:
        return x
    everything = jax.tree.map(lambda part: lax.all_gather(part, axis), x)
    leading = jax.tree.map(lambda part: part[0], everything)

    def lap(k, so_far):
        return combine(so_far, jax.tree.map(lambda part: part[k], everything))

    return lax.fori_loop(1, lax.axis_size(axis), lap, leading)


def attend_keys(query, keys, valid, value_width):
    scores = (
        lax.dot_general(query, keys, (((1,), (1,)), ((), ())), preferred_element_type=jnp.float32)
        * SCALE
    )
    scores = jnp.where(valid[None, :], scores, NEG)
    peak = jnp.max(scores, axis=1)
    expo = jnp.where(valid[None, :], jnp.exp(scores - peak[:, None]), 0.0)
    total = jnp.sum(expo, axis=1)
    mixed = jnp.dot(
        expo.astype(jnp.bfloat16), keys[:, :value_width], preferred_element_type=jnp.float32
    )
    return (peak, total, mixed)


def join_parts(first, second):
    peak = jnp.maximum(first[0], second[0])
    left = jnp.exp(first[0] - peak)
    right = jnp.exp(second[0] - peak)
    return (
        peak,
        first[1] * left + second[1] * right,
        first[2] * left[:, None] + second[2] * right[:, None],
    )


def ring_experts(tokens, share, gate_weight, up_weight, down_weight):
    rows = lax.all_gather(tokens, "ep", axis=0, tiled=True)
    gate = jnp.dot(rows, gate_weight[0], preferred_element_type=jnp.float32)
    upper = jnp.dot(rows, up_weight[0], preferred_element_type=jnp.float32)
    hidden = (jax.nn.silu(gate) * upper).astype(jnp.bfloat16)
    if lax.axis_size("tp") > 1:
        hidden = lax.all_gather(hidden, "tp", axis=1, tiled=True)
    partial_out = jnp.dot(hidden, down_weight[0], preferred_element_type=jnp.float32)
    scaled = partial_out * share.reshape(-1)[:, None]
    return lax.psum_scatter(scaled, "ep", scatter_dimension=0, tiled=True).astype(jnp.bfloat16)


MIB = 1024 * 1024

LINKS = (1, 2, 4, 12)
PIECES = ((5, (1, 0, 3, 2)), (5, (0, 2, 1, 3)), (4, (2, 1, 0, 3)))
TURNS = (0, 2, 1)


def across(value, link):
    peers = lax.axis_size("ep")
    return lax.ppermute(value, "ep", [(i, i ^ (2 * LINKS[link])) for i in range(peers)])


def swap_cores(value):
    return lax.ppermute(value, "ep", [(i, i ^ 1) for i in range(lax.axis_size("ep"))])


def slot_of(place, order):
    slot = 0
    for i, step in enumerate(order):
        slot |= ((place >> (len(order) - 1 - i)) & 1) << step
    return slot


ORDERS = [order for _, order in PIECES]


def piece_columns(width):
    shares = [share for share, _ in PIECES]
    one = width // sum(shares)
    ends = [one * sum(shares[: at + 1]) for at in range(len(shares))]
    ends[-1] = width
    return list(zip([0] + ends[:-1], ends))


def whole_call(kernel, operands, out_shape, name, after=()):
    given = len(operands)

    def body(*refs):
        kernel(*refs[:given], *refs[given + len(after) :])

    return pl.pallas_call(
        body,
        in_specs=[pl.BlockSpec(memory_space=pltpu.VMEM)] * given
        + [pl.BlockSpec(memory_space=pl.ANY)] * len(after),
        out_specs=[pl.BlockSpec(memory_space=pltpu.VMEM)] * len(out_shape),
        out_shape=out_shape,
        compiler_params=pltpu.CompilerParams(vmem_limit_bytes=12 * MIB),
        cost_estimate=pl.CostEstimate(
            flops=0,
            bytes_accessed=sum(x.size * x.dtype.itemsize for x in list(operands) + list(out_shape)),
            transcendentals=0,
        ),
        name=name,
    )(*operands, *after)


def joined(held, got, after):
    count = len(held)
    out_shape = [jax.ShapeDtypeStruct((2 * x.shape[0], x.shape[1]), x.dtype) for x in held]

    def kernel(*refs):
        for first, second, out in zip(refs[:count], refs[count : 2 * count], refs[2 * count :]):
            rows = first.shape[0]
            out[:rows] = first[...]
            out[rows:] = second[...]

    return whole_call(kernel, [*held, *got], out_shape, "joined", after)


def hold_back(array, after):
    def kernel(in_ref, out_ref):
        out_ref[...] = in_ref[...]

    shape = jax.ShapeDtypeStruct(array.shape, array.dtype)
    return whole_call(kernel, [array], [shape], "hold_back", (after,))[0]


def first_joined(held, got, widths, after):
    rows = held[0].shape[0]
    out_shape = [jax.ShapeDtypeStruct((2 * rows, width), held[0].dtype) for width in widths]

    def kernel(first, rest, got_first, got_rest, *outs):
        outs[0][:rows] = first[...]
        outs[0][rows:] = got_first[...]
        start = 0
        for out, width in zip(outs[1:], widths[1:]):
            out[:rows] = rest[:, start : start + width]
            out[rows:] = got_rest[:, start : start + width]
            start += width

    return whole_call(kernel, [*held, *got], out_shape, "first_joined", after)


def gather_cube(unit, chip, tokens, side, gate, up, down):
    steps = len(LINKS)
    others = [swap_cores(weight) for weight in (gate, up, down)]
    columns = piece_columns(tokens.shape[1])
    widths = [stop - start for start, stop in columns]
    widths[-1] += side.shape[1]
    cut = columns[0][1]
    held = [tokens[:, :cut], jnp.concatenate([tokens[:, cut:], side], axis=1)]
    got = [across(piece, order[-1]) for piece, order in zip(held, ORDERS)]
    held = first_joined(held, got, widths, others[2:])
    for phase in range(1, steps):
        got = [across(piece, order[steps - 1 - phase]) for piece, order in zip(held, ORDERS)]
        if phase < steps - 1:
            held = joined(held, got, others[:2] if phase == 1 else ())
    weights = (gate, up, *others[:2])
    so_far = expert_part(unit, chip, held, weights)
    return expert_part(unit, chip, got, weights, so_far), others


def part_kernel(unit, last, chip_ref, *refs):
    count = len(ORDERS)
    pieces = refs[:count]
    gate_ref, up_ref, gate_other_ref, up_other_ref = refs[count : count + 4]
    if last:
        gate_part, up_part, scale_part, hidden_ref, scale_ref, gate_sum, up_sum = refs[count + 4 :]
    else:
        gate_sum, up_sum, scale_ref = refs[count + 4 :]
    step = pl.program_id(0)
    own_steps = pl.num_programs(0) // 2
    columns = piece_columns(gate_ref.shape[0])
    places = pieces[0].shape[0] // unit

    def slots(order):
        for at in range(places):
            slot = slot_of(at + (places if last else 0), order)
            yield slice(slot * unit, (slot + 1) * unit), slice(at * unit, (at + 1) * unit)

    @pl.when(step == 0)
    def _():
        scale_ref[...] = scale_part[...] if last else jnp.zeros_like(scale_ref)
        start, stop = columns[-1]
        side = pieces[-1][:, stop - start :].astype(jnp.float32)
        column = lax.broadcasted_iota(jnp.int32, side.shape, 1)
        experts = 1 << len(LINKS)
        mine = jnp.logical_and(column % experts == chip_ref[0], column < 3 * experts)
        scale = jnp.sum(jnp.where(mine, side, 0.0), axis=1, keepdims=True)
        for to, source in slots(ORDERS[-1]):
            scale_ref[to, :] = scale[source]

    def add_up(tile, total, so_far):
        total[...] = so_far[...] if last else jnp.zeros_like(total)
        for piece, (start, stop) in enumerate(columns):
            part = jnp.dot(
                pieces[piece][:, : stop - start],
                tile[start:stop, :],
                preferred_element_type=jnp.float32,
            )
            for to, source in slots(ORDERS[piece]):
                total[to, :] += part[source]

    def units(gate_tile, up_tile):
        add_up(gate_tile, gate_sum, gate_part if last else None)
        add_up(up_tile, up_sum, up_part if last else None)
        if last:
            gate = gate_sum[...]
            hidden_ref[...] = (gate / (1.0 + jnp.exp(-gate)) * up_sum[...]).astype(jnp.bfloat16)

    @pl.when(step < own_steps)
    def _():
        units(gate_ref, up_ref)

    @pl.when(step >= own_steps)
    def _():
        units(gate_other_ref, up_other_ref)


def expert_part(unit, chip, pieces, weights, so_far=()):
    width, units = weights[0].shape
    rows = pieces[0].shape[0]
    tile = 256
    steps = units // tile
    own = pl.BlockSpec((width, tile), lambda i: (0, jnp.minimum(i, steps - 1)))
    other = pl.BlockSpec((width, tile), lambda i: (0, jnp.maximum(i - steps, 0)))
    tiled = pl.BlockSpec((2 * rows, tile), lambda i: (0, i))
    single = pl.BlockSpec((2 * rows, 1), lambda i: (0, 0))
    total = jax.ShapeDtypeStruct((2 * rows, 2 * units), jnp.float32)
    scale = jax.ShapeDtypeStruct((2 * rows, 1), jnp.float32)
    hidden = jax.ShapeDtypeStruct((2 * rows, 2 * units), jnp.bfloat16)
    last = len(so_far) > 0
    return pl.pallas_call(
        functools.partial(part_kernel, unit, last),
        grid=(2 * steps,),
        in_specs=[pl.BlockSpec(memory_space=pltpu.SMEM)]
        + [pl.BlockSpec(array.shape, lambda i: (0, 0)) for array in pieces]
        + [own, own, other, other]
        + ([tiled, tiled, single] if last else []),
        out_specs=[tiled, single] if last else [tiled, tiled, single],
        out_shape=[hidden, scale] if last else [total, total, scale],
        scratch_shapes=[pltpu.VMEM((2 * rows, tile), jnp.float32)] * (2 if last else 0),
        compiler_params=pltpu.CompilerParams(vmem_limit_bytes=48 * MIB),
        cost_estimate=pl.CostEstimate(
            flops=8 * rows * width * units,
            bytes_accessed=8 * width * units + 2 * rows * width + 24 * rows * units,
            transcendentals=4 * rows * units if last else 0,
        ),
        name="expert_part",
    )(chip, *pieces, *weights, *so_far)


def output_kernel(unit, order, first, tiles, scale_ref, hidden_ref, *refs):
    down, down_other, out_ref = refs[:tiles], refs[tiles : 2 * tiles], refs[-1]
    units, tile = down[0].shape
    slots = [slot_of(first + at, order) for at in range(out_ref.shape[0] // unit)]
    rows = [slice(slot * unit, (slot + 1) * unit) for slot in slots]
    hidden = jnp.concatenate([hidden_ref[row] for row in rows], axis=0)
    scale = jnp.concatenate([scale_ref[row] for row in rows], axis=0)
    for at in range(tiles):
        out = jnp.dot(hidden[:, :units], down[at][...], preferred_element_type=jnp.float32)
        out += jnp.dot(hidden[:, units:], down_other[at][...], preferred_element_type=jnp.float32)
        out_ref[:, at * tile : (at + 1) * tile] = out * scale


def expert_output(unit, order, send, columns, scale, hidden, down, down_other, after):
    units = down.shape[0]
    start, stop = columns
    count = hidden.shape[0]
    tile = 256
    tiles = (stop - start) // tile
    first = count // unit // 2 if send else 0

    def tile_at(at):
        return pl.BlockSpec((units, tile), lambda i: (0, start // tile + at))

    return pl.pallas_call(
        functools.partial(output_kernel, unit, order, first, tiles),
        grid=(1,),
        in_specs=[
            pl.BlockSpec((count, 1), lambda i: (0, 0)),
            pl.BlockSpec((count, 2 * units), lambda i: (0, 0)),
        ]
        + [tile_at(at) for at in range(tiles)] * 2
        + [pl.BlockSpec(memory_space=pl.ANY)] * len(after),
        out_specs=pl.BlockSpec((count // 2, stop - start), lambda i: (0, 0)),
        out_shape=jax.ShapeDtypeStruct((count // 2, stop - start), jnp.float32),
        compiler_params=pltpu.CompilerParams(vmem_limit_bytes=24 * MIB),
        cost_estimate=pl.CostEstimate(
            flops=2 * count * (stop - start) * units,
            bytes_accessed=4 * (stop - start) * units + 4 * count * (stop - start + units),
            transcendentals=0,
        ),
        name="expert_output",
    )(scale, hidden, *[down] * tiles, *[down_other] * tiles, *after)


def halved(keep, got, after):
    rows, width = keep.shape
    half = jax.ShapeDtypeStruct((rows // 2, width), keep.dtype)

    def kernel(keep_ref, got_ref, first_ref, second_ref):
        second_ref[...] = keep_ref[rows // 2 :] + got_ref[rows // 2 :]
        first_ref[...] = keep_ref[: rows // 2] + got_ref[: rows // 2]

    return whole_call(kernel, [keep, got], [half, half], "halved", after)


def finished(keep, got):
    count = len(keep)
    width = sum(piece.shape[1] for piece in keep)

    def kernel(*refs):
        for at, (start, stop) in enumerate(piece_columns(width)):
            total = refs[at][...] + refs[count + at][...]
            refs[2 * count][:, start:stop] = total.astype(jnp.bfloat16)

    shape = jax.ShapeDtypeStruct((keep[0].shape[0], width), jnp.bfloat16)
    return whole_call(kernel, [*keep, *got], [shape], "finished")[0]


def cube_outputs(unit, hidden, scale, down, down_other):
    columns = piece_columns(down.shape[1])
    arrays = (scale, hidden, down, down_other)
    keep, coming, after = {}, [], ()
    for order, piece in zip(ORDERS, columns):
        send = expert_output(unit, order, True, piece, *arrays, after)
        coming.append(across(send, order[0]))
        after = (send,)
    for at in TURNS:
        keep[at] = expert_output(unit, ORDERS[at], False, columns[at], *arrays, after)
        after = (keep[at],)
    keep = [keep[at] for at in range(len(ORDERS))]
    return keep, coming


def cube_sums(keep, got):
    keep, got, after = list(keep), list(got), ()
    for phase in range(1, len(LINKS)):
        for at in TURNS:
            keep[at], send = halved(keep[at], got[at], after)
            got[at] = across(send, ORDERS[at][phase])
            after = (keep[at],)
    return finished(keep, got)


def three_parts(value):
    high = lax.reduce_precision(value, 8, 7)
    middle = lax.reduce_precision(value - high, 8, 7)
    return high, middle, value - high - middle


def per_device(
    query_latent,
    latent_cache,
    cache_length,
    prefill_latent,
    block_owner,
    tokens,
    expert_ids,
    route_weight,
    gate_weight,
    up_weight,
    down_weight,
):
    peers = lax.axis_size("ep")
    blocks = prefill_latent.shape[1]
    block_len = prefill_latent.shape[2]
    latent = prefill_latent.shape[3]
    tok_rows, top_k = expert_ids.shape

    cube = peers == 2 << len(LINKS) and lax.axis_size("tp") == 1
    weights = (gate_weight[0], up_weight[0], down_weight[0])
    if cube:
        experts = jnp.arange(peers // 2, dtype=jnp.int32)
        named = expert_ids[:, :, None] == experts[None, None, :]
        share = jnp.sum(jnp.where(named, route_weight[:, :, None], 0.0), axis=1)
        parts = jnp.concatenate(three_parts(share), axis=1).astype(jnp.bfloat16)
        parts = jnp.pad(parts, ((0, 0), (0, 128 - parts.shape[1])))
        chip = (lax.axis_index("ep") // 2).astype(jnp.int32).reshape(1)
        (hidden, scale), others = gather_cube(tok_rows, chip, tokens, parts, *weights)
        keep, coming = cube_outputs(tok_rows, hidden, scale, weights[2], others[2])
        prefill_latent = hold_back(prefill_latent, keep[TURNS[-1]])

    owner = block_owner.reshape(blocks)
    same = owner[:, None] == owner[None, :]
    earlier = jnp.arange(blocks)[None, :] < jnp.arange(blocks)[:, None]
    order_in = jnp.sum(jnp.logical_and(same, earlier).astype(jnp.int32), axis=1)
    target = owner * 2 + order_in
    chosen = jnp.arange(2 * peers, dtype=jnp.int32)[:, None] == target[None, :]
    packed = jnp.dot(
        chosen.astype(jnp.bfloat16),
        prefill_latent.reshape(blocks, block_len * latent),
        preferred_element_type=jnp.float32,
    ).astype(jnp.bfloat16)

    filled = jnp.sum(chosen.astype(jnp.float32), axis=1).reshape(peers, 1, 2)
    side = jnp.zeros((peers, 2 * block_len, max(tok_rows, 2)), jnp.float32)
    side = side.at[:, 3:4, :2].set(filled)
    if not cube:
        expert_of = jnp.arange(peers, dtype=jnp.int32) // 2
        named = expert_ids[None, :, :] == expert_of[:, None, None]
        share = jnp.sum(jnp.where(named, route_weight[None, :, :], 0.0), axis=2)
        side = side.at[:, :3, :tok_rows].set(jnp.stack(three_parts(share), axis=1))
    leaving = jnp.concatenate(
        [packed.reshape(peers, 2 * block_len, latent), side.astype(jnp.bfloat16)], axis=2
    )
    arrived = lax.all_to_all(leaving, "ep", split_axis=0, concat_axis=0, tiled=True)
    side_in = arrived[:, :, latent:].astype(jnp.float32)
    present = side_in[:, 3, :2].reshape(peers * 2)
    arrived = arrived[:, :, :latent]
    shard_len = latent_cache.shape[1]
    positions = lax.axis_index("tp") * shard_len + jnp.arange(shard_len, dtype=jnp.int32)
    keys = jnp.concatenate(
        [latent_cache[0], arrived.reshape(peers * 2 * block_len, latent)], axis=0
    )
    valid = jnp.concatenate([positions < cache_length[0], jnp.repeat(present > 0, block_len)])
    peak, total, mixed = attend_keys(query_latent[0], keys, valid, VAL)
    peak, total, mixed = combined_all((peak, total, mixed), "tp", join_parts)
    attn_out = (mixed / total[:, None]).astype(jnp.bfloat16)[None]

    if cube:
        moe_out = cube_sums(keep, coming)
    else:
        share_in = jnp.sum(side_in[:, :3, :tok_rows], axis=1)
        moe_out = ring_experts(tokens, share_in, gate_weight, up_weight, down_weight)
    return (attn_out, moe_out)


def solution(mesh):
    in_specs = (
        P(("groups", "ep"), None, None),
        P(("groups", "ep"), "tp", None),
        P(("groups", "ep")),
        P(("groups", "ep"), "tp", None, None),
        P(("groups", "ep"), "tp", None),
        P(("groups", "ep"), None),
        P(("groups", "ep"), None),
        P(("groups", "ep"), None),
        P("ep", None, "tp"),
        P("ep", None, "tp"),
        P("ep", None, "tp"),
    )
    out_specs = (P(("groups", "ep"), None, None), P(("groups", "ep"), "tp"))
    return jax.shard_map(
        per_device, mesh=mesh, in_specs=in_specs, out_specs=out_specs, check_vma=False
    )
```

```python
import functools

import jax
import jax.numpy as jnp
from jax import lax
from jax.experimental import pallas as pl
from jax.experimental.pallas import tpu as pltpu
from jax.sharding import PartitionSpec as P

VAL = 512


SCALE = 192.0 ** (-0.5)
NEG = -1e30


def combined_all(x, axis, combine):
    if lax.axis_size(axis) == 1:
        return x
    everything = jax.tree.map(lambda part: lax.all_gather(part, axis), x)
    leading = jax.tree.map(lambda part: part[0], everything)

    def lap(k, so_far):
        return combine(so_far, jax.tree.map(lambda part: part[k], everything))

    return lax.fori_loop(1, lax.axis_size(axis), lap, leading)


def attend_keys(query, keys, valid, value_width):
    scores = (
        lax.dot_general(query, keys, (((1,), (1,)), ((), ())), preferred_element_type=jnp.float32)
        * SCALE
    )
    scores = jnp.where(valid[None, :], scores, NEG)
    peak = jnp.max(scores, axis=1)
    expo = jnp.where(valid[None, :], jnp.exp(scores - peak[:, None]), 0.0)
    total = jnp.sum(expo, axis=1)
    mixed = jnp.dot(
        expo.astype(jnp.bfloat16), keys[:, :value_width], preferred_element_type=jnp.float32
    )
    return (peak, total, mixed)


def join_parts(first, second):
    peak = jnp.maximum(first[0], second[0])
    left = jnp.exp(first[0] - peak)
    right = jnp.exp(second[0] - peak)
    return (
        peak,
        first[1] * left + second[1] * right,
        first[2] * left[:, None] + second[2] * right[:, None],
    )


def ring_experts(tokens, share, gate_weight, up_weight, down_weight):
    rows = lax.all_gather(tokens, "ep", axis=0, tiled=True)
    gate = jnp.dot(rows, gate_weight[0], preferred_element_type=jnp.float32)
    upper = jnp.dot(rows, up_weight[0], preferred_element_type=jnp.float32)
    hidden = (jax.nn.silu(gate) * upper).astype(jnp.bfloat16)
    if lax.axis_size("tp") > 1:
        hidden = lax.all_gather(hidden, "tp", axis=1, tiled=True)
    partial_out = jnp.dot(hidden, down_weight[0], preferred_element_type=jnp.float32)
    scaled = partial_out * share.reshape(-1)[:, None]
    return lax.psum_scatter(scaled, "ep", scatter_dimension=0, tiled=True).astype(jnp.bfloat16)


MIB = 1024 * 1024

LINKS = (1, 2, 4, 12)
PIECES = ((5, (1, 0, 3, 2)), (5, (0, 2, 1, 3)), (4, (2, 1, 0, 3)))
TURNS = (0, 2, 1)


def across(value, link):
    peers = lax.axis_size("ep")
    return lax.ppermute(value, "ep", [(i, i ^ (2 * LINKS[link])) for i in range(peers)])


def swap_cores(value):
    return lax.ppermute(value, "ep", [(i, i ^ 1) for i in range(lax.axis_size("ep"))])


def slot_of(place, order):
    slot = 0
    for i, step in enumerate(order):
        slot |= ((place >> (len(order) - 1 - i)) & 1) << step
    return slot


ORDERS = [order for _, order in PIECES]


def piece_columns(width):
    shares = [share for share, _ in PIECES]
    one = width // sum(shares)
    ends = [one * sum(shares[: at + 1]) for at in range(len(shares))]
    ends[-1] = width
    return list(zip([0] + ends[:-1], ends))


def whole_call(kernel, operands, out_shape, name, after=()):
    given = len(operands)

    def body(*refs):
        kernel(*refs[:given], *refs[given + len(after) :])

    return pl.pallas_call(
        body,
        in_specs=[pl.BlockSpec(memory_space=pltpu.VMEM)] * given
        + [pl.BlockSpec(memory_space=pl.ANY)] * len(after),
        out_specs=[pl.BlockSpec(memory_space=pltpu.VMEM)] * len(out_shape),
        out_shape=out_shape,
        compiler_params=pltpu.CompilerParams(vmem_limit_bytes=12 * MIB),
        cost_estimate=pl.CostEstimate(
            flops=0,
            bytes_accessed=sum(x.size * x.dtype.itemsize for x in list(operands) + list(out_shape)),
            transcendentals=0,
        ),
        name=name,
    )(*operands, *after)


def joined(held, got, after):
    count = len(held)
    out_shape = [jax.ShapeDtypeStruct((2 * x.shape[0], x.shape[1]), x.dtype) for x in held]

    def kernel(*refs):
        for first, second, out in zip(refs[:count], refs[count : 2 * count], refs[2 * count :]):
            rows = first.shape[0]
            out[:rows] = first[...]
            out[rows:] = second[...]

    return whole_call(kernel, [*held, *got], out_shape, "joined", after)


def hold_back(array, after):
    def kernel(in_ref, out_ref):
        out_ref[...] = in_ref[...]

    shape = jax.ShapeDtypeStruct(array.shape, array.dtype)
    return whole_call(kernel, [array], [shape], "hold_back", (after,))[0]


def first_joined(held, got, widths, after):
    rows = held[0].shape[0]
    out_shape = [jax.ShapeDtypeStruct((2 * rows, width), held[0].dtype) for width in widths]

    def kernel(first, rest, got_first, got_rest, *outs):
        outs[0][:rows] = first[...]
        outs[0][rows:] = got_first[...]
        start = 0
        for out, width in zip(outs[1:], widths[1:]):
            out[:rows] = rest[:, start : start + width]
            out[rows:] = got_rest[:, start : start + width]
            start += width

    return whole_call(kernel, [*held, *got], out_shape, "first_joined", after)


def gather_cube(unit, chip, tokens, side, gate, up, down):
    steps = len(LINKS)
    others = [swap_cores(weight) for weight in (gate, up, down)]
    columns = piece_columns(tokens.shape[1])
    widths = [stop - start for start, stop in columns]
    widths[-1] += side.shape[1]
    cut = columns[0][1]
    held = [tokens[:, :cut], jnp.concatenate([tokens[:, cut:], side], axis=1)]
    got = [across(piece, order[-1]) for piece, order in zip(held, ORDERS)]
    held = first_joined(held, got, widths, others[2:])
    for phase in range(1, steps):
        got = [across(piece, order[steps - 1 - phase]) for piece, order in zip(held, ORDERS)]
        if phase < steps - 1:
            held = joined(held, got, others[:2] if phase == 1 else ())
    weights = (gate, up, *others[:2])
    so_far = expert_part(unit, chip, held, weights)
    return expert_part(unit, chip, got, weights, so_far), others


def part_kernel(unit, last, chip_ref, *refs):
    count = len(ORDERS)
    pieces = refs[:count]
    gate_ref, up_ref, gate_other_ref, up_other_ref = refs[count : count + 4]
    if last:
        gate_part, up_part, scale_part, hidden_ref, scale_ref, gate_sum, up_sum = refs[count + 4 :]
    else:
        gate_sum, up_sum, scale_ref = refs[count + 4 :]
    step = pl.program_id(0)
    own_steps = pl.num_programs(0) // 2
    columns = piece_columns(gate_ref.shape[0])
    places = pieces[0].shape[0] // unit

    def slots(order):
        for at in range(places):
            slot = slot_of(at + (places if last else 0), order)
            yield slice(slot * unit, (slot + 1) * unit), slice(at * unit, (at + 1) * unit)

    @pl.when(step == 0)
    def _():
        scale_ref[...] = scale_part[...] if last else jnp.zeros_like(scale_ref)
        start, stop = columns[-1]
        side = pieces[-1][:, stop - start :].astype(jnp.float32)
        column = lax.broadcasted_iota(jnp.int32, side.shape, 1)
        experts = 1 << len(LINKS)
        mine = jnp.logical_and(column % experts == chip_ref[0], column < 3 * experts)
        scale = jnp.sum(jnp.where(mine, side, 0.0), axis=1, keepdims=True)
        for to, source in slots(ORDERS[-1]):
            scale_ref[to, :] = scale[source]

    def add_up(tile, total, so_far):
        total[...] = so_far[...] if last else jnp.zeros_like(total)
        for piece, (start, stop) in enumerate(columns):
            part = jnp.dot(
                pieces[piece][:, : stop - start],
                tile[start:stop, :],
                preferred_element_type=jnp.float32,
            )
            for to, source in slots(ORDERS[piece]):
                total[to, :] += part[source]

    def units(gate_tile, up_tile):
        add_up(gate_tile, gate_sum, gate_part if last else None)
        add_up(up_tile, up_sum, up_part if last else None)
        if last:
            gate = gate_sum[...]
            hidden_ref[...] = (gate / (1.0 + jnp.exp(-gate)) * up_sum[...]).astype(jnp.bfloat16)

    @pl.when(step < own_steps)
    def _():
        units(gate_ref, up_ref)

    @pl.when(step >= own_steps)
    def _():
        units(gate_other_ref, up_other_ref)


def expert_part(unit, chip, pieces, weights, so_far=()):
    width, units = weights[0].shape
    rows = pieces[0].shape[0]
    tile = 256
    steps = units // tile
    own = pl.BlockSpec((width, tile), lambda i: (0, jnp.minimum(i, steps - 1)))
    other = pl.BlockSpec((width, tile), lambda i: (0, jnp.maximum(i - steps, 0)))
    tiled = pl.BlockSpec((2 * rows, tile), lambda i: (0, i))
    single = pl.BlockSpec((2 * rows, 1), lambda i: (0, 0))
    total = jax.ShapeDtypeStruct((2 * rows, 2 * units), jnp.float32)
    scale = jax.ShapeDtypeStruct((2 * rows, 1), jnp.float32)
    hidden = jax.ShapeDtypeStruct((2 * rows, 2 * units), jnp.bfloat16)
    last = len(so_far) > 0
    return pl.pallas_call(
        functools.partial(part_kernel, unit, last),
        grid=(2 * steps,),
        in_specs=[pl.BlockSpec(memory_space=pltpu.SMEM)]
        + [pl.BlockSpec(array.shape, lambda i: (0, 0)) for array in pieces]
        + [own, own, other, other]
        + ([tiled, tiled, single] if last else []),
        out_specs=[tiled, single] if last else [tiled, tiled, single],
        out_shape=[hidden, scale] if last else [total, total, scale],
        scratch_shapes=[pltpu.VMEM((2 * rows, tile), jnp.float32)] * (2 if last else 0),
        compiler_params=pltpu.CompilerParams(vmem_limit_bytes=48 * MIB),
        cost_estimate=pl.CostEstimate(
            flops=8 * rows * width * units,
            bytes_accessed=8 * width * units + 2 * rows * width + 24 * rows * units,
            transcendentals=4 * rows * units if last else 0,
        ),
        name="expert_part",
    )(chip, *pieces, *weights, *so_far)


def output_kernel(unit, order, tiles, scale_ref, hidden_ref, *refs):
    down, down_other = refs[:tiles], refs[tiles : 2 * tiles]
    keep_ref, send_ref = refs[-2:]
    units, tile = down[0].shape
    places = hidden_ref.shape[0] // unit
    for out_ref, first in ((send_ref, places // 2), (keep_ref, 0)):
        slots = [slot_of(first + at, order) for at in range(places // 2)]
        rows = [slice(slot * unit, (slot + 1) * unit) for slot in slots]
        hidden = jnp.concatenate([hidden_ref[row] for row in rows], axis=0)
        scale = jnp.concatenate([scale_ref[row] for row in rows], axis=0)
        for at in range(tiles):
            out = jnp.dot(hidden[:, :units], down[at][...], preferred_element_type=jnp.float32)
            out += jnp.dot(hidden[:, units:], down_other[at][...], preferred_element_type=jnp.float32)
            out_ref[:, at * tile : (at + 1) * tile] = out * scale


def expert_output(unit, order, columns, scale, hidden, down, down_other, after):
    units = down.shape[0]
    start, stop = columns
    count = hidden.shape[0]
    tile = 256
    tiles = (stop - start) // tile
    half = jax.ShapeDtypeStruct((count // 2, stop - start), jnp.float32)

    def tile_at(at):
        return pl.BlockSpec((units, tile), lambda i: (0, start // tile + at))

    return pl.pallas_call(
        functools.partial(output_kernel, unit, order, tiles),
        grid=(1,),
        in_specs=[
            pl.BlockSpec((count, 1), lambda i: (0, 0)),
            pl.BlockSpec((count, 2 * units), lambda i: (0, 0)),
        ]
        + [tile_at(at) for at in range(tiles)] * 2
        + [pl.BlockSpec(memory_space=pl.ANY)] * len(after),
        out_specs=[pl.BlockSpec((count // 2, stop - start), lambda i: (0, 0))] * 2,
        out_shape=[half] * 2,
        compiler_params=pltpu.CompilerParams(vmem_limit_bytes=24 * MIB),
        cost_estimate=pl.CostEstimate(
            flops=4 * count * (stop - start) * units,
            bytes_accessed=4 * (stop - start) * units + 4 * count * (stop - start + units),
            transcendentals=0,
        ),
        name="expert_output",
    )(scale, hidden, *[down] * tiles, *[down_other] * tiles, *after)


def halved(keep, got, after):
    rows, width = keep.shape
    tiles = 2 if rows * width >= 1 << 18 else 1
    half = jax.ShapeDtypeStruct((rows // 2, width), keep.dtype)

    def kernel(keep_ref, got_ref, *refs):
        first_ref, second_ref = refs[-2:]
        second_ref[...] = keep_ref[rows // 2 :] + got_ref[rows // 2 :]
        first_ref[...] = keep_ref[: rows // 2] + got_ref[: rows // 2]

    return pl.pallas_call(
        kernel,
        grid=(tiles,),
        in_specs=[pl.BlockSpec((rows, width // tiles), lambda i: (0, i))] * 2
        + [pl.BlockSpec(memory_space=pl.ANY)] * len(after),
        out_specs=[pl.BlockSpec((rows // 2, width // tiles), lambda i: (0, i))] * 2,
        out_shape=[half, half],
        compiler_params=pltpu.CompilerParams(vmem_limit_bytes=12 * MIB),
        cost_estimate=pl.CostEstimate(
            flops=rows * width, bytes_accessed=12 * rows * width, transcendentals=0
        ),
        name="halved",
    )(keep, got, *after)


def finished(keep, got):
    count = len(keep)
    width = sum(piece.shape[1] for piece in keep)

    def kernel(*refs):
        for at, (start, stop) in enumerate(piece_columns(width)):
            total = refs[at][...] + refs[count + at][...]
            refs[2 * count][:, start:stop] = total.astype(jnp.bfloat16)

    shape = jax.ShapeDtypeStruct((keep[0].shape[0], width), jnp.bfloat16)
    return whole_call(kernel, [*keep, *got], [shape], "finished")[0]


def cube_outputs(unit, hidden, scale, down, down_other):
    keep, coming = [], []
    for order, columns in zip(ORDERS, piece_columns(down.shape[1])):
        after = keep[-1:]
        mine, send = expert_output(unit, order, columns, scale, hidden, down, down_other, after)
        keep.append(mine)
        coming.append(across(send, order[0]))
    return keep, coming


def cube_sums(keep, got):
    keep, got, after = list(keep), list(got), ()
    for phase in range(1, len(LINKS)):
        for at in TURNS:
            keep[at], send = halved(keep[at], got[at], after)
            got[at] = across(send, ORDERS[at][phase])
            after = (keep[at],)
    return finished(keep, got)


def three_parts(value):
    high = lax.reduce_precision(value, 8, 7)
    middle = lax.reduce_precision(value - high, 8, 7)
    return high, middle, value - high - middle


def per_device(
    query_latent,
    latent_cache,
    cache_length,
    prefill_latent,
    block_owner,
    tokens,
    expert_ids,
    route_weight,
    gate_weight,
    up_weight,
    down_weight,
):
    peers = lax.axis_size("ep")
    blocks = prefill_latent.shape[1]
    block_len = prefill_latent.shape[2]
    latent = prefill_latent.shape[3]
    tok_rows, top_k = expert_ids.shape

    cube = peers == 2 << len(LINKS) and lax.axis_size("tp") == 1
    weights = (gate_weight[0], up_weight[0], down_weight[0])
    if cube:
        experts = jnp.arange(peers // 2, dtype=jnp.int32)
        named = expert_ids[:, :, None] == experts[None, None, :]
        share = jnp.sum(jnp.where(named, route_weight[:, :, None], 0.0), axis=1)
        parts = jnp.concatenate(three_parts(share), axis=1).astype(jnp.bfloat16)
        parts = jnp.pad(parts, ((0, 0), (0, 128 - parts.shape[1])))
        chip = (lax.axis_index("ep") // 2).astype(jnp.int32).reshape(1)
        (hidden, scale), others = gather_cube(tok_rows, chip, tokens, parts, *weights)
        keep, coming = cube_outputs(tok_rows, hidden, scale, weights[2], others[2])
        prefill_latent = hold_back(prefill_latent, keep[-1])

    owner = block_owner.reshape(blocks)
    same = owner[:, None] == owner[None, :]
    earlier = jnp.arange(blocks)[None, :] < jnp.arange(blocks)[:, None]
    order_in = jnp.sum(jnp.logical_and(same, earlier).astype(jnp.int32), axis=1)
    target = owner * 2 + order_in
    chosen = jnp.arange(2 * peers, dtype=jnp.int32)[:, None] == target[None, :]
    packed = jnp.dot(
        chosen.astype(jnp.bfloat16),
        prefill_latent.reshape(blocks, block_len * latent),
        preferred_element_type=jnp.float32,
    ).astype(jnp.bfloat16)

    filled = jnp.sum(chosen.astype(jnp.float32), axis=1).reshape(peers, 1, 2)
    side = jnp.zeros((peers, 2 * block_len, max(tok_rows, 2)), jnp.float32)
    side = side.at[:, 3:4, :2].set(filled)
    if not cube:
        expert_of = jnp.arange(peers, dtype=jnp.int32) // 2
        named = expert_ids[None, :, :] == expert_of[:, None, None]
        share = jnp.sum(jnp.where(named, route_weight[None, :, :], 0.0), axis=2)
        side = side.at[:, :3, :tok_rows].set(jnp.stack(three_parts(share), axis=1))
    leaving = jnp.concatenate(
        [packed.reshape(peers, 2 * block_len, latent), side.astype(jnp.bfloat16)], axis=2
    )
    arrived = lax.all_to_all(leaving, "ep", split_axis=0, concat_axis=0, tiled=True)
    side_in = arrived[:, :, latent:].astype(jnp.float32)
    present = side_in[:, 3, :2].reshape(peers * 2)
    arrived = arrived[:, :, :latent]
    shard_len = latent_cache.shape[1]
    positions = lax.axis_index("tp") * shard_len + jnp.arange(shard_len, dtype=jnp.int32)
    keys = jnp.concatenate(
        [latent_cache[0], arrived.reshape(peers * 2 * block_len, latent)], axis=0
    )
    valid = jnp.concatenate([positions < cache_length[0], jnp.repeat(present > 0, block_len)])
    peak, total, mixed = attend_keys(query_latent[0], keys, valid, VAL)
    peak, total, mixed = combined_all((peak, total, mixed), "tp", join_parts)
    attn_out = (mixed / total[:, None]).astype(jnp.bfloat16)[None]

    if cube:
        moe_out = cube_sums(keep, coming)
    else:
        share_in = jnp.sum(side_in[:, :3, :tok_rows], axis=1)
        moe_out = ring_experts(tokens, share_in, gate_weight, up_weight, down_weight)
    return (attn_out, moe_out)


def solution(mesh):
    in_specs = (
        P(("groups", "ep"), None, None),
        P(("groups", "ep"), "tp", None),
        P(("groups", "ep")),
        P(("groups", "ep"), "tp", None, None),
        P(("groups", "ep"), "tp", None),
        P(("groups", "ep"), None),
        P(("groups", "ep"), None),
        P(("groups", "ep"), None),
        P("ep", None, "tp"),
        P("ep", None, "tp"),
        P("ep", None, "tp"),
    )
    out_specs = (P(("groups", "ep"), None, None), P(("groups", "ep"), "tp"))
    return jax.shard_map(
        per_device, mesh=mesh, in_specs=in_specs, out_specs=out_specs, check_vma=False
    )
```
